32 devices in a mesh: dom: 8 (over z, y), rep: 4 (over x, core).
Axes of the slice: x: 2, y: 2, z: 4, core: 2. Of those that a mesh axis runs over, the one named last changes fastest.
Arguments:
- features: bfloat16 [2048, 1024], P('dom', 'rep'), may hold values from -6 to 6
- w_self: bfloat16 [1024, 1024], P('rep'), may hold values from -0.1875 to 0.1875
- w_neigh: bfloat16 [1024, 1024], P('rep'), may hold values from -0.1875 to 0.1875
- grad_out: bfloat16 [2048, 1024], P('dom', 'rep'), may hold values from -6 to 6
- mirror_list: int32 [64, 64], P('dom'), may hold values from 0 to 255, as said below
- mirror_count: int32 [64], P('dom'), may hold values from 1 to 64, as said below
- tile_dst: int32 [64], P('dom'), may hold values from 0 to 1
- tile_src: int32 [64], P('dom'), may hold values from 0 to 5
- tiles: bfloat16 [64, 128, 128], P('dom'), may hold values from 0 to 4, as said below
Outputs:
- hidden_out: bfloat16 [2048, 1024], P('dom', 'rep')
- grad_features: bfloat16 [2048, 1024], P('dom', 'rep')
- grad_self: bfloat16 [1024, 1024], P('rep')
- grad_neigh: bfloat16 [1024, 1024], P('rep')
The draws below stay inside these ranges and needn't reach their ends.
Inputs may be any that keep to these rules, and one draw needn't show every extreme that they name: `mirror_list`: the entries of one row are distinct. `mirror_count`: every partition has a peer whose count is exactly 64. Weights are zero in columns that fall on unused mirror slots; on each partition the slots after its live tiles hold zeros, and some partition has all 8 slots live.
All inputs are finite; a program needn't handle non-finite values.
Results may differ from the reference program's by a relative error of at most 0.0058.
Values may be sent and summed in bfloat16 or wider, within the bound.
No kernel may reach another device: no remote copies, remote signals or barrier semaphores. Data moves between devices by JAX's collectives and lax.ppermute only.
A program may use at most 64 MiB of HBM per device.

```python
import jax
import jax.numpy as jnp
from jax import lax

D = 1024
TILE = 128
V = 256
MIRROR_DEV = 512
TILES = 8
M_PEER = 64
VERTICES = 2048
N_DOM = 8


def count_table(key):
    base = jax.random.fold_in(key, 11)
    counts = jax.random.randint(jax.random.fold_in(base, 1), (N_DOM, N_DOM), 1, M_PEER + 1)
    full_peer = jax.random.randint(jax.random.fold_in(base, 2), (N_DOM,), 0, N_DOM)
    counts = jnp.where(jnp.arange(N_DOM)[None, :] == full_peer[:, None], M_PEER, counts)
    return counts.astype(jnp.int32)


def live_tiles(key):
    base = jax.random.fold_in(key, 31)
    first = jax.random.randint(jax.random.fold_in(base, 1), (N_DOM,), 0, TILES)
    second = jax.random.randint(jax.random.fold_in(base, 2), (N_DOM,), 0, TILES)
    counts = 1 + first * second // TILES
    busiest = jax.random.randint(jax.random.fold_in(base, 3), (), 0, N_DOM)
    counts = jnp.where(jnp.arange(N_DOM) == busiest, TILES, counts)
    return counts.astype(jnp.int32)


def source_tiles(key):
    base = jax.random.fold_in(key, 41)
    return jax.random.randint(base, (N_DOM * TILES,), 0, (V + MIRROR_DEV) // TILE).astype(jnp.int32)


def draw_mirror_count(key, part):
    return count_table(key).reshape(-1)


def draw_mirror_list(key, part):
    base = jax.random.fold_in(key, 23)
    row_keys = jax.random.split(base, N_DOM * N_DOM)
    picked = jax.vmap(lambda row_key: jax.random.permutation(row_key, V)[:M_PEER])(row_keys)
    return picked.astype(jnp.int32)


def draw_tile_dst(key, part):
    base = jax.random.fold_in(key, 53)
    return jax.random.randint(base, (N_DOM * TILES,), 0, V // TILE).astype(jnp.int32)


def draw_tile_src(key, part):
    return source_tiles(key)


def draw_tiles(key, part):
    counts = count_table(key)
    live_count = live_tiles(key)
    src_ids = source_tiles(key).reshape(N_DOM, TILES)
    column = src_ids[:, :, None] * TILE + jnp.arange(TILE)[None, None, :]
    mirror_slot = jnp.maximum(column - V, 0)
    peer_ids = jnp.minimum(mirror_slot // M_PEER, N_DOM - 1)
    slot_ids = mirror_slot % M_PEER
    device_ids = jnp.broadcast_to(jnp.arange(N_DOM)[:, None, None], column.shape)
    count_for = counts[peer_ids, device_ids]
    column_live = (column < V) | (slot_ids < count_for)
    tile_live = jnp.arange(TILES)[None, :] < live_count[:, None]
    base = jax.random.fold_in(key, 67)
    shape = (N_DOM, TILES, TILE, TILE)
    edge_mask = jax.random.randint(jax.random.fold_in(base, 1), shape, 0, 8) == 0
    values = jnp.exp(jax.random.uniform(jax.random.fold_in(base, 2), shape, jnp.float32, jnp.log(0.25), jnp.log(4.0)))
    keep = edge_mask & column_live[:, :, None, :] & tile_live[:, :, None, None]
    result = jnp.where(keep, values, 0.0)
    return result.reshape(N_DOM * TILES, TILE, TILE).astype(jnp.bfloat16)


def levels(stream_key, dims, shards, smallest, high):
    level = 1.0
    for axis_at, parts in shards:
        heights = jax.random.uniform(jax.random.fold_in(jax.random.fold_in(stream_key, 6), axis_at), (parts,), jnp.float32, smallest / len(shards), high / len(shards))
        level = level * jnp.repeat(jnp.exp(heights), dims[axis_at] // parts).reshape((-1,) + (1,) * (len(dims) - 1 - axis_at))
    return level


def gaussian(key, shape, spread, bound, shards=(), kind=jnp.bfloat16):
    values = jax.random.normal(key, shape, jnp.float32) * spread
    if len(shards) > 0:
        values = levels(key, shape, shards, -0.22, 0.18) * values
    return jnp.clip(values, min=-bound, max=bound).astype(kind)


def setup_inputs(seed: int = 0) -> dict:
    arg_keys = jax.random.split(jax.random.key(seed), 10)
    return {
        "features": gaussian(arg_keys[0], (VERTICES, D), 1.0, 6.0, ((0, 8), (1, 4))),
        "w_self": gaussian(arg_keys[1], (D, D), D ** -0.5, 0.1875, ((0, 4),)),
        "w_neigh": gaussian(arg_keys[2], (D, D), D ** -0.5, 0.1875, ((0, 4),)),
        "grad_out": gaussian(arg_keys[3], (VERTICES, D), 1.0, 6.0, ((0, 8), (1, 4))),
        "mirror_list": draw_mirror_list(jax.random.fold_in(arg_keys[9], 71), 0),
        "mirror_count": draw_mirror_count(jax.random.fold_in(arg_keys[9], 71), 0),
        "tile_dst": draw_tile_dst(jax.random.fold_in(arg_keys[9], 71), 0),
        "tile_src": draw_tile_src(jax.random.fold_in(arg_keys[9], 71), 0),
        "tiles": draw_tiles(jax.random.fold_in(arg_keys[9], 71), 0),
    }


def mirror_index(mirror_list, mirror_count, device):
    slot_count = MIRROR_DEV // N_DOM
    peer_lists = mirror_list.reshape(N_DOM, N_DOM, slot_count)[:, device, :]
    counts = mirror_count.reshape(N_DOM, N_DOM)[:, device]
    source_rows = (jnp.arange(N_DOM, dtype=jnp.int32)[:, None] * V + peer_lists).reshape(-1)
    slot_ids = jnp.arange(slot_count, dtype=jnp.int32)
    live_mask = (slot_ids[None, :] < counts[:, None]).reshape(-1)
    return source_rows, live_mask


def reference(features, w_self, w_neigh, grad_out, mirror_list, mirror_count, tile_dst, tile_src, tiles):
    src_count = (V + MIRROR_DEV) // TILE
    dst_count = V // TILE
    highest = lax.Precision.HIGHEST

    def device_tiles(device):
        block = lax.dynamic_slice_in_dim(tiles, device * TILES, TILES, 0).astype(jnp.float32)
        dst_ids = lax.dynamic_slice_in_dim(tile_dst, device * TILES, TILES, 0)
        src_ids = lax.dynamic_slice_in_dim(tile_src, device * TILES, TILES, 0)
        dst_onehot = (dst_ids[None, :] == jnp.arange(dst_count, dtype=jnp.int32)[:, None]).astype(jnp.float32)
        src_onehot = (src_ids[None, :] == jnp.arange(src_count, dtype=jnp.int32)[:, None]).astype(jnp.float32)
        return block, dst_ids, src_ids, dst_onehot, src_onehot

    def forward_one(device):
        source_rows, live_mask = mirror_index(mirror_list, mirror_count, device)
        mirrors = jnp.where(live_mask[:, None], features[source_rows], 0).astype(features.dtype)
        own_rows = lax.dynamic_slice_in_dim(features, device * V, V, 0)
        row_table = jnp.concatenate([own_rows, mirrors], axis=0)
        block, dst_ids, src_ids, dst_onehot, src_onehot = device_tiles(device)
        gathered = row_table.reshape(src_count, TILE, D)[src_ids].astype(jnp.float32)
        contrib = jnp.einsum('tij,tjd->tid', block, gathered, precision=highest)
        summed = jnp.einsum('st,tid->sid', dst_onehot, contrib, precision=highest).reshape(V, D)
        degree = jnp.einsum('st,ti->si', dst_onehot, jnp.sum(block, axis=2), precision=highest).reshape(V)
        aggregated = (summed / jnp.maximum(degree, 1.0)[:, None]).astype(jnp.bfloat16)
        return aggregated, degree

    aggregated, degree = lax.map(forward_one, jnp.arange(N_DOM, dtype=jnp.int32))
    aggregated = aggregated.reshape(VERTICES, D)
    degree = degree.reshape(VERTICES)
    pre_act = jnp.dot(features, w_self, preferred_element_type=jnp.float32) + jnp.dot(aggregated, w_neigh, preferred_element_type=jnp.float32)
    gate_sig = jax.nn.sigmoid(pre_act)
    hidden_out = (pre_act * gate_sig).astype(jnp.bfloat16)
    grad_pre = (grad_out.astype(jnp.float32) * (gate_sig + pre_act * gate_sig * (1.0 - gate_sig))).astype(jnp.bfloat16)
    grad_scale = float(VERTICES) ** -0.5
    grad_self = (jnp.dot(features.T, grad_pre, preferred_element_type=jnp.float32) * grad_scale).astype(jnp.bfloat16)
    grad_neigh = (jnp.dot(aggregated.T, grad_pre, preferred_element_type=jnp.float32) * grad_scale).astype(jnp.bfloat16)
    direct = jnp.dot(grad_pre, w_self.T, preferred_element_type=jnp.float32)
    grad_agg = (jnp.dot(grad_pre, w_neigh.T, preferred_element_type=jnp.float32) / jnp.maximum(degree, 1.0)[:, None]).astype(jnp.bfloat16)

    def backward_one(accum, device):
        block, dst_ids, src_ids, dst_onehot, src_onehot = device_tiles(device)
        grad_dev = lax.dynamic_slice_in_dim(grad_agg, device * V, V, 0)
        grad_tiles = grad_dev.reshape(dst_count, TILE, D)[dst_ids].astype(jnp.float32)
        contrib = jnp.einsum('tij,tid->tjd', block, grad_tiles, precision=highest)
        table_grad = jnp.einsum('st,tjd->sjd', src_onehot, contrib, precision=highest).reshape(src_count * TILE, D)
        own_part = lax.dynamic_slice_in_dim(accum, device * V, V, 0) + table_grad[:V]
        accum = lax.dynamic_update_slice_in_dim(accum, own_part, device * V, 0)
        source_rows, live_mask = mirror_index(mirror_list, mirror_count, device)
        mirror_part = jnp.where(live_mask[:, None], table_grad[V:], jnp.float32(0.0))
        accum = accum.at[source_rows].add(mirror_part)
        return accum, None

    accum, unused = lax.scan(backward_one, jnp.zeros((VERTICES, D), jnp.float32), jnp.arange(N_DOM, dtype=jnp.int32))
    grad_features = (direct + accum).astype(jnp.bfloat16)
    return hidden_out, grad_features, grad_self, grad_neigh
```

```python
import functools

import jax
import jax.numpy as jnp
from jax import lax
from jax.experimental import pallas as pl
from jax.experimental.pallas import tpu as pltpu
from jax.sharding import PartitionSpec as P

F32 = jnp.float32
BF16 = jnp.bfloat16
VMEM = pl.BlockSpec(memory_space=pltpu.VMEM)
SMEM = pl.BlockSpec(memory_space=pltpu.SMEM)
ROWS = (((0,), (0,)), ((), ()))
COLS = (((1,), (1,)), ((), ()))


def call(body, outs, ins, scratch=(), flops=0, moved=0):
    return pl.pallas_call(
        body,
        out_shape=outs,
        in_specs=[SMEM if spec == "s" else VMEM for spec, _ in ins],
        out_specs=jax.tree.map(lambda _: VMEM, outs),
        scratch_shapes=list(scratch),
        compiler_params=pltpu.CompilerParams(vmem_limit_bytes=32 * 1024 * 1024),
        cost_estimate=pl.CostEstimate(flops=flops, bytes_accessed=moved, transcendentals=0),
    )(*[array for _, array in ins])


def row_onehot(count_ref, list_ref, rows):
    peers, slots = list_ref.shape
    peer = lax.broadcasted_iota(jnp.int32, (peers, slots), 0)
    slot = lax.broadcasted_iota(jnp.int32, (peers, slots), 1)

    def fill(at, used):
        return jnp.where(peer == at, count_ref[at], used)

    used = jnp.zeros((peers, slots), jnp.int32)
    if peers <= 16:
        for at in range(peers):
            used = fill(at, used)
    else:
        used = lax.fori_loop(0, peers, fill, used)
    index = jnp.where(slot < used, list_ref[...], -1).astype(F32).astype(BF16)
    flat = peers * slots
    spread = (
        lax.broadcasted_iota(jnp.int32, (slots, flat), 0)
        == lax.broadcasted_iota(jnp.int32, (slots, flat), 1) % slots
    )
    wide = jnp.dot(index, spread.astype(F32).astype(BF16), preferred_element_type=F32)
    mine = (
        lax.broadcasted_iota(jnp.int32, (peers, flat), 0)
        == lax.broadcasted_iota(jnp.int32, (peers, flat), 1) // slots
    )
    line = jnp.sum(jnp.where(mine, wide, 0.0), axis=0, keepdims=True).astype(jnp.int32)
    hit = lax.broadcasted_iota(jnp.int32, (rows, flat), 0) == line
    return hit.astype(F32).astype(BF16)


def pick_body(count_ref, list_ref, feat_ref, out_ref):
    onehot = row_onehot(count_ref, list_ref, feat_ref.shape[0])
    out_ref[...] = lax.dot_general(
        onehot, feat_ref[...], ROWS, preferred_element_type=F32
    ).astype(BF16)


def forward_body(
    rep_ref, dst_ref, src_ref, feat_ref, inc_ref, tiles_ref, self_ref, neigh_ref,
    part_ref, own_ref, agg_ref, deg_ref, adj_ref, table_ref, picked_ref,
):
    rows, cols = feat_ref.shape
    slots, side, _ = tiles_ref.shape
    table_ref[:rows] = feat_ref[...]
    table_ref[rows:] = inc_ref[...]
    for t in range(slots):
        dst = dst_ref[t]
        tile = tiles_ref[t].astype(F32)
        for s in range(rows // side):
            adj_ref[s * side:(s + 1) * side, t * side:(t + 1) * side] = jnp.where(
                dst == s, tile, 0.0
            ).astype(BF16)
        start = pl.multiple_of(src_ref[t] * side, side)
        picked_ref[t * side:(t + 1) * side] = table_ref[pl.ds(start, side)]
    adj = adj_ref[...]
    summed = jnp.dot(adj, picked_ref[...], preferred_element_type=F32)
    degree = jnp.dot(adj, jnp.ones((slots * side, 128), BF16), preferred_element_type=F32)
    degree = jnp.maximum(degree, 1.0)
    deg_ref[...] = degree
    agg = (summed / jnp.concatenate([degree] * (cols // 128), axis=1)).astype(BF16)
    agg_ref[...] = agg
    feat = feat_ref[...]
    for c in range(part_ref.shape[0]):
        at = slice(c * cols, (c + 1) * cols)
        value = jnp.dot(feat, self_ref[:, at], preferred_element_type=F32) + jnp.dot(
            agg, neigh_ref[:, at], preferred_element_type=F32
        )
        part_ref[c] = value.astype(BF16)

        @pl.when(rep_ref[0] == c)
        def _():
            own_ref[...] = value


def gate_body(rep_ref, recv_ref, own_ref, gout_ref, hid_ref, gpre_ref):
    pre = own_ref[...]
    for c in range(recv_ref.shape[0]):
        pre = pre + jnp.where(rep_ref[0] == c, 0.0, recv_ref[c].astype(F32))
    gate = jax.nn.sigmoid(pre)
    hid_ref[...] = (pre * gate).astype(BF16)
    gpre_ref[...] = (gout_ref[...].astype(F32) * (gate + pre * gate * (1.0 - gate))).astype(BF16)


def back_body(
    dst_ref, src_ref, gfull_ref, self_ref, neigh_ref, deg_ref, tiles_ref,
    mirror_ref, total_ref, gagg_ref, table_ref,
):
    rows, cols = total_ref.shape
    slots, side, _ = tiles_ref.shape
    direct = jnp.zeros((rows, cols), F32)
    gagg = jnp.zeros((rows, cols), F32)
    for c in range(gfull_ref.shape[0]):
        at = slice(c * cols, (c + 1) * cols)
        direct += lax.dot_general(gfull_ref[c], self_ref[:, at], COLS, preferred_element_type=F32)
        gagg += lax.dot_general(gfull_ref[c], neigh_ref[:, at], COLS, preferred_element_type=F32)
    gagg_ref[...] = (gagg / jnp.concatenate([deg_ref[...]] * (cols // 128), axis=1)).astype(BF16)
    table_ref[:rows] = direct
    table_ref[rows:] = jnp.zeros((table_ref.shape[0] - rows, cols), F32)
    for t in range(slots):
        dst = pl.multiple_of(dst_ref[t] * side, side)
        src = pl.multiple_of(src_ref[t] * side, side)
        table_ref[pl.ds(src, side)] += lax.dot_general(
            tiles_ref[t], gagg_ref[pl.ds(dst, side)], ROWS, preferred_element_type=F32
        )
    total_ref[...] = table_ref[:rows]
    mirror_ref[...] = table_ref[rows:].astype(BF16)


def weight_body(feat_ref, agg_ref, gfull_ref, out_ref):
    cols = feat_ref.shape[1]
    parts = out_ref.shape[0]
    piece = out_ref.shape[1] // 2
    for k, ref in enumerate((feat_ref, agg_ref)):
        left = ref[...]
        for c in range(gfull_ref.shape[0]):
            value = lax.dot_general(left, gfull_ref[c], ROWS, preferred_element_type=F32)
            out_ref[:, k * piece:(k + 1) * piece, c * cols:(c + 1) * cols] = value.reshape(
                parts, piece, cols
            ).astype(BF16)


def sum_body(scale, recv_ref, self_ref, neigh_ref):
    piece = self_ref.shape[0]
    for k, ref in enumerate((self_ref, neigh_ref)):
        total = jnp.zeros(ref.shape, F32)
        for d in range(recv_ref.shape[0]):
            total += recv_ref[d, k * piece:(k + 1) * piece].astype(F32)
        ref[...] = (total * scale).astype(BF16)


def scatter_body(count_ref, list_ref, ret_ref, total_ref, out_ref):
    onehot = row_onehot(count_ref, list_ref, total_ref.shape[0])
    out_ref[...] = (
        total_ref[...] + jnp.dot(onehot, ret_ref[...], preferred_element_type=F32)
    ).astype(BF16)


def local(
    features, w_self, w_neigh, grad_out, mirror_list, mirror_count, tile_dst, tile_src, tiles
):
    rows, cols = features.shape
    width = w_self.shape[1]
    peers, slots = mirror_list.shape
    mirrors = peers * slots
    tile_count, side, _ = tiles.shape
    reps = width // cols
    struct = jax.ShapeDtypeStruct
    rep = lax.axis_index("rep").astype(jnp.int32).reshape(1)

    outgoing = call(
        pick_body, struct((mirrors, cols), BF16),
        [("s", mirror_count), ("v", mirror_list), ("v", features)],
        flops=2 * mirrors * rows * cols, moved=600_000,
    )
    incoming = lax.all_to_all(
        outgoing.reshape(peers, slots, cols), "dom", split_axis=0, concat_axis=0, tiled=True
    ).reshape(mirrors, cols)
    part, own, agg, degree = call(
        forward_body,
        (
            struct((reps, rows, cols), BF16), struct((rows, cols), F32),
            struct((rows, cols), BF16), struct((rows, 128), F32),
        ),
        [
            ("s", rep), ("s", tile_dst), ("s", tile_src), ("v", features), ("v", incoming),
            ("v", tiles), ("v", w_self), ("v", w_neigh),
        ],
        scratch=[
            pltpu.VMEM((rows, tile_count * side), BF16),
            pltpu.VMEM((rows + mirrors, cols), BF16),
            pltpu.VMEM((tile_count * side, cols), BF16),
        ],
        flops=600_000_000, moved=3_000_000,
    )
    recv = lax.all_to_all(part, "rep", split_axis=0, concat_axis=0, tiled=True)
    hidden, grad_pre = call(
        gate_body, (struct((rows, cols), BF16), struct((rows, cols), BF16)),
        [("s", rep), ("v", recv), ("v", own), ("v", grad_out)],
        flops=2_000_000, moved=1_300_000,
    )
    grad_full = lax.all_gather(grad_pre, "rep", axis=0, tiled=False)
    piece = cols // peers
    partial = call(
        weight_body, struct((peers, 2 * piece, width), BF16),
        [("v", features), ("v", agg), ("v", grad_full)],
        flops=600_000_000, moved=2_000_000,
    )
    mirror_grad, total = call(
        back_body, (struct((mirrors, cols), BF16), struct((rows, cols), F32)),
        [
            ("s", tile_dst), ("s", tile_src), ("v", grad_full), ("v", w_self), ("v", w_neigh),
            ("v", degree), ("v", tiles),
        ],
        scratch=[pltpu.VMEM((rows, cols), BF16), pltpu.VMEM((rows + mirrors, cols), F32)],
        flops=600_000_000, moved=3_000_000,
    )
    returned = lax.all_to_all(
        mirror_grad.reshape(peers, slots, cols), "dom", split_axis=0, concat_axis=0, tiled=True
    ).reshape(mirrors, cols)
    gathered = lax.all_to_all(partial, "dom", split_axis=0, concat_axis=0, tiled=True)
    scale = float(rows * peers) ** (-0.5)
    mine_self, mine_neigh = call(
        functools.partial(sum_body, scale),
        (struct((piece, width), BF16), struct((piece, width), BF16)),
        [("v", gathered)], flops=1_000_000, moved=1_200_000,
    )
    out_self = lax.all_gather(mine_self, "dom", axis=0, tiled=True)
    out_neigh = lax.all_gather(mine_neigh, "dom", axis=0, tiled=True)
    grad_features = call(
        scatter_body, struct((rows, cols), BF16),
        [("s", mirror_count), ("v", mirror_list), ("v", returned), ("v", total)],
        flops=2 * mirrors * rows * cols, moved=700_000,
    )
    return hidden, grad_features, out_self, out_neigh


def solution(mesh):
    in_specs = (
        P("dom", "rep"),
        P("rep", None),
        P("rep", None),
        P("dom", "rep"),
        P("dom", None),
        P("dom"),
        P("dom"),
        P("dom"),
        P("dom", None, None),
    )
    out_specs = (P("dom", "rep"), P("dom", "rep"), P("rep", None), P("rep", None))
    return jax.shard_map(local, mesh=mesh, in_specs=in_specs, out_specs=out_specs, check_vma=False)
```

```python
import functools

import jax
import jax.numpy as jnp
from jax import lax
from jax.experimental import pallas as pl
from jax.experimental.pallas import tpu as pltpu
from jax.sharding import PartitionSpec as P

F32 = jnp.float32
BF16 = jnp.bfloat16
VMEM = pl.BlockSpec(memory_space=pltpu.VMEM)
SMEM = pl.BlockSpec(memory_space=pltpu.SMEM)
ROWS = (((0,), (0,)), ((), ()))
COLS = (((1,), (1,)), ((), ()))


def call(body, outs, ins, scratch=(), flops=0, moved=0):
    return pl.pallas_call(
        body,
        out_shape=outs,
        in_specs=[SMEM if spec == "s" else VMEM for spec, _ in ins],
        out_specs=jax.tree.map(lambda _: VMEM, outs),
        scratch_shapes=list(scratch),
        compiler_params=pltpu.CompilerParams(vmem_limit_bytes=32 * 1024 * 1024),
        cost_estimate=pl.CostEstimate(flops=flops, bytes_accessed=moved, transcendentals=0),
    )(*[array for _, array in ins])


def row_onehot(count_ref, list_ref, rows):
    peers, slots = list_ref.shape
    peer = lax.broadcasted_iota(jnp.int32, (peers, slots), 0)
    slot = lax.broadcasted_iota(jnp.int32, (peers, slots), 1)

    def fill(at, used):
        return jnp.where(peer == at, count_ref[at], used)

    used = jnp.zeros((peers, slots), jnp.int32)
    if peers <= 16:
        for at in range(peers):
            used = fill(at, used)
    else:
        used = lax.fori_loop(0, peers, fill, used)
    index = jnp.where(slot < used, list_ref[...], -1).astype(F32).astype(BF16)
    flat = peers * slots
    spread = (
        lax.broadcasted_iota(jnp.int32, (slots, flat), 0)
        == lax.broadcasted_iota(jnp.int32, (slots, flat), 1) % slots
    )
    wide = jnp.dot(index, spread.astype(F32).astype(BF16), preferred_element_type=F32)
    mine = (
        lax.broadcasted_iota(jnp.int32, (peers, flat), 0)
        == lax.broadcasted_iota(jnp.int32, (peers, flat), 1) // slots
    )
    line = jnp.sum(jnp.where(mine, wide, 0.0), axis=0, keepdims=True).astype(jnp.int32)
    hit = lax.broadcasted_iota(jnp.int32, (rows, flat), 0) == line
    return hit.astype(F32).astype(BF16)


def pick_body(count_ref, list_ref, feat_ref, out_ref):
    onehot = row_onehot(count_ref, list_ref, feat_ref.shape[0])
    out_ref[...] = lax.dot_general(
        onehot, feat_ref[...], ROWS, preferred_element_type=F32
    ).astype(BF16)


def forward_body(
    split, rep_ref, dst_ref, src_ref, feat_ref, inc_ref, tiles_ref, self_ref, neigh_ref, own_ref,
    agg_ref, deg_ref, *refs,
):
    part_refs, (adj_ref, table_ref, picked_ref) = refs[:-3], refs[-3:]
    rows, cols = feat_ref.shape
    slots, side, _ = tiles_ref.shape
    table_ref[:rows] = feat_ref[...]
    table_ref[rows:] = inc_ref[...]
    for t in range(slots):
        dst = dst_ref[t]
        tile = tiles_ref[t].astype(F32)
        for s in range(rows // side):
            adj_ref[s * side:(s + 1) * side, t * side:(t + 1) * side] = jnp.where(
                dst == s, tile, 0.0
            ).astype(BF16)
        start = pl.multiple_of(src_ref[t] * side, side)
        picked_ref[t * side:(t + 1) * side] = table_ref[pl.ds(start, side)]
    adj = adj_ref[...]
    summed = jnp.dot(adj, picked_ref[...], preferred_element_type=F32)
    degree = jnp.dot(adj, jnp.ones((slots * side, 128), BF16), preferred_element_type=F32)
    degree = jnp.maximum(degree, 1.0)
    deg_ref[...] = degree
    agg = (summed / jnp.concatenate([degree] * (cols // 128), axis=1)).astype(BF16)
    agg_ref[...] = agg
    feat = feat_ref[...]
    reps = self_ref.shape[1] // cols
    for c in range(reps):
        other = lax.bitwise_xor(rep_ref[0], c) if split else lax.rem(rep_ref[0] + c, reps)
        at = pl.ds(pl.multiple_of(other * cols, cols), cols)
        value = jnp.dot(feat, self_ref[:, at], preferred_element_type=F32) + jnp.dot(
            agg, neigh_ref[:, at], preferred_element_type=F32
        )
        if c == 0:
            own_ref[...] = value
        if not split:
            part_refs[0][other] = value.astype(BF16)
        elif c > 0:
            part_refs[c - 1][...] = value.astype(BF16)


def finish_gate(pre, gout_ref, hid_ref, gpre_ref):
    gate = jax.nn.sigmoid(pre)
    hid_ref[...] = (pre * gate).astype(BF16)
    grad = (gout_ref[...].astype(F32) * (gate + pre * gate * (1.0 - gate))).astype(BF16)
    gpre_ref[...] = grad
    return grad


def gate_body(rep_ref, recv_ref, own_ref, gout_ref, hid_ref, gpre_ref):
    pre = own_ref[...]
    for c in range(recv_ref.shape[0]):
        pre = pre + jnp.where(rep_ref[0] == c, 0.0, recv_ref[c].astype(F32))
    finish_gate(pre, gout_ref, hid_ref, gpre_ref)


def gate_blocks_body(reps, dom_ref, own_ref, gout_ref, *refs):
    blocks, (hid_ref, gpre_ref), send_refs = refs[:-4], refs[-4:-2], refs[-2:]
    pre = own_ref[...]
    for block in blocks:
        pre = pre + block[...].astype(F32)
    finish_gate(pre, gout_ref, hid_ref, gpre_ref)
    halves = len(send_refs)
    for turn, ref in enumerate(send_refs):
        half = lax.rem(turn + dom_ref[0] // reps, halves)
        lanes = ref.shape[1]
        ref[...] = gpre_ref[:, pl.ds(pl.multiple_of(half * lanes, lanes), lanes)]


def back_body(
    dst_ref, src_ref, gfull_ref, self_ref, neigh_ref, deg_ref, tiles_ref,
    mirror_ref, total_ref, gagg_ref, table_ref,
):
    rows, cols = total_ref.shape
    slots, side, _ = tiles_ref.shape
    direct = jnp.zeros((rows, cols), F32)
    gagg = jnp.zeros((rows, cols), F32)
    for c in range(gfull_ref.shape[0]):
        at = slice(c * cols, (c + 1) * cols)
        direct += lax.dot_general(gfull_ref[c], self_ref[:, at], COLS, preferred_element_type=F32)
        gagg += lax.dot_general(gfull_ref[c], neigh_ref[:, at], COLS, preferred_element_type=F32)
    gagg_ref[...] = (gagg / jnp.concatenate([deg_ref[...]] * (cols // 128), axis=1)).astype(BF16)
    table_ref[:rows] = direct
    table_ref[rows:] = jnp.zeros((table_ref.shape[0] - rows, cols), F32)
    for t in range(slots):
        dst = pl.multiple_of(dst_ref[t] * side, side)
        src = pl.multiple_of(src_ref[t] * side, side)
        table_ref[pl.ds(src, side)] += lax.dot_general(
            tiles_ref[t], gagg_ref[pl.ds(dst, side)], ROWS, preferred_element_type=F32
        )
    total_ref[...] = table_ref[:rows]
    mirror_ref[...] = table_ref[rows:].astype(BF16)


def weight_body(feat_ref, agg_ref, gfull_ref, out_ref):
    cols = feat_ref.shape[1]
    parts = out_ref.shape[0]
    piece = out_ref.shape[1] // 2
    for k, ref in enumerate((feat_ref, agg_ref)):
        left = ref[...]
        for c in range(gfull_ref.shape[0]):
            value = lax.dot_general(left, gfull_ref[c], ROWS, preferred_element_type=F32)
            out_ref[:, k * piece:(k + 1) * piece, c * cols:(c + 1) * cols] = value.reshape(
                parts, piece, cols
            ).astype(BF16)


def sum_body(scale, recv_ref, self_ref, neigh_ref):
    piece = self_ref.shape[0]
    for k, ref in enumerate((self_ref, neigh_ref)):
        total = jnp.zeros(ref.shape, F32)
        for d in range(recv_ref.shape[0]):
            total += recv_ref[d, k * piece:(k + 1) * piece].astype(F32)
        ref[...] = (total * scale).astype(BF16)


def whole_weight_body(scale, peers, reps, place_ref, *refs):
    feats, aggs = refs[:peers], refs[peers:2 * peers]
    grads = refs[2 * peers:-2]
    out_ref, hold_ref = refs[-2:]
    dom, rep = place_ref[0], place_ref[1]
    halves = peers // reps
    for at, ref in enumerate(grads):
        turn, offset = at // reps, at % reps
        owner = lax.bitwise_xor(rep, offset) + reps * lax.rem(dom + halves - turn, halves)
        hold_ref[owner] = ref[...]
    self_total = jnp.zeros(out_ref.shape[1:], F32)
    neigh_total = jnp.zeros(out_ref.shape[1:], F32)
    for offset in range(peers):
        grad = hold_ref[lax.bitwise_xor(dom, offset)]
        self_total += lax.dot_general(feats[offset][...], grad, ROWS, preferred_element_type=F32)
        neigh_total += lax.dot_general(aggs[offset][...], grad, ROWS, preferred_element_type=F32)
    out_ref[0] = (self_total * scale).astype(BF16)
    out_ref[1] = (neigh_total * scale).astype(BF16)


def place_body(dom_ref, *refs):
    blocks, (self_ref, neigh_ref) = refs[:-2], refs[-2:]
    lanes = blocks[0].shape[2]
    for offset, block in enumerate(blocks):
        at = pl.multiple_of(lax.bitwise_xor(dom_ref[0], offset) * lanes, lanes)
        self_ref[:, pl.ds(at, lanes)] = block[0]
        neigh_ref[:, pl.ds(at, lanes)] = block[1]


def scatter_body(count_ref, list_ref, ret_ref, total_ref, out_ref):
    onehot = row_onehot(count_ref, list_ref, total_ref.shape[0])
    out_ref[...] = (
        total_ref[...] + jnp.dot(onehot, ret_ref[...], preferred_element_type=F32)
    ).astype(BF16)


def swap(array, axis, offset, count):
    return lax.ppermute(array, axis, [(i, i ^ offset) for i in range(count)])


def gather_rows(array, peers):
    out = {offset: swap(array, "dom", offset, peers) for offset in range(2, peers, 2)}
    out[0] = array
    for offset in range(0, peers, 2):
        out[offset + 1] = swap(out[offset], "dom", 1, peers)
    return [out[offset] for offset in range(peers)]


def local(
    features, w_self, w_neigh, grad_out, mirror_list, mirror_count, tile_dst, tile_src, tiles
):
    rows, cols = features.shape
    width = w_self.shape[1]
    peers, slots = mirror_list.shape
    mirrors = peers * slots
    tile_count, side, _ = tiles.shape
    reps = width // cols
    struct = jax.ShapeDtypeStruct
    rep = lax.axis_index("rep").astype(jnp.int32).reshape(1)
    dom = lax.axis_index("dom").astype(jnp.int32).reshape(1)

    outgoing = call(
        pick_body, struct((mirrors, cols), BF16),
        [("s", mirror_count), ("v", mirror_list), ("v", features)],
        flops=2 * mirrors * rows * cols, moved=600_000,
    )
    incoming = lax.all_to_all(
        outgoing.reshape(peers, slots, cols), "dom", split_axis=0, concat_axis=0, tiled=True
    ).reshape(mirrors, cols)
    lanes = width // peers
    two_stage = peers == 2 * reps and peers & (peers - 1) == 0 and lanes % 128 == 0
    block = struct((rows, cols), BF16)
    own, agg, degree, *parts = call(
        functools.partial(forward_body, two_stage),
        (struct((rows, cols), F32), block, struct((rows, 128), F32))
        + ((block,) * (reps - 1) if two_stage else (struct((reps, rows, cols), BF16),)),
        [
            ("s", rep), ("s", tile_dst), ("s", tile_src), ("v", features), ("v", incoming),
            ("v", tiles), ("v", w_self), ("v", w_neigh),
        ],
        scratch=[
            pltpu.VMEM((rows, tile_count * side), BF16),
            pltpu.VMEM((rows + mirrors, cols), BF16),
            pltpu.VMEM((tile_count * side, cols), BF16),
        ],
        flops=600_000_000, moved=3_000_000,
    )
    scale = float(rows * peers) ** (-0.5)
    if two_stage:
        halves = peers // reps
        kept = gather_rows(features, peers)
        kept_agg = gather_rows(agg, peers)
        blocks = [swap(parts[offset - 1], "rep", offset, reps) for offset in range(1, reps)]
        hidden, grad_pre, *send = call(
            functools.partial(gate_blocks_body, reps), (block, block) + (struct((rows, lanes), BF16),) * halves,
            [("s", dom), ("v", own), ("v", grad_out)] + [("v", got) for got in blocks],
            flops=2_000_000, moved=1_300_000,
        )
    else:
        recv = lax.all_to_all(parts[0], "rep", split_axis=0, concat_axis=0, tiled=True)
        hidden, grad_pre = call(
            gate_body, (struct((rows, cols), BF16), struct((rows, cols), BF16)),
            [("s", rep), ("v", recv), ("v", own), ("v", grad_out)],
            flops=2_000_000, moved=1_300_000,
        )
    grad_full = lax.all_gather(grad_pre, "rep", axis=0, tiled=False)
    mirror_grad, total = call(
        back_body, (struct((mirrors, cols), BF16), struct((rows, cols), F32)),
        [
            ("s", tile_dst), ("s", tile_src), ("v", grad_full), ("v", w_self), ("v", w_neigh),
            ("v", degree), ("v", tiles),
        ],
        scratch=[pltpu.VMEM((rows, cols), BF16), pltpu.VMEM((rows + mirrors, cols), F32)],
        flops=600_000_000, moved=3_000_000,
    )
    returned = lax.all_to_all(
        mirror_grad.reshape(peers, slots, cols), "dom", split_axis=0, concat_axis=0, tiled=True
    ).reshape(mirrors, cols)
    if two_stage:
        columns = []
        for turn in range(halves):
            perm = []
            for p in range(peers):
                for r in range(reps):
                    half = (turn + p // reps) % halves
                    perm.append((p * reps + r, (halves * r + half) * reps + p % reps))
            got = lax.ppermute(send[turn], ("dom", "rep"), perm)
            columns += [got] + [swap(got, "rep", offset, reps) for offset in range(1, reps)]
        mine = call(
            functools.partial(whole_weight_body, scale, peers, reps),
            struct((2, rows, lanes), BF16),
            [("s", jnp.concatenate([dom, rep]))]
            + [("v", part) for part in kept + kept_agg + columns],
            scratch=[pltpu.VMEM((peers, rows, lanes), BF16)],
            flops=600_000_000, moved=3_000_000,
        )
        pieces = gather_rows(mine, peers)
        out_self, out_neigh = call(
            place_body, (struct((rows, width), BF16), struct((rows, width), BF16)),
            [("s", dom)] + [("v", part) for part in pieces], moved=2_000_000,
        )
    else:
        piece = cols // peers
        partial = call(
            weight_body, struct((peers, 2 * piece, width), BF16),
            [("v", features), ("v", agg), ("v", grad_full)],
            flops=600_000_000, moved=2_000_000,
        )
        gathered = lax.all_to_all(partial, "dom", split_axis=0, concat_axis=0, tiled=True)
        mine_self, mine_neigh = call(
            functools.partial(sum_body, scale),
            (struct((piece, width), BF16), struct((piece, width), BF16)),
            [("v", gathered)], flops=1_000_000, moved=1_200_000,
        )
        out_self = lax.all_gather(mine_self, "dom", axis=0, tiled=True)
        out_neigh = lax.all_gather(mine_neigh, "dom", axis=0, tiled=True)
    grad_features = call(
        scatter_body, struct((rows, cols), BF16),
        [("s", mirror_count), ("v", mirror_list), ("v", returned), ("v", total)],
        flops=2 * mirrors * rows * cols, moved=700_000,
    )
    return hidden, grad_features, out_self, out_neigh


def solution(mesh):
    in_specs = (
        P("dom", "rep"),
        P("rep", None),
        P("rep", None),
        P("dom", "rep"),
        P("dom", None),
        P("dom"),
        P("dom"),
        P("dom"),
        P("dom", None, None),
    )
    out_specs = (P("dom", "rep"), P("dom", "rep"), P("rep", None), P("rep", None))
    return jax.shard_map(local, mesh=mesh, in_specs=in_specs, out_specs=out_specs, check_vma=False)
```

```python
import functools

import jax
import jax.numpy as jnp
from jax import lax
from jax.experimental import pallas as pl
from jax.experimental.pallas import tpu as pltpu
from jax.sharding import PartitionSpec as P

F32 = jnp.float32
BF16 = jnp.bfloat16
SPECS = {
    "v": pl.BlockSpec(memory_space=pltpu.VMEM),
    "s": pl.BlockSpec(memory_space=pltpu.SMEM),
    "h": pl.BlockSpec(memory_space=pltpu.HBM),
}
ROWS = (((0,), (0,)), ((), ()))
COLS = (((1,), (1,)), ((), ()))


def call(body, outs, ins, scratch=(), flops=0, moved=0):
    return pl.pallas_call(
        body,
        out_shape=outs,
        in_specs=[SPECS[spec] for spec, _ in ins],
        out_specs=jax.tree.map(lambda _: SPECS["v"], outs),
        scratch_shapes=list(scratch),
        compiler_params=pltpu.CompilerParams(vmem_limit_bytes=32 * 1024 * 1024),
        cost_estimate=pl.CostEstimate(flops=flops, bytes_accessed=moved, transcendentals=0),
    )(*[array for _, array in ins])


def dot(left, right, dims=(((1,), (0,)), ((), ()))):
    return lax.dot_general(left, right, dims, preferred_element_type=F32)


def block_rows(place, offset, size):
    return pl.ds(pl.multiple_of(lax.bitwise_xor(place, offset) * size, size), size)


def row_onehot(count_ref, lists, rows):
    peers, slots = lists.shape
    peer = lax.broadcasted_iota(jnp.int32, (peers, slots), 0)
    slot = lax.broadcasted_iota(jnp.int32, (peers, slots), 1)

    def fill(at, used):
        return jnp.where(peer == at, count_ref[at], used)

    used = jnp.zeros((peers, slots), jnp.int32)
    if peers <= 16:
        for at in range(peers):
            used = fill(at, used)
    else:
        used = lax.fori_loop(0, peers, fill, used)
    index = jnp.where(slot < used, lists, -1).astype(F32).astype(BF16)
    flat = peers * slots
    spread = (
        lax.broadcasted_iota(jnp.int32, (slots, flat), 0)
        == lax.broadcasted_iota(jnp.int32, (slots, flat), 1) % slots
    )
    wide = dot(index, spread.astype(F32).astype(BF16))
    mine = (
        lax.broadcasted_iota(jnp.int32, (peers, flat), 0)
        == lax.broadcasted_iota(jnp.int32, (peers, flat), 1) // slots
    )
    line = jnp.sum(jnp.where(mine, wide, 0.0), axis=0, keepdims=True).astype(jnp.int32)
    hit = lax.broadcasted_iota(jnp.int32, (rows, flat), 0) == line
    return hit.astype(F32).astype(BF16)


def pick_body(dom_ref, count_hbm, list_hbm, feat_hbm, onehot_ref, *refs):
    out_refs, (count_ref, list_ref, feat_ref, picked_ref, sems) = refs[:-5], refs[-5:]
    copies = [
        pltpu.make_async_copy(src, dst, sems.at[k])
        for k, (src, dst) in enumerate(
            ((count_hbm, count_ref), (list_hbm, list_ref), (feat_hbm, feat_ref))
        )
    ]
    for copy in copies:
        copy.start()
    for copy in copies:
        copy.wait()
    onehot = row_onehot(count_ref, list_ref[...], feat_ref.shape[0])
    onehot_ref[...] = onehot
    picked = dot(onehot, feat_ref[...], ROWS).astype(BF16)
    if len(out_refs) == 1:
        out_refs[0][...] = picked
        return
    picked_ref[...] = picked
    for offset, ref in enumerate(out_refs):
        ref[...] = picked_ref[block_rows(dom_ref[0], offset, ref.shape[0])]


def prep_body(
    split, rep_ref, dst_ref, src_ref, feat_ref, tiles_ref, self_ref,
    high_ref, low_ref, deg_ref, base_ref, adj_ref,
):
    slots, side, _ = tiles_ref.shape
    reps, _, cols = base_ref.shape
    adj_ref[...] = jnp.zeros(adj_ref.shape, F32)
    for t in range(slots):
        dst = pl.ds(pl.multiple_of(dst_ref[t] * side, side), side)
        src = pl.ds(pl.multiple_of(src_ref[t] * side, side), side)
        adj_ref[dst, src] += tiles_ref[t].astype(F32)
    adj = adj_ref[...]
    high = adj.astype(BF16)
    high_ref[...] = high
    low_ref[...] = (adj - high.astype(F32)).astype(BF16)
    degree = jnp.maximum(jnp.sum(adj, axis=1, keepdims=True), 1.0)
    deg_ref[...] = jnp.broadcast_to(degree, deg_ref.shape)
    feat = feat_ref[...]
    for c in range(reps):
        base_ref[c] = dot(feat, self_ref[:, column_block(split, rep_ref[0], c, reps, cols)])


def column_block(split, rep, c, reps, cols):
    other = lax.bitwise_xor(rep, c) if split else c
    return pl.ds(pl.multiple_of(other * cols, cols), cols)


def wide_degree(deg_ref, cols):
    return jnp.concatenate([deg_ref[...]] * (cols // deg_ref.shape[1]), axis=1)


def aggregate_body(
    split, incoming, dom_ref, rep_ref, feat_ref, high_ref, low_ref, deg_ref, base_ref, neigh_ref,
    *refs,
):
    inc_refs, (own_ref, agg_ref), part_refs, table_ref = (
        refs[:incoming], refs[incoming:incoming + 2], refs[incoming + 2:-1], refs[-1]
    )
    rows, cols = feat_ref.shape
    table_ref[:rows] = feat_ref[...]
    if split:
        for offset, ref in enumerate(inc_refs):
            size = ref.shape[0]
            at = rows + lax.bitwise_xor(dom_ref[0], offset) * size
            table_ref[pl.ds(pl.multiple_of(at, size), size)] = ref[...]
    else:
        table_ref[rows:] = inc_refs[0][...]
    table = table_ref[...]
    summed = dot(high_ref[...], table) + dot(low_ref[...], table)
    agg = (summed / wide_degree(deg_ref, cols)).astype(BF16)
    agg_ref[...] = agg
    reps = base_ref.shape[0]
    for c in range(reps):
        value = base_ref[c] + dot(agg, neigh_ref[:, column_block(split, rep_ref[0], c, reps, cols)])
        if not split:
            part_refs[0][c] = value.astype(BF16)

            @pl.when(rep_ref[0] == c)
            def _():
                own_ref[...] = value
        elif c == 0:
            own_ref[...] = value
        else:
            part_refs[c - 1][...] = value.astype(BF16)


def finish_gate(pre, gout_ref, hid_ref, gpre_ref):
    gate = jax.nn.sigmoid(pre)
    hid_ref[...] = (pre * gate).astype(BF16)
    gpre_ref[...] = (gout_ref[...].astype(F32) * (gate + pre * gate * (1.0 - gate))).astype(BF16)


def gate_body(rep_ref, recv_ref, own_ref, gout_ref, hid_ref, gpre_ref):
    pre = own_ref[...]
    for c in range(recv_ref.shape[0]):
        pre = pre + jnp.where(rep_ref[0] == c, 0.0, recv_ref[c].astype(F32))
    finish_gate(pre, gout_ref, hid_ref, gpre_ref)


def gate_blocks_body(reps, dom_ref, own_ref, gout_ref, *refs):
    blocks, (hid_ref, gpre_ref), send_refs = refs[:reps - 1], refs[reps - 1:reps + 1], refs[reps + 1:]
    pre = own_ref[...]
    for block in blocks:
        pre = pre + block[...].astype(F32)
    finish_gate(pre, gout_ref, hid_ref, gpre_ref)
    halves = len(send_refs)
    for turn, ref in enumerate(send_refs):
        half = lax.rem(turn + dom_ref[0] // reps, halves)
        lanes = ref.shape[1]
        ref[...] = gpre_ref[:, pl.ds(pl.multiple_of(half * lanes, lanes), lanes)]


def back_body(
    split, given, dom_ref, rep_ref, high_ref, low_ref, deg_ref, self_ref, neigh_ref, *refs,
):
    grads, total_ref, mirror_refs, table_ref = (
        refs[:given], refs[given], refs[given + 1:-1], refs[-1]
    )
    rows, cols = total_ref.shape
    reps = self_ref.shape[1] // cols
    direct = jnp.zeros((rows, cols), F32)
    gagg = jnp.zeros((rows, cols), F32)
    for c in range(reps):
        grad = grads[c][...] if split else grads[0][c]
        at = column_block(split, rep_ref[0], c, reps, cols)
        gagg += dot(grad, neigh_ref[:, at], COLS)
        direct += dot(grad, self_ref[:, at], COLS)
    gagg = (gagg / wide_degree(deg_ref, cols)).astype(BF16)
    table = dot(high_ref[...], gagg, ROWS) + dot(low_ref[...], gagg, ROWS)
    total_ref[...] = direct + table[:rows]
    if not split:
        mirror_refs[0][...] = table[rows:].astype(BF16)
        return
    table_ref[...] = table[rows:].astype(BF16)
    for offset, ref in enumerate(mirror_refs):
        ref[...] = table_ref[block_rows(dom_ref[0], offset, ref.shape[0])]


def weight_body(feat_ref, agg_ref, gfull_ref, out_ref):
    cols = feat_ref.shape[1]
    parts = out_ref.shape[0]
    piece = out_ref.shape[1] // 2
    for k, ref in enumerate((feat_ref, agg_ref)):
        left = ref[...]
        for c in range(gfull_ref.shape[0]):
            value = dot(left, gfull_ref[c], ROWS)
            out_ref[:, k * piece:(k + 1) * piece, c * cols:(c + 1) * cols] = value.reshape(
                parts, piece, cols
            ).astype(BF16)


def sum_body(scale, recv_ref, self_ref, neigh_ref):
    piece = self_ref.shape[0]
    for k, ref in enumerate((self_ref, neigh_ref)):
        total = jnp.zeros(ref.shape, F32)
        for d in range(recv_ref.shape[0]):
            total += recv_ref[d, k * piece:(k + 1) * piece].astype(F32)
        ref[...] = (total * scale).astype(BF16)


def whole_weight_body(scale, peers, reps, dom_ref, rep_ref, *refs):
    even = peers // 2
    kept, grads, (out_ref, hold_ref) = refs[:2 * (even + 1)], refs[2 * (even + 1):-2], refs[-2:]
    dom, rep = dom_ref[0], rep_ref[0]
    halves = peers // reps
    for offset, ref in enumerate(grads):
        for turn in range(halves):
            owner = lax.bitwise_xor(rep, offset) + reps * lax.rem(dom + halves - turn, halves)
            hold_ref[owner] = ref[turn]
    for k in range(2):
        mine = kept[k * (even + 1):(k + 1) * (even + 1)]
        total = jnp.zeros(out_ref.shape[1:], F32)
        for offset in range(peers):
            left = mine[even][offset // 2] if offset % 2 else mine[offset // 2][...]
            total += dot(left, hold_ref[lax.bitwise_xor(dom, offset)], ROWS)
        out_ref[k] = (total * scale).astype(BF16)


def place_body(dom_ref, *refs):
    blocks, (self_ref, neigh_ref) = refs[:-2], refs[-2:]
    lanes = blocks[0].shape[2]
    for offset, block in enumerate(blocks):
        at = block_rows(dom_ref[0], offset, lanes)
        self_ref[:, at] = block[0]
        neigh_ref[:, at] = block[1]


def scatter_body(dom_ref, onehot_ref, total_ref, *refs):
    rets, (out_ref, table_ref) = refs[:-2], refs[-2:]
    if len(rets) == 1:
        table = rets[0][...]
    else:
        for offset, ref in enumerate(rets):
            table_ref[block_rows(dom_ref[0], offset, ref.shape[0])] = ref[...]
        table = table_ref[...]
    out_ref[...] = (total_ref[...] + dot(onehot_ref[...], table)).astype(BF16)


def swap(array, axis, offset):
    return lax.ppermute(array, axis, [(i, i ^ offset) for i in range(lax.axis_size(axis))])


def swap_all(blocks, axis):
    return [blocks[0]] + [swap(blocks[k], axis, k) for k in range(1, len(blocks))]


def gather_columns(array):
    beside = swap(array, "rep", 1)
    across = swap(array, "rep", 2)
    return [array, beside, across, swap(across, "rep", 1)]


def gather_rows(array, peers):
    even = [array] + [swap(array, "dom", offset) for offset in range(2, peers, 2)]
    return even + [swap(jnp.stack(even), "dom", 1)]


def gather_pieces(array, peers):
    out = {offset: swap(array, "dom", offset) for offset in range(peers - 2, 0, -2)}
    out[0] = array
    for offset in range(0, peers, 2):
        out[offset + 1] = swap(out[offset], "dom", 1)
    return [out[offset] for offset in range(peers)]


def local(
    features, w_self, w_neigh, grad_out, mirror_list, mirror_count, tile_dst, tile_src, tiles
):
    rows, cols = features.shape
    width = w_self.shape[1]
    peers, slots = mirror_list.shape
    mirrors = peers * slots
    table_rows = rows + mirrors
    reps = width // cols
    struct = jax.ShapeDtypeStruct
    block = struct((rows, cols), BF16)
    rep = lax.axis_index("rep").astype(jnp.int32).reshape(1)
    dom = lax.axis_index("dom").astype(jnp.int32).reshape(1)
    lanes = width // peers
    halves = peers // reps
    split = peers == 8 and reps == 4 and slots % 16 == 0 and lanes % 128 == 0
    mirror_outs = (struct((slots, cols), BF16),) * peers if split else (struct((mirrors, cols), BF16),)

    def exchange(blocks):
        if split:
            return swap_all(blocks, "dom")
        got = lax.all_to_all(
            blocks[0].reshape(peers, slots, cols), "dom", split_axis=0, concat_axis=0, tiled=True
        )
        return [got.reshape(mirrors, cols)]

    onehot, *outgoing = call(
        pick_body, (struct((rows, mirrors), BF16),) + mirror_outs,
        [("s", dom), ("h", mirror_count), ("h", mirror_list), ("h", features)],
        scratch=[
            pltpu.SMEM(mirror_count.shape, jnp.int32), pltpu.VMEM(mirror_list.shape, jnp.int32),
            pltpu.VMEM((rows, cols), BF16), pltpu.VMEM((mirrors, cols), BF16),
            pltpu.SemaphoreType.DMA((3,)),
        ],
        flops=2 * mirrors * rows * cols, moved=600_000,
    )
    incoming = exchange(outgoing)
    tiles_late, feat_late, *_ = lax.optimization_barrier((tiles, features, outgoing[0]))
    high, low, degree, base = call(
        functools.partial(prep_body, split),
        (
            struct((rows, table_rows), BF16), struct((rows, table_rows), BF16),
            struct((rows, 128), F32), struct((reps, rows, cols), F32),
        ),
        [
            ("s", rep), ("s", tile_dst), ("s", tile_src), ("v", feat_late), ("v", tiles_late),
            ("v", w_self),
        ],
        scratch=[pltpu.VMEM((rows, table_rows), F32)],
        flops=200_000_000, moved=3_000_000,
    )
    if split:
        kept = gather_rows(feat_late, peers)
    own, agg, *parts = call(
        functools.partial(aggregate_body, split, len(incoming)),
        (struct((rows, cols), F32), block)
        + ((block,) * (reps - 1) if split else (struct((reps, rows, cols), BF16),)),
        [
            ("s", dom), ("s", rep), ("v", feat_late), ("v", high), ("v", low), ("v", degree),
            ("v", base), ("v", w_neigh),
        ] + [("v", got) for got in incoming],
        scratch=[pltpu.VMEM((table_rows, cols), BF16)],
        flops=400_000_000, moved=3_000_000,
    )
    scale = float(rows * peers) ** (-0.5)
    if split:
        blocks = swap_all([own] + list(parts), "rep")
        kept_agg = gather_rows(agg, peers)
        hidden, grad_pre, *send = call(
            functools.partial(gate_blocks_body, reps),
            (block, block) + (struct((rows, lanes), BF16),) * halves,
            [("s", dom), ("v", own), ("v", grad_out)] + [("v", got) for got in blocks[1:]],
            flops=2_000_000, moved=1_300_000,
        )
        halved = []
        for turn in range(halves):
            perm = []
            for p in range(peers):
                for r in range(reps):
                    half = (turn + p // reps) % halves
                    perm.append((p * reps + r, (halves * r + half) * reps + p % reps))
            halved.append(lax.ppermute(send[turn], ("dom", "rep"), perm))
        grad_full = gather_columns(grad_pre)
        columns = gather_columns(jnp.stack(halved))
    else:
        recv = lax.all_to_all(parts[0], "rep", split_axis=0, concat_axis=0, tiled=True)
        hidden, grad_pre = call(
            gate_body, (block, block),
            [("s", rep), ("v", recv), ("v", own), ("v", grad_out)],
            flops=2_000_000, moved=1_300_000,
        )
        grad_full = [lax.all_gather(grad_pre, "rep", axis=0, tiled=False)]
    total, *mirror_grad = call(
        functools.partial(back_body, split, len(grad_full)),
        (struct((rows, cols), F32),) + mirror_outs,
        [
            ("s", dom), ("s", rep), ("v", high), ("v", low), ("v", degree), ("v", w_self),
            ("v", w_neigh),
        ] + [("v", got) for got in grad_full],
        scratch=[pltpu.VMEM((mirrors, cols), BF16)],
        flops=600_000_000, moved=3_000_000,
    )
    if split:
        mine = call(
            functools.partial(whole_weight_body, scale, peers, reps),
            struct((2, rows, lanes), BF16),
            [("s", dom), ("s", rep)] + [("v", part) for part in kept + kept_agg + columns],
            scratch=[pltpu.VMEM((peers, rows, lanes), BF16)],
            flops=600_000_000, moved=3_000_000,
        )
        pieces = gather_pieces(mine, peers)
    returned = exchange(mirror_grad)
    grad_features = call(
        scatter_body, block,
        [("s", dom), ("v", onehot), ("v", total)] + [("v", got) for got in returned],
        scratch=[pltpu.VMEM((mirrors, cols), BF16)],
        flops=2 * mirrors * rows * cols, moved=700_000,
    )
    if split:
        out_self, out_neigh = call(
            place_body, (struct((rows, width), BF16), struct((rows, width), BF16)),
            [("s", dom)] + [("v", part) for part in pieces], moved=2_000_000,
        )
    else:
        piece = cols // peers
        partial = call(
            weight_body, struct((peers, 2 * piece, width), BF16),
            [("v", features), ("v", agg), ("v", grad_full[0])],
            flops=600_000_000, moved=2_000_000,
        )
        gathered = lax.all_to_all(partial, "dom", split_axis=0, concat_axis=0, tiled=True)
        mine_self, mine_neigh = call(
            functools.partial(sum_body, scale),
            (struct((piece, width), BF16), struct((piece, width), BF16)),
            [("v", gathered)], flops=1_000_000, moved=1_200_000,
        )
        out_self = lax.all_gather(mine_self, "dom", axis=0, tiled=True)
        out_neigh = lax.all_gather(mine_neigh, "dom", axis=0, tiled=True)
    return hidden, grad_features, out_self, out_neigh


def solution(mesh):
    in_specs = (
        P("dom", "rep"),
        P("rep", None),
        P("rep", None),
        P("dom", "rep"),
        P("dom", None),
        P("dom"),
        P("dom"),
        P("dom"),
        P("dom", None, None),
    )
    out_specs = (P("dom", "rep"), P("dom", "rep"), P("rep", None), P("rep", None))
    return jax.shard_map(local, mesh=mesh, in_specs=in_specs, out_specs=out_specs, check_vma=False)
```

```python
import functools

import jax
import jax.numpy as jnp
from jax import lax
from jax.experimental import pallas as pl
from jax.experimental.pallas import tpu as pltpu
from jax.sharding import PartitionSpec as P

F32 = jnp.float32
BF16 = jnp.bfloat16
SPECS = {
    "v": pl.BlockSpec(memory_space=pltpu.VMEM),
    "s": pl.BlockSpec(memory_space=pltpu.SMEM),
    "h": pl.BlockSpec(memory_space=pltpu.HBM),
}
ROWS = (((0,), (0,)), ((), ()))
COLS = (((1,), (1,)), ((), ()))


def call(body, outs, ins, scratch=(), flops=0, moved=0):
    return pl.pallas_call(
        body,
        out_shape=outs,
        in_specs=[SPECS[spec] for spec, _ in ins],
        out_specs=jax.tree.map(lambda _: SPECS["v"], outs),
        scratch_shapes=list(scratch),
        compiler_params=pltpu.CompilerParams(vmem_limit_bytes=32 * 1024 * 1024),
        cost_estimate=pl.CostEstimate(flops=flops, bytes_accessed=moved, transcendentals=0),
    )(*[array for _, array in ins])


def dot(left, right, dims=(((1,), (0,)), ((), ()))):
    return lax.dot_general(left, right, dims, preferred_element_type=F32)


def block_rows(place, offset, size):
    return pl.ds(pl.multiple_of(lax.bitwise_xor(place, offset) * size, size), size)


def row_onehot(count_ref, lists, rows):
    peers, slots = lists.shape
    peer = lax.broadcasted_iota(jnp.int32, (peers, slots), 0)
    slot = lax.broadcasted_iota(jnp.int32, (peers, slots), 1)

    def fill(at, used):
        return jnp.where(peer == at, count_ref[at], used)

    used = jnp.zeros((peers, slots), jnp.int32)
    if peers <= 16:
        for at in range(peers):
            used = fill(at, used)
    else:
        used = lax.fori_loop(0, peers, fill, used)
    index = jnp.where(slot < used, lists, -1).astype(F32).astype(BF16)
    flat = peers * slots
    spread = (
        lax.broadcasted_iota(jnp.int32, (slots, flat), 0)
        == lax.broadcasted_iota(jnp.int32, (slots, flat), 1) % slots
    )
    wide = dot(index, spread.astype(F32).astype(BF16))
    mine = (
        lax.broadcasted_iota(jnp.int32, (peers, flat), 0)
        == lax.broadcasted_iota(jnp.int32, (peers, flat), 1) // slots
    )
    line = jnp.sum(jnp.where(mine, wide, 0.0), axis=0, keepdims=True).astype(jnp.int32)
    hit = lax.broadcasted_iota(jnp.int32, (rows, flat), 0) == line
    return hit.astype(F32).astype(BF16)


def pick_body(
    count_hbm, list_hbm, feat_hbm, onehot_ref, out_ref, count_ref, list_ref, feat_ref, sems
):
    copies = [
        pltpu.make_async_copy(src, dst, sems.at[k])
        for k, (src, dst) in enumerate(
            ((count_hbm, count_ref), (list_hbm, list_ref), (feat_hbm, feat_ref))
        )
    ]
    for copy in copies:
        copy.start()
    for copy in copies:
        copy.wait()
    onehot = row_onehot(count_ref, list_ref[...], feat_ref.shape[0])
    onehot_ref[...] = onehot
    out_ref[...] = dot(onehot, feat_ref[...], ROWS).astype(BF16)


def prep_body(
    dst_ref, src_ref, tiles_ref, self_hbm, neigh_hbm,
    high_ref, low_ref, deg_ref, self_ref, neigh_ref, adj_ref, sems,
):
    copies = [
        pltpu.make_async_copy(src, dst, sems.at[k])
        for k, (src, dst) in enumerate(((self_hbm, self_ref), (neigh_hbm, neigh_ref)))
    ]
    for copy in copies:
        copy.start()
    slots, side, _ = tiles_ref.shape
    adj_ref[...] = jnp.zeros(adj_ref.shape, F32)
    for t in range(slots):
        dst = pl.ds(pl.multiple_of(dst_ref[t] * side, side), side)
        src = pl.ds(pl.multiple_of(src_ref[t] * side, side), side)
        adj_ref[dst, src] += tiles_ref[t].astype(F32)
    adj = adj_ref[...]
    high = adj.astype(BF16)
    high_ref[...] = high
    low_ref[...] = (adj - high.astype(F32)).astype(BF16)
    degree = jnp.maximum(jnp.sum(adj, axis=1, keepdims=True), 1.0)
    deg_ref[...] = jnp.broadcast_to(degree, deg_ref.shape)
    for copy in copies:
        copy.wait()


def column_block(split, rep, c, reps, cols):
    other = lax.bitwise_xor(rep, c) if split else c
    return pl.ds(pl.multiple_of(other * cols, cols), cols)


def wide_degree(deg_ref, cols):
    return jnp.concatenate([deg_ref[...]] * (cols // deg_ref.shape[1]), axis=1)


def aggregate_body(
    split, rep_ref, feat_ref, inc_ref, high_ref, low_ref, deg_ref, self_ref, neigh_ref,
    own_ref, agg_ref, *refs,
):
    part_refs, table_ref = refs[:-1], refs[-1]
    rows, cols = feat_ref.shape
    feat = feat_ref[...]
    table_ref[:rows] = feat
    table_ref[rows:] = inc_ref[...]
    table = table_ref[...]
    summed = dot(high_ref[...], table) + dot(low_ref[...], table)
    agg = (summed / wide_degree(deg_ref, cols)).astype(BF16)
    agg_ref[...] = agg
    reps = self_ref.shape[1] // cols
    for c in reversed(range(reps)):
        at = column_block(split, rep_ref[0], c, reps, cols)
        value = dot(feat, self_ref[:, at]) + dot(agg, neigh_ref[:, at])
        if not split:
            part_refs[0][c] = value.astype(BF16)

            @pl.when(rep_ref[0] == c)
            def _():
                own_ref[...] = value
        elif c == 0:
            own_ref[...] = value
        else:
            part_refs[c - 1][...] = value.astype(BF16)


def finish_gate(pre, gout_ref, hid_ref, gpre_ref):
    gate = jax.nn.sigmoid(pre)
    hid_ref[...] = (pre * gate).astype(BF16)
    gpre_ref[...] = (gout_ref[...].astype(F32) * (gate + pre * gate * (1.0 - gate))).astype(BF16)


def gate_body(rep_ref, recv_ref, own_ref, gout_ref, hid_ref, gpre_ref):
    pre = own_ref[...]
    for c in range(recv_ref.shape[0]):
        pre = pre + jnp.where(rep_ref[0] == c, 0.0, recv_ref[c].astype(F32))
    finish_gate(pre, gout_ref, hid_ref, gpre_ref)


def gate_blocks_body(own_ref, gout_ref, *refs):
    blocks, (hid_ref, gpre_ref) = refs[:-2], refs[-2:]
    pre = own_ref[...]
    for block in blocks:
        pre = pre + block[...].astype(F32)
    finish_gate(pre, gout_ref, hid_ref, gpre_ref)


def back_body(
    high_ref, low_ref, deg_ref, self_ref, neigh_ref, grad_ref, total_ref, mirror_ref
):
    rows, cols = total_ref.shape
    direct = jnp.zeros((rows, cols), F32)
    gagg = jnp.zeros((rows, cols), F32)
    for c in range(grad_ref.shape[0]):
        grad = grad_ref[c]
        at = slice(c * cols, (c + 1) * cols)
        gagg += dot(grad, neigh_ref[:, at], COLS)
        direct += dot(grad, self_ref[:, at], COLS)
    gagg = (gagg / wide_degree(deg_ref, cols)).astype(BF16)
    table = dot(high_ref[...], gagg, ROWS) + dot(low_ref[...], gagg, ROWS)
    total_ref[...] = direct + table[:rows]
    mirror_ref[...] = table[rows:].astype(BF16)


def weight_body(feat_ref, agg_ref, gfull_ref, out_ref):
    cols = feat_ref.shape[1]
    parts = out_ref.shape[0]
    piece = out_ref.shape[1] // 2
    for k, ref in enumerate((feat_ref, agg_ref)):
        left = ref[...]
        for c in range(gfull_ref.shape[0]):
            value = dot(left, gfull_ref[c], ROWS)
            out_ref[:, k * piece:(k + 1) * piece, c * cols:(c + 1) * cols] = value.reshape(
                parts, piece, cols
            ).astype(BF16)


def sum_body(scale, recv_ref, self_ref, neigh_ref):
    piece = self_ref.shape[0]
    for k, ref in enumerate((self_ref, neigh_ref)):
        total = jnp.zeros(ref.shape, F32)
        for d in range(recv_ref.shape[0]):
            total += recv_ref[d, k * piece:(k + 1) * piece].astype(F32)
        ref[...] = (total * scale).astype(BF16)


def group_weight_body(count, dom_ref, rep_ref, *refs):
    rows, grads, (mine_ref, send_ref, hold_ref, total_ref) = (
        refs[:2 * count], refs[2 * count:3 * count], refs[3 * count:]
    )
    for offset, ref in enumerate(grads):
        hold_ref[lax.bitwise_xor(rep_ref[0], offset)] = ref[...]
    lanes = mine_ref.shape[2]
    layer, side = dom_ref[0] // 2, dom_ref[0] % 2
    for k in range(2):
        total = jnp.zeros(total_ref.shape, F32)
        for offset in range(count):
            grad = hold_ref[lax.bitwise_xor(layer, offset)]
            total += dot(rows[k * count + offset][...], grad, ROWS)
        total_ref[...] = total
        mine_ref[k] = total_ref[:, block_rows(side, 0, lanes)]
        send_ref[k] = total_ref[:, block_rows(side, 1, lanes)].astype(BF16)


def join_body(scale, mine_ref, recv_ref, out_ref):
    out_ref[...] = ((mine_ref[...] + recv_ref[...].astype(F32)) * scale).astype(BF16)


def place_body(dom_ref, *refs):
    blocks, (self_ref, neigh_ref) = refs[:-2], refs[-2:]
    lanes = blocks[0].shape[2]
    for offset, block in enumerate(blocks):
        at = block_rows(dom_ref[0], offset, lanes)
        self_ref[:, at] = block[0]
        neigh_ref[:, at] = block[1]


def scatter_body(onehot_ref, total_ref, ret_ref, out_ref):
    out_ref[...] = (total_ref[...] + dot(onehot_ref[...], ret_ref[...])).astype(BF16)


def swap(array, axis, offset):
    return lax.ppermute(array, axis, [(i, i ^ offset) for i in range(lax.axis_size(axis))])


def swap_all(blocks, axis):
    return [blocks[0]] + [swap(blocks[k], axis, k) for k in range(1, len(blocks))]


def gather_layers(array, peers):
    return [array] + [swap(array, "dom", offset) for offset in range(2, peers, 2)]


def gather_pieces(array, peers):
    out = {offset: swap(array, "dom", offset) for offset in range(peers - 2, 0, -2)}
    out[0] = array
    for offset in range(0, peers, 2):
        out[offset + 1] = swap(out[offset], "dom", 1)
    return [out[offset] for offset in range(peers)]


def local(
    features, w_self, w_neigh, grad_out, mirror_list, mirror_count, tile_dst, tile_src, tiles
):
    rows, cols = features.shape
    width = w_self.shape[1]
    peers, slots = mirror_list.shape
    mirrors = peers * slots
    table_rows = rows + mirrors
    reps = width // cols
    struct = jax.ShapeDtypeStruct
    block = struct((rows, cols), BF16)
    rep = lax.axis_index("rep").astype(jnp.int32).reshape(1)
    dom = lax.axis_index("dom").astype(jnp.int32).reshape(1)
    lanes = width // peers
    halves = peers // reps
    split = peers == 8 and reps == 4 and slots % 16 == 0 and lanes % 128 == 0
    mirror_out = struct((mirrors, cols), BF16)

    def exchange(array):
        return lax.all_to_all(
            array.reshape(peers, slots, cols), "dom", split_axis=0, concat_axis=0, tiled=True
        ).reshape(mirrors, cols)

    onehot, outgoing = call(
        pick_body, (struct((rows, mirrors), BF16), mirror_out),
        [("h", mirror_count), ("h", mirror_list), ("h", features)],
        scratch=[
            pltpu.SMEM(mirror_count.shape, jnp.int32), pltpu.VMEM(mirror_list.shape, jnp.int32),
            pltpu.VMEM((rows, cols), BF16), pltpu.SemaphoreType.DMA((3,)),
        ],
        flops=2 * mirrors * rows * cols, moved=600_000,
    )
    incoming = exchange(outgoing)
    tiles_late, feat_late, self_late, neigh_late, _ = lax.optimization_barrier(
        (tiles, features, w_self, w_neigh, outgoing)
    )
    high, low, degree, self_near, neigh_near = call(
        prep_body,
        (
            struct((rows, table_rows), BF16), struct((rows, table_rows), BF16),
            struct((rows, 128), F32), struct(w_self.shape, BF16), struct(w_neigh.shape, BF16),
        ),
        [
            ("s", tile_dst), ("s", tile_src), ("v", tiles_late), ("h", self_late),
            ("h", neigh_late),
        ],
        scratch=[pltpu.VMEM((rows, table_rows), F32), pltpu.SemaphoreType.DMA((2,))],
        flops=1_000_000, moved=3_000_000,
    )
    own, agg, *parts = call(
        functools.partial(aggregate_body, split),
        (struct((rows, cols), F32), block)
        + ((block,) * (reps - 1) if split else (struct((reps, rows, cols), BF16),)),
        [
            ("s", rep), ("v", feat_late), ("v", incoming), ("v", high), ("v", low),
            ("v", degree), ("v", self_near), ("v", neigh_near),
        ],
        scratch=[pltpu.VMEM((table_rows, cols), BF16)],
        flops=600_000_000, moved=3_000_000,
    )
    scale = float(rows * peers) ** (-0.5)
    if split:
        kept = gather_layers(feat_late, peers)
        blocks = swap_all([own] + list(parts), "rep")
        hidden, grad_pre = call(
            gate_blocks_body, (block, block),
            [("v", own), ("v", grad_out)] + [("v", got) for got in blocks[1:]],
            flops=2_000_000, moved=1_300_000,
        )
        perm = [
            (p * reps + r, (halves * r + p % halves) * reps + p // halves)
            for p in range(peers) for r in range(reps)
        ]
        layer_grad = lax.ppermute(grad_pre, ("dom", "rep"), perm)
        agg_late, _ = lax.optimization_barrier((agg, grad_pre))
        kept_agg = gather_layers(agg_late, peers)
    else:
        recv = lax.all_to_all(parts[0], "rep", split_axis=0, concat_axis=0, tiled=True)
        hidden, grad_pre = call(
            gate_body, (block, block),
            [("s", rep), ("v", recv), ("v", own), ("v", grad_out)],
            flops=2_000_000, moved=1_300_000,
        )
    grad_full = lax.all_gather(grad_pre, "rep", axis=0, tiled=False)
    total, mirror_grad = call(
        back_body, (struct((rows, cols), F32), mirror_out),
        [
            ("v", high), ("v", low), ("v", degree), ("v", self_near), ("v", neigh_near),
            ("v", grad_full),
        ],
        flops=600_000_000, moved=3_000_000,
    )
    if split:
        layer_grad, grad_full = lax.optimization_barrier((layer_grad, grad_full))
        layer_grads = swap_all([layer_grad] * reps, "rep")
        half, send = call(
            functools.partial(group_weight_body, reps),
            (struct((2, rows, lanes), F32), struct((2, rows, lanes), BF16)),
            [("s", dom), ("s", rep)] + [("v", part) for part in kept + kept_agg + layer_grads],
            scratch=[pltpu.VMEM((reps, rows, cols), BF16), pltpu.VMEM((rows, cols), F32)],
            flops=600_000_000, moved=3_000_000,
        )
        mirror_grad, _ = lax.optimization_barrier((mirror_grad, send))
        mine = call(
            functools.partial(join_body, scale), struct((2, rows, lanes), BF16),
            [("v", half), ("v", swap(send, "dom", 1))], flops=200_000, moved=500_000,
        )
        pieces = gather_pieces(mine, peers)
    returned = exchange(mirror_grad)
    grad_features = call(
        scatter_body, block, [("v", onehot), ("v", total), ("v", returned)],
        flops=2 * mirrors * rows * cols, moved=700_000,
    )
    if split:
        out_self, out_neigh = call(
            place_body, (struct((rows, width), BF16), struct((rows, width), BF16)),
            [("s", dom)] + [("v", part) for part in pieces], moved=2_000_000,
        )
    else:
        piece = cols // peers
        partial = call(
            weight_body, struct((peers, 2 * piece, width), BF16),
            [("v", features), ("v", agg), ("v", grad_full)],
            flops=600_000_000, moved=2_000_000,
        )
        gathered = lax.all_to_all(partial, "dom", split_axis=0, concat_axis=0, tiled=True)
        mine_self, mine_neigh = call(
            functools.partial(sum_body, scale),
            (struct((piece, width), BF16), struct((piece, width), BF16)),
            [("v", gathered)], flops=1_000_000, moved=1_200_000,
        )
        out_self = lax.all_gather(mine_self, "dom", axis=0, tiled=True)
        out_neigh = lax.all_gather(mine_neigh, "dom", axis=0, tiled=True)
    return hidden, grad_features, out_self, out_neigh


def solution(mesh):
    in_specs = (
        P("dom", "rep"),
        P("rep", None),
        P("rep", None),
        P("dom", "rep"),
        P("dom", None),
        P("dom"),
        P("dom"),
        P("dom"),
        P("dom", None, None),
    )
    out_specs = (P("dom", "rep"), P("dom", "rep"), P("rep", None), P("rep", None))
    return jax.shard_map(local, mesh=mesh, in_specs=in_specs, out_specs=out_specs, check_vma=False)
```

```python
import functools

import jax
import jax.numpy as jnp
from jax import lax
from jax.experimental import pallas as pl
from jax.experimental.pallas import tpu as pltpu
from jax.sharding import PartitionSpec as P

F32 = jnp.float32
BF16 = jnp.bfloat16
SPECS = {
    "v": pl.BlockSpec(memory_space=pltpu.VMEM),
    "s": pl.BlockSpec(memory_space=pltpu.SMEM),
    "h": pl.BlockSpec(memory_space=pltpu.HBM),
}
ROWS = (((0,), (0,)), ((), ()))
COLS = (((1,), (1,)), ((), ()))


def call(body, outs, ins, scratch=(), flops=0, moved=0, vmem=16):
    return pl.pallas_call(
        body,
        out_shape=outs,
        in_specs=[SPECS[spec] for spec, _ in ins],
        out_specs=jax.tree.map(lambda _: SPECS["v"], outs),
        scratch_shapes=list(scratch),
        compiler_params=pltpu.CompilerParams(vmem_limit_bytes=vmem * 1024 * 1024),
        cost_estimate=pl.CostEstimate(flops=flops, bytes_accessed=moved, transcendentals=0),
    )(*[array for _, array in ins])


def dot(left, right, dims=(((1,), (0,)), ((), ()))):
    return lax.dot_general(left, right, dims, preferred_element_type=F32)


def block_rows(place, offset, size):
    return pl.ds(pl.multiple_of(lax.bitwise_xor(place, offset) * size, size), size)


def row_onehot(count_ref, lists, rows):
    peers, slots = lists.shape
    peer = lax.broadcasted_iota(jnp.int32, (peers, slots), 0)
    slot = lax.broadcasted_iota(jnp.int32, (peers, slots), 1)

    def fill(at, used):
        return jnp.where(peer == at, count_ref[at], used)

    used = jnp.zeros((peers, slots), jnp.int32)
    if peers <= 16:
        for at in range(peers):
            used = fill(at, used)
    else:
        used = lax.fori_loop(0, peers, fill, used)
    index = jnp.where(slot < used, lists, -1).astype(F32).astype(BF16)
    flat = peers * slots
    spread = (
        lax.broadcasted_iota(jnp.int32, (slots, flat), 0)
        == lax.broadcasted_iota(jnp.int32, (slots, flat), 1) % slots
    )
    wide = dot(index, spread.astype(F32).astype(BF16))
    mine = (
        lax.broadcasted_iota(jnp.int32, (peers, flat), 0)
        == lax.broadcasted_iota(jnp.int32, (peers, flat), 1) // slots
    )
    line = jnp.sum(jnp.where(mine, wide, 0.0), axis=0, keepdims=True).astype(jnp.int32)
    hit = lax.broadcasted_iota(jnp.int32, (rows, flat), 0) == line
    return hit.astype(F32).astype(BF16)


def pick_body(
    count_hbm, list_hbm, feat_hbm, onehot_ref, out_ref, count_ref, list_ref, feat_ref, sems
):
    copies = [
        pltpu.make_async_copy(src, dst, sems.at[k])
        for k, (src, dst) in enumerate(
            ((count_hbm, count_ref), (list_hbm, list_ref), (feat_hbm, feat_ref))
        )
    ]
    for copy in copies:
        copy.start()
    for copy in copies:
        copy.wait()
    onehot = row_onehot(count_ref, list_ref[...], feat_ref.shape[0])
    onehot_ref[...] = onehot
    out_ref[...] = dot(onehot, feat_ref[...], ROWS).astype(BF16)


def prep_body(
    dst_ref, src_ref, tiles_ref, self_hbm, neigh_hbm,
    high_ref, low_ref, deg_ref, self_ref, neigh_ref, adj_ref, sems,
):
    copies = [
        pltpu.make_async_copy(src, dst, sems.at[k])
        for k, (src, dst) in enumerate(((self_hbm, self_ref), (neigh_hbm, neigh_ref)))
    ]
    for copy in copies:
        copy.start()
    slots, side, _ = tiles_ref.shape
    adj_ref[...] = jnp.zeros(adj_ref.shape, F32)
    for t in range(slots):
        dst = pl.ds(pl.multiple_of(dst_ref[t] * side, side), side)
        src = pl.ds(pl.multiple_of(src_ref[t] * side, side), side)
        adj_ref[dst, src] += tiles_ref[t].astype(F32)
    adj = adj_ref[...]
    high = adj.astype(BF16)
    high_ref[...] = high
    low_ref[...] = (adj - high.astype(F32)).astype(BF16)
    degree = jnp.maximum(jnp.sum(adj, axis=1, keepdims=True), 1.0)
    deg_ref[...] = jnp.broadcast_to(degree, deg_ref.shape)
    for copy in copies:
        copy.wait()


def column_block(split, rep, c, reps, cols):
    other = lax.bitwise_xor(rep, c) if split else c
    return pl.ds(pl.multiple_of(other * cols, cols), cols)


def wide_degree(deg_ref, cols):
    return jnp.concatenate([deg_ref[...]] * (cols // deg_ref.shape[1]), axis=1)


def aggregate_body(
    split, rep_ref, feat_ref, inc_ref, high_ref, low_ref, deg_ref, self_ref, neigh_ref,
    own_ref, agg_ref, *refs,
):
    part_refs, table_ref = refs[:-1], refs[-1]
    rows, cols = feat_ref.shape
    feat = feat_ref[...]
    table_ref[:rows] = feat
    table_ref[rows:] = inc_ref[...]
    table = table_ref[...]
    summed = dot(high_ref[...], table) + dot(low_ref[...], table)
    agg = (summed / wide_degree(deg_ref, cols)).astype(BF16)
    agg_ref[...] = agg
    reps = self_ref.shape[1] // cols
    for c in reversed(range(reps)):
        at = column_block(split, rep_ref[0], c, reps, cols)
        value = dot(feat, self_ref[:, at]) + dot(agg, neigh_ref[:, at])
        if not split:
            part_refs[0][c] = value.astype(BF16)

            @pl.when(rep_ref[0] == c)
            def _():
                own_ref[...] = value
        elif c == 0:
            own_ref[...] = value
        else:
            part_refs[c - 1][...] = value.astype(BF16)


def finish_gate(pre, gout_ref, hid_ref, gpre_ref):
    gate = jax.nn.sigmoid(pre)
    hid_ref[...] = (pre * gate).astype(BF16)
    gpre_ref[...] = (gout_ref[...].astype(F32) * (gate + pre * gate * (1.0 - gate))).astype(BF16)


def gate_body(rep_ref, recv_ref, own_ref, gout_ref, hid_ref, gpre_ref):
    pre = own_ref[...]
    for c in range(recv_ref.shape[0]):
        pre = pre + jnp.where(rep_ref[0] == c, 0.0, recv_ref[c].astype(F32))
    finish_gate(pre, gout_ref, hid_ref, gpre_ref)


def gate_blocks_body(own_ref, gout_ref, *refs):
    blocks, (hid_ref, gpre_ref) = refs[:-2], refs[-2:]
    pre = own_ref[...]
    for block in blocks:
        pre = pre + block[...].astype(F32)
    finish_gate(pre, gout_ref, hid_ref, gpre_ref)


def back_body(
    high_ref, low_ref, deg_ref, self_ref, neigh_ref, grad_ref, total_ref, mirror_ref
):
    rows, cols = total_ref.shape
    direct = jnp.zeros((rows, cols), F32)
    gagg = jnp.zeros((rows, cols), F32)
    for c in range(grad_ref.shape[0]):
        grad = grad_ref[c]
        at = slice(c * cols, (c + 1) * cols)
        gagg += dot(grad, neigh_ref[:, at], COLS)
        direct += dot(grad, self_ref[:, at], COLS)
    gagg = (gagg / wide_degree(deg_ref, cols)).astype(BF16)
    table = dot(high_ref[...], gagg, ROWS) + dot(low_ref[...], gagg, ROWS)
    total_ref[...] = direct + table[:rows]
    mirror_ref[...] = table[rows:].astype(BF16)


def weight_body(feat_ref, agg_ref, gfull_ref, out_ref):
    cols = feat_ref.shape[1]
    parts = out_ref.shape[0]
    piece = out_ref.shape[1] // 2
    for k, ref in enumerate((feat_ref, agg_ref)):
        left = ref[...]
        for c in range(gfull_ref.shape[0]):
            value = dot(left, gfull_ref[c], ROWS)
            out_ref[:, k * piece:(k + 1) * piece, c * cols:(c + 1) * cols] = value.reshape(
                parts, piece, cols
            ).astype(BF16)


def sum_body(scale, recv_ref, self_ref, neigh_ref):
    piece = self_ref.shape[0]
    for k, ref in enumerate((self_ref, neigh_ref)):
        total = jnp.zeros(ref.shape, F32)
        for d in range(recv_ref.shape[0]):
            total += recv_ref[d, k * piece:(k + 1) * piece].astype(F32)
        ref[...] = (total * scale).astype(BF16)


def group_weight_body(count, dom_ref, rep_ref, *refs):
    rows, grads, (mine_ref, send_ref, hold_ref, total_ref) = (
        refs[:2 * count], refs[2 * count:3 * count], refs[3 * count:]
    )
    for offset, ref in enumerate(grads):
        hold_ref[lax.bitwise_xor(rep_ref[0], offset)] = ref[...]
    lanes = mine_ref.shape[2]
    layer, side = dom_ref[0] // 2, dom_ref[0] % 2
    for k in range(2):
        total = jnp.zeros(total_ref.shape, F32)
        for offset in range(count):
            grad = hold_ref[lax.bitwise_xor(layer, offset)]
            total += dot(rows[k * count + offset][...], grad, ROWS)
        total_ref[...] = total
        mine_ref[k] = total_ref[:, block_rows(side, 0, lanes)]
        send_ref[k] = total_ref[:, block_rows(side, 1, lanes)].astype(BF16)


def join_body(scale, mine_ref, recv_ref, out_ref):
    out_ref[...] = ((mine_ref[...] + recv_ref[...].astype(F32)) * scale).astype(BF16)


def place_body(dom_ref, *refs):
    blocks, (self_ref, neigh_ref) = refs[:-2], refs[-2:]
    lanes = blocks[0].shape[2]
    for offset, block in enumerate(blocks):
        at = block_rows(dom_ref[0], offset, lanes)
        self_ref[:, at] = block[0]
        neigh_ref[:, at] = block[1]


def scatter_body(onehot_ref, total_ref, ret_ref, out_ref):
    out_ref[...] = (total_ref[...] + dot(onehot_ref[...], ret_ref[...])).astype(BF16)


def swap(array, axis, offset):
    return lax.ppermute(array, axis, [(i, i ^ offset) for i in range(lax.axis_size(axis))])


def swap_all(blocks, axis):
    return [blocks[0]] + [swap(blocks[k], axis, k) for k in range(1, len(blocks))]


def gather_layers(array, peers):
    return [array] + [swap(array, "dom", offset) for offset in range(2, peers, 2)]


def gather_pieces(array, peers):
    out = {offset: swap(array, "dom", offset) for offset in range(peers - 2, 0, -2)}
    out[0] = array
    for offset in range(0, peers, 2):
        out[offset + 1] = swap(out[offset], "dom", 1)
    return [out[offset] for offset in range(peers)]


def local(
    features, w_self, w_neigh, grad_out, mirror_list, mirror_count, tile_dst, tile_src, tiles
):
    rows, cols = features.shape
    width = w_self.shape[1]
    peers, slots = mirror_list.shape
    mirrors = peers * slots
    table_rows = rows + mirrors
    reps = width // cols
    struct = jax.ShapeDtypeStruct
    block = struct((rows, cols), BF16)
    rep = lax.axis_index("rep").astype(jnp.int32).reshape(1)
    dom = lax.axis_index("dom").astype(jnp.int32).reshape(1)
    lanes = width // peers
    halves = peers // reps
    split = peers == 8 and reps == 4 and slots % 16 == 0 and lanes % 128 == 0
    mirror_out = struct((mirrors, cols), BF16)

    def exchange(array):
        return lax.all_to_all(
            array.reshape(peers, slots, cols), "dom", split_axis=0, concat_axis=0, tiled=True
        ).reshape(mirrors, cols)

    onehot, outgoing = call(
        pick_body, (struct((rows, mirrors), BF16), mirror_out),
        [("h", mirror_count), ("h", mirror_list), ("h", features)],
        scratch=[
            pltpu.SMEM(mirror_count.shape, jnp.int32), pltpu.VMEM(mirror_list.shape, jnp.int32),
            pltpu.VMEM((rows, cols), BF16), pltpu.SemaphoreType.DMA((3,)),
        ],
        vmem=58,
        flops=2 * mirrors * rows * cols, moved=600_000,
    )
    incoming = exchange(outgoing)
    tiles_late, feat_late, self_late, neigh_late, _ = lax.optimization_barrier(
        (tiles, features, w_self, w_neigh, outgoing)
    )
    high, low, degree, self_near, neigh_near = call(
        prep_body,
        (
            struct((rows, table_rows), BF16), struct((rows, table_rows), BF16),
            struct((rows, 128), F32), struct(w_self.shape, BF16), struct(w_neigh.shape, BF16),
        ),
        [
            ("s", tile_dst), ("s", tile_src), ("v", tiles_late), ("h", self_late),
            ("h", neigh_late),
        ],
        scratch=[pltpu.VMEM((rows, table_rows), F32), pltpu.SemaphoreType.DMA((2,))],
        flops=1_000_000, moved=3_000_000,
    )
    if split:
        kept = gather_layers(features, peers)
        incoming, kept[1] = lax.optimization_barrier((incoming, kept[1]))
    own, agg, *parts = call(
        functools.partial(aggregate_body, split),
        (struct((rows, cols), F32), block)
        + ((block,) * (reps - 1) if split else (struct((reps, rows, cols), BF16),)),
        [
            ("s", rep), ("v", feat_late), ("v", incoming), ("v", high), ("v", low),
            ("v", degree), ("v", self_near), ("v", neigh_near),
        ],
        scratch=[pltpu.VMEM((table_rows, cols), BF16)],
        flops=600_000_000, moved=3_000_000,
    )
    scale = float(rows * peers) ** (-0.5)
    if split:
        kept_agg = gather_layers(agg, peers)
        grad_out, *kept[2:] = lax.optimization_barrier((grad_out, *kept[2:]))
        blocks = swap_all([own] + list(parts), "rep")
        hidden, grad_pre = call(
            gate_blocks_body, (block, block),
            [("v", own), ("v", grad_out)] + [("v", got) for got in blocks[1:]],
            flops=2_000_000, moved=1_300_000,
        )
        perm = [
            (p * reps + r, (halves * r + p % halves) * reps + p // halves)
            for p in range(peers) for r in range(reps)
        ]
        layer_grad = lax.ppermute(grad_pre, ("dom", "rep"), perm)
        grad_pre, layer_grad = lax.optimization_barrier((grad_pre, layer_grad))
    else:
        recv = lax.all_to_all(parts[0], "rep", split_axis=0, concat_axis=0, tiled=True)
        hidden, grad_pre = call(
            gate_body, (block, block),
            [("s", rep), ("v", recv), ("v", own), ("v", grad_out)],
            flops=2_000_000, moved=1_300_000,
        )
    grad_full = lax.all_gather(grad_pre, "rep", axis=0, tiled=False)
    total, mirror_grad = call(
        back_body, (struct((rows, cols), F32), mirror_out),
        [
            ("v", high), ("v", low), ("v", degree), ("v", self_near), ("v", neigh_near),
            ("v", grad_full),
        ],
        flops=600_000_000, moved=3_000_000,
    )
    if split:
        layer_grads = swap_all([layer_grad] * reps, "rep")
        half, send = call(
            functools.partial(group_weight_body, reps),
            (struct((2, rows, lanes), F32), struct((2, rows, lanes), BF16)),
            [("s", dom), ("s", rep)] + [("v", part) for part in kept + kept_agg + layer_grads],
            scratch=[pltpu.VMEM((reps, rows, cols), BF16), pltpu.VMEM((rows, cols), F32)],
            flops=600_000_000, moved=3_000_000,
        )
        mine = call(
            functools.partial(join_body, scale), struct((2, rows, lanes), BF16),
            [("v", half), ("v", swap(send, "dom", 1))], flops=200_000, moved=500_000,
        )
        pieces = gather_pieces(mine, peers)
        mirror_grad, pieces[2] = lax.optimization_barrier((mirror_grad, pieces[2]))
    returned = exchange(mirror_grad)
    grad_features = call(
        scatter_body, block, [("v", onehot), ("v", total), ("v", returned)],
        flops=2 * mirrors * rows * cols, moved=700_000,
    )
    if split:
        out_self, out_neigh = call(
            place_body, (struct((rows, width), BF16), struct((rows, width), BF16)),
            [("s", dom)] + [("v", part) for part in pieces], moved=2_000_000,
        )
    else:
        piece = cols // peers
        partial = call(
            weight_body, struct((peers, 2 * piece, width), BF16),
            [("v", features), ("v", agg), ("v", grad_full)],
            flops=600_000_000, moved=2_000_000,
        )
        gathered = lax.all_to_all(partial, "dom", split_axis=0, concat_axis=0, tiled=True)
        mine_self, mine_neigh = call(
            functools.partial(sum_body, scale),
            (struct((piece, width), BF16), struct((piece, width), BF16)),
            [("v", gathered)], flops=1_000_000, moved=1_200_000,
        )
        out_self = lax.all_gather(mine_self, "dom", axis=0, tiled=True)
        out_neigh = lax.all_gather(mine_neigh, "dom", axis=0, tiled=True)
    return hidden, grad_features, out_self, out_neigh


def solution(mesh):
    in_specs = (
        P("dom", "rep"),
        P("rep", None),
        P("rep", None),
        P("dom", "rep"),
        P("dom", None),
        P("dom"),
        P("dom"),
        P("dom"),
        P("dom", None, None),
    )
    out_specs = (P("dom", "rep"), P("dom", "rep"), P("rep", None), P("rep", None))
    return jax.shard_map(local, mesh=mesh, in_specs=in_specs, out_specs=out_specs, check_vma=False)
```

```python
import functools

import jax
import jax.numpy as jnp
from jax import lax
from jax.experimental import pallas as pl
from jax.experimental.pallas import tpu as pltpu
from jax.sharding import PartitionSpec as P

F32 = jnp.float32
BF16 = jnp.bfloat16
SPECS = {
    "v": pl.BlockSpec(memory_space=pltpu.VMEM),
    "s": pl.BlockSpec(memory_space=pltpu.SMEM),
    "h": pl.BlockSpec(memory_space=pltpu.HBM),
}
ROWS = (((0,), (0,)), ((), ()))
COLS = (((1,), (1,)), ((), ()))


def call(body, outs, ins, scratch=(), flops=0, moved=0, vmem=16):
    return pl.pallas_call(
        body,
        out_shape=outs,
        in_specs=[SPECS[spec] for spec, _ in ins],
        out_specs=jax.tree.map(lambda _: SPECS["v"], outs),
        scratch_shapes=list(scratch),
        compiler_params=pltpu.CompilerParams(vmem_limit_bytes=vmem * 1024 * 1024),
        cost_estimate=pl.CostEstimate(flops=flops, bytes_accessed=moved, transcendentals=0),
    )(*[array for _, array in ins])


def dot(left, right, dims=(((1,), (0,)), ((), ()))):
    return lax.dot_general(left, right, dims, preferred_element_type=F32)


def block_rows(place, offset, size):
    return pl.ds(pl.multiple_of(lax.bitwise_xor(place, offset) * size, size), size)


def row_onehot(count_ref, lists, rows):
    peers, slots = lists.shape
    peer = lax.broadcasted_iota(jnp.int32, (peers, slots), 0)
    slot = lax.broadcasted_iota(jnp.int32, (peers, slots), 1)

    def fill(at, used):
        return jnp.where(peer == at, count_ref[at], used)

    used = jnp.zeros((peers, slots), jnp.int32)
    if peers <= 16:
        for at in range(peers):
            used = fill(at, used)
    else:
        used = lax.fori_loop(0, peers, fill, used)
    index = jnp.where(slot < used, lists, -1).astype(F32).astype(BF16)
    flat = peers * slots
    spread = (
        lax.broadcasted_iota(jnp.int32, (slots, flat), 0)
        == lax.broadcasted_iota(jnp.int32, (slots, flat), 1) % slots
    )
    wide = dot(index, spread.astype(F32).astype(BF16))
    mine = (
        lax.broadcasted_iota(jnp.int32, (peers, flat), 0)
        == lax.broadcasted_iota(jnp.int32, (peers, flat), 1) // slots
    )
    line = jnp.sum(jnp.where(mine, wide, 0.0), axis=0, keepdims=True).astype(jnp.int32)
    hit = lax.broadcasted_iota(jnp.int32, (rows, flat), 0) == line
    return hit.astype(F32).astype(BF16)


def pick_body(
    count_hbm, list_hbm, feat_hbm, onehot_ref, out_ref, count_ref, list_ref, feat_ref, sems
):
    copies = [
        pltpu.make_async_copy(src, dst, sems.at[k])
        for k, (src, dst) in enumerate(
            ((count_hbm, count_ref), (list_hbm, list_ref), (feat_hbm, feat_ref))
        )
    ]
    for copy in copies:
        copy.start()
    for copy in copies:
        copy.wait()
    onehot = row_onehot(count_ref, list_ref[...], feat_ref.shape[0])
    onehot_ref[...] = onehot
    out_ref[...] = dot(onehot, feat_ref[...], ROWS).astype(BF16)


def prep_body(
    dst_ref, src_ref, tiles_ref, self_hbm, neigh_hbm,
    high_ref, low_ref, deg_ref, self_ref, neigh_ref, adj_ref, sems,
):
    copies = [
        pltpu.make_async_copy(src, dst, sems.at[k])
        for k, (src, dst) in enumerate(((self_hbm, self_ref), (neigh_hbm, neigh_ref)))
    ]
    for copy in copies:
        copy.start()
    slots, side, _ = tiles_ref.shape
    adj_ref[...] = jnp.zeros(adj_ref.shape, F32)
    for t in range(slots):
        dst = pl.ds(pl.multiple_of(dst_ref[t] * side, side), side)
        src = pl.ds(pl.multiple_of(src_ref[t] * side, side), side)
        adj_ref[dst, src] += tiles_ref[t].astype(F32)
    adj = adj_ref[...]
    high = adj.astype(BF16)
    high_ref[...] = high
    low_ref[...] = (adj - high.astype(F32)).astype(BF16)
    degree = jnp.maximum(jnp.sum(adj, axis=1, keepdims=True), 1.0)
    deg_ref[...] = jnp.broadcast_to(degree, deg_ref.shape)
    for copy in copies:
        copy.wait()


def column_block(split, rep, c, reps, cols):
    other = lax.bitwise_xor(rep, c) if split else c
    return pl.ds(pl.multiple_of(other * cols, cols), cols)


def wide_degree(deg_ref, cols):
    return jnp.concatenate([deg_ref[...]] * (cols // deg_ref.shape[1]), axis=1)


def aggregate_body(
    split, rep_ref, feat_ref, inc_ref, high_ref, low_ref, deg_ref, self_ref, neigh_ref,
    own_ref, agg_ref, *refs,
):
    part_refs, table_ref = refs[:-1], refs[-1]
    rows, cols = feat_ref.shape
    feat = feat_ref[...]
    table_ref[:rows] = feat
    table_ref[rows:] = inc_ref[...]
    table = table_ref[...]
    summed = dot(high_ref[...], table) + dot(low_ref[...], table)
    agg = (summed / wide_degree(deg_ref, cols)).astype(BF16)
    agg_ref[...] = agg
    reps = self_ref.shape[1] // cols
    for c in reversed(range(reps)):
        at = column_block(split, rep_ref[0], c, reps, cols)
        value = dot(feat, self_ref[:, at]) + dot(agg, neigh_ref[:, at])
        if not split:
            part_refs[0][c] = value.astype(BF16)

            @pl.when(rep_ref[0] == c)
            def _():
                own_ref[...] = value
        elif c == 0:
            own_ref[...] = value
        else:
            part_refs[c - 1][...] = value.astype(BF16)


def finish_gate(pre, gout_ref, hid_ref, gpre_ref):
    gate = jax.nn.sigmoid(pre)
    hid_ref[...] = (pre * gate).astype(BF16)
    gpre_ref[...] = (gout_ref[...].astype(F32) * (gate + pre * gate * (1.0 - gate))).astype(BF16)


def gate_body(rep_ref, recv_ref, own_ref, gout_ref, hid_ref, gpre_ref):
    pre = own_ref[...]
    for c in range(recv_ref.shape[0]):
        pre = pre + jnp.where(rep_ref[0] == c, 0.0, recv_ref[c].astype(F32))
    finish_gate(pre, gout_ref, hid_ref, gpre_ref)


def gate_blocks_body(own_ref, gout_ref, *refs):
    blocks, (hid_ref, gpre_ref) = refs[:-2], refs[-2:]
    pre = own_ref[...]
    for block in blocks:
        pre = pre + block[...].astype(F32)
    finish_gate(pre, gout_ref, hid_ref, gpre_ref)


def back_body(
    high_ref, low_ref, deg_ref, self_ref, neigh_ref, grad_ref, total_ref, mirror_ref
):
    rows, cols = total_ref.shape
    direct = jnp.zeros((rows, cols), F32)
    gagg = jnp.zeros((rows, cols), F32)
    for c in range(grad_ref.shape[0]):
        grad = grad_ref[c]
        at = slice(c * cols, (c + 1) * cols)
        gagg += dot(grad, neigh_ref[:, at], COLS)
        direct += dot(grad, self_ref[:, at], COLS)
    gagg = (gagg / wide_degree(deg_ref, cols)).astype(BF16)
    table = dot(high_ref[...], gagg, ROWS) + dot(low_ref[...], gagg, ROWS)
    total_ref[...] = direct + table[:rows]
    mirror_ref[...] = table[rows:].astype(BF16)


def weight_body(feat_ref, agg_ref, gfull_ref, out_ref):
    cols = feat_ref.shape[1]
    parts = out_ref.shape[0]
    piece = out_ref.shape[1] // 2
    for k, ref in enumerate((feat_ref, agg_ref)):
        left = ref[...]
        for c in range(gfull_ref.shape[0]):
            value = dot(left, gfull_ref[c], ROWS)
            out_ref[:, k * piece:(k + 1) * piece, c * cols:(c + 1) * cols] = value.reshape(
                parts, piece, cols
            ).astype(BF16)


def sum_body(scale, recv_ref, self_ref, neigh_ref):
    piece = self_ref.shape[0]
    for k, ref in enumerate((self_ref, neigh_ref)):
        total = jnp.zeros(ref.shape, F32)
        for d in range(recv_ref.shape[0]):
            total += recv_ref[d, k * piece:(k + 1) * piece].astype(F32)
        ref[...] = (total * scale).astype(BF16)


def group_weight_body(count, dom_ref, rep_ref, *refs):
    rows, grads, (mine_ref, send_ref, hold_ref, total_ref) = (
        refs[:2 * count], refs[2 * count:3 * count], refs[3 * count:]
    )
    for offset, ref in enumerate(grads):
        hold_ref[lax.bitwise_xor(rep_ref[0], offset)] = ref[...]
    lanes = mine_ref.shape[2]
    layer, side = dom_ref[0] // 2, dom_ref[0] % 2
    for k in range(2):
        total = jnp.zeros(total_ref.shape, F32)
        for offset in range(count):
            grad = hold_ref[lax.bitwise_xor(layer, offset)]
            total += dot(rows[k * count + offset][...], grad, ROWS)
        total_ref[...] = total
        mine_ref[k] = total_ref[:, block_rows(side, 0, lanes)]
        send_ref[k] = total_ref[:, block_rows(side, 1, lanes)].astype(BF16)


def join_body(scale, mine_ref, recv_ref, out_ref):
    out_ref[...] = ((mine_ref[...] + recv_ref[...].astype(F32)) * scale).astype(BF16)


def place_body(dom_ref, *refs):
    blocks, (self_ref, neigh_ref) = refs[:-2], refs[-2:]
    lanes = blocks[0].shape[2]
    for offset, block in enumerate(blocks):
        at = block_rows(dom_ref[0], offset, lanes)
        self_ref[:, at] = block[0]
        neigh_ref[:, at] = block[1]


def scatter_body(onehot_ref, total_ref, ret_ref, out_ref):
    out_ref[...] = (total_ref[...] + dot(onehot_ref[...], ret_ref[...])).astype(BF16)


def swap(array, axis, offset):
    return lax.ppermute(array, axis, [(i, i ^ offset) for i in range(lax.axis_size(axis))])


def swap_all(blocks, axis):
    return [blocks[0]] + [swap(blocks[k], axis, k) for k in range(1, len(blocks))]


def gather_layers(array, peers):
    return [array] + [swap(array, "dom", offset) for offset in range(2, peers, 2)]


def gather_pieces(array, peers):
    out = {offset: swap(array, "dom", offset) for offset in range(peers - 2, 0, -2)}
    out[0] = array
    for offset in range(0, peers, 2):
        out[offset + 1] = swap(out[offset], "dom", 1)
    return [out[offset] for offset in range(peers)]


def local(
    features, w_self, w_neigh, grad_out, mirror_list, mirror_count, tile_dst, tile_src, tiles
):
    rows, cols = features.shape
    width = w_self.shape[1]
    peers, slots = mirror_list.shape
    mirrors = peers * slots
    table_rows = rows + mirrors
    reps = width // cols
    struct = jax.ShapeDtypeStruct
    block = struct((rows, cols), BF16)
    rep = lax.axis_index("rep").astype(jnp.int32).reshape(1)
    dom = lax.axis_index("dom").astype(jnp.int32).reshape(1)
    lanes = width // peers
    halves = peers // reps
    split = peers == 8 and reps == 4 and slots % 16 == 0 and lanes % 128 == 0
    mirror_out = struct((mirrors, cols), BF16)

    def exchange(array):
        return lax.all_to_all(
            array.reshape(peers, slots, cols), "dom", split_axis=0, concat_axis=0, tiled=True
        ).reshape(mirrors, cols)

    onehot, outgoing = call(
        pick_body, (struct((rows, mirrors), BF16), mirror_out),
        [("h", mirror_count), ("h", mirror_list), ("h", features)],
        scratch=[
            pltpu.SMEM(mirror_count.shape, jnp.int32), pltpu.VMEM(mirror_list.shape, jnp.int32),
            pltpu.VMEM((rows, cols), BF16), pltpu.SemaphoreType.DMA((3,)),
        ],
        vmem=58,
        flops=2 * mirrors * rows * cols, moved=600_000,
    )
    incoming = exchange(outgoing)
    tiles_late, feat_late, self_late, neigh_late, _ = lax.optimization_barrier(
        (tiles, features, w_self, w_neigh, outgoing)
    )
    high, low, degree, self_near, neigh_near = call(
        prep_body,
        (
            struct((rows, table_rows), BF16), struct((rows, table_rows), BF16),
            struct((rows, 128), F32), struct(w_self.shape, BF16), struct(w_neigh.shape, BF16),
        ),
        [
            ("s", tile_dst), ("s", tile_src), ("v", tiles_late), ("h", self_late),
            ("h", neigh_late),
        ],
        scratch=[pltpu.VMEM((rows, table_rows), F32), pltpu.SemaphoreType.DMA((2,))],
        flops=1_000_000, moved=3_000_000,
    )
    if split:
        kept = gather_layers(features, peers)
        incoming, kept[1] = lax.optimization_barrier((incoming, kept[1]))
    own, agg, *parts = call(
        functools.partial(aggregate_body, split),
        (struct((rows, cols), F32), block)
        + ((block,) * (reps - 1) if split else (struct((reps, rows, cols), BF16),)),
        [
            ("s", rep), ("v", feat_late), ("v", incoming), ("v", high), ("v", low),
            ("v", degree), ("v", self_near), ("v", neigh_near),
        ],
        scratch=[pltpu.VMEM((table_rows, cols), BF16)],
        flops=600_000_000, moved=3_000_000,
    )
    scale = float(rows * peers) ** (-0.5)
    if split:
        kept_agg = gather_layers(agg, peers)
        grad_out, kept_agg[1], *kept[2:] = lax.optimization_barrier(
            (grad_out, kept_agg[1], *kept[2:])
        )
        blocks = swap_all([own] + list(parts), "rep")
        hidden, grad_pre = call(
            gate_blocks_body, (block, block),
            [("v", own), ("v", grad_out)] + [("v", got) for got in blocks[1:]],
            flops=2_000_000, moved=1_300_000,
        )
        perm = [
            (p * reps + r, (halves * r + p % halves) * reps + p // halves)
            for p in range(peers) for r in range(reps)
        ]
        layer_grad = lax.ppermute(grad_pre, ("dom", "rep"), perm)
    else:
        recv = lax.all_to_all(parts[0], "rep", split_axis=0, concat_axis=0, tiled=True)
        hidden, grad_pre = call(
            gate_body, (block, block),
            [("s", rep), ("v", recv), ("v", own), ("v", grad_out)],
            flops=2_000_000, moved=1_300_000,
        )
    grad_full = lax.all_gather(grad_pre, "rep", axis=0, tiled=False)
    total, mirror_grad = call(
        back_body, (struct((rows, cols), F32), mirror_out),
        [
            ("v", high), ("v", low), ("v", degree), ("v", self_near), ("v", neigh_near),
            ("v", grad_full),
        ],
        flops=600_000_000, moved=3_000_000,
    )
    if split:
        layer_grad, _ = lax.optimization_barrier((layer_grad, grad_full))
        layer_grads = swap_all([layer_grad] * reps, "rep")
        half, send = call(
            functools.partial(group_weight_body, reps),
            (struct((2, rows, lanes), F32), struct((2, rows, lanes), BF16)),
            [("s", dom), ("s", rep)] + [("v", part) for part in kept + kept_agg + layer_grads],
            scratch=[pltpu.VMEM((reps, rows, cols), BF16), pltpu.VMEM((rows, cols), F32)],
            flops=600_000_000, moved=3_000_000,
        )
        mine = call(
            functools.partial(join_body, scale), struct((2, rows, lanes), BF16),
            [("v", half), ("v", swap(send, "dom", 1))], flops=200_000, moved=500_000,
        )
        pieces = gather_pieces(mine, peers)
    returned = exchange(mirror_grad)
    grad_features = call(
        scatter_body, block, [("v", onehot), ("v", total), ("v", returned)],
        flops=2 * mirrors * rows * cols, moved=700_000,
    )
    if split:
        out_self, out_neigh = call(
            place_body, (struct((rows, width), BF16), struct((rows, width), BF16)),
            [("s", dom)] + [("v", part) for part in pieces], moved=2_000_000,
        )
    else:
        piece = cols // peers
        partial = call(
            weight_body, struct((peers, 2 * piece, width), BF16),
            [("v", features), ("v", agg), ("v", grad_full)],
            flops=600_000_000, moved=2_000_000,
        )
        gathered = lax.all_to_all(partial, "dom", split_axis=0, concat_axis=0, tiled=True)
        mine_self, mine_neigh = call(
            functools.partial(sum_body, scale),
            (struct((piece, width), BF16), struct((piece, width), BF16)),
            [("v", gathered)], flops=1_000_000, moved=1_200_000,
        )
        out_self = lax.all_gather(mine_self, "dom", axis=0, tiled=True)
        out_neigh = lax.all_gather(mine_neigh, "dom", axis=0, tiled=True)
    return hidden, grad_features, out_self, out_neigh


def solution(mesh):
    in_specs = (
        P("dom", "rep"),
        P("rep", None),
        P("rep", None),
        P("dom", "rep"),
        P("dom", None),
        P("dom"),
        P("dom"),
        P("dom"),
        P("dom", None, None),
    )
    out_specs = (P("dom", "rep"), P("dom", "rep"), P("rep", None), P("rep", None))
    return jax.shard_map(local, mesh=mesh, in_specs=in_specs, out_specs=out_specs, check_vma=False)
```

```python
import functools

import jax
import jax.numpy as jnp
from jax import lax
from jax.experimental import pallas as pl
from jax.experimental.pallas import tpu as pltpu
from jax.sharding import PartitionSpec as P

F32 = jnp.float32
BF16 = jnp.bfloat16
SPECS = {
    "v": pl.BlockSpec(memory_space=pltpu.VMEM),
    "s": pl.BlockSpec(memory_space=pltpu.SMEM),
    "h": pl.BlockSpec(memory_space=pltpu.HBM),
}
ROWS = (((0,), (0,)), ((), ()))
COLS = (((1,), (1,)), ((), ()))


def call(body, outs, ins, scratch=(), flops=0, moved=0, vmem=16):
    return pl.pallas_call(
        body,
        out_shape=outs,
        in_specs=[SPECS[spec] for spec, _ in ins],
        out_specs=jax.tree.map(lambda _: SPECS["v"], outs),
        scratch_shapes=list(scratch),
        compiler_params=pltpu.CompilerParams(vmem_limit_bytes=vmem * 1024 * 1024),
        cost_estimate=pl.CostEstimate(flops=flops, bytes_accessed=moved, transcendentals=0),
    )(*[array for _, array in ins])


def dot(left, right, dims=(((1,), (0,)), ((), ()))):
    return lax.dot_general(left, right, dims, preferred_element_type=F32)


def block_rows(place, offset, size):
    return pl.ds(pl.multiple_of(lax.bitwise_xor(place, offset) * size, size), size)


def row_onehot(count_ref, lists, rows):
    peers, slots = lists.shape
    peer = lax.broadcasted_iota(jnp.int32, (peers, slots), 0)
    slot = lax.broadcasted_iota(jnp.int32, (peers, slots), 1)

    def fill(at, used):
        return jnp.where(peer == at, count_ref[at], used)

    used = jnp.zeros((peers, slots), jnp.int32)
    if peers <= 16:
        for at in range(peers):
            used = fill(at, used)
    else:
        used = lax.fori_loop(0, peers, fill, used)
    index = jnp.where(slot < used, lists, -1).astype(F32).astype(BF16)
    flat = peers * slots
    spread = (
        lax.broadcasted_iota(jnp.int32, (slots, flat), 0)
        == lax.broadcasted_iota(jnp.int32, (slots, flat), 1) % slots
    )
    wide = dot(index, spread.astype(F32).astype(BF16))
    mine = (
        lax.broadcasted_iota(jnp.int32, (peers, flat), 0)
        == lax.broadcasted_iota(jnp.int32, (peers, flat), 1) // slots
    )
    line = jnp.sum(jnp.where(mine, wide, 0.0), axis=0, keepdims=True).astype(jnp.int32)
    hit = lax.broadcasted_iota(jnp.int32, (rows, flat), 0) == line
    return hit.astype(F32).astype(BF16)


def pick_body(
    count_hbm, list_hbm, feat_hbm, onehot_ref, out_ref, count_ref, list_ref, feat_ref, sems
):
    copies = [
        pltpu.make_async_copy(src, dst, sems.at[k])
        for k, (src, dst) in enumerate(
            ((count_hbm, count_ref), (list_hbm, list_ref), (feat_hbm, feat_ref))
        )
    ]
    for copy in copies:
        copy.start()
    for copy in copies:
        copy.wait()
    onehot = row_onehot(count_ref, list_ref[...], feat_ref.shape[0])
    onehot_ref[...] = onehot
    out_ref[...] = dot(onehot, feat_ref[...], ROWS).astype(BF16)


def prep_body(
    dst_ref, src_ref, tiles_ref, self_hbm, neigh_hbm,
    high_ref, low_ref, deg_ref, self_ref, neigh_ref, adj_ref, sems,
):
    copies = [
        pltpu.make_async_copy(src, dst, sems.at[k])
        for k, (src, dst) in enumerate(((self_hbm, self_ref), (neigh_hbm, neigh_ref)))
    ]
    for copy in copies:
        copy.start()
    slots, side, _ = tiles_ref.shape
    adj_ref[...] = jnp.zeros(adj_ref.shape, F32)
    for t in range(slots):
        dst = pl.ds(pl.multiple_of(dst_ref[t] * side, side), side)
        src = pl.ds(pl.multiple_of(src_ref[t] * side, side), side)
        adj_ref[dst, src] += tiles_ref[t].astype(F32)
    adj = adj_ref[...]
    high = adj.astype(BF16)
    high_ref[...] = high
    low_ref[...] = (adj - high.astype(F32)).astype(BF16)
    degree = jnp.maximum(jnp.sum(adj, axis=1, keepdims=True), 1.0)
    deg_ref[...] = jnp.broadcast_to(degree, deg_ref.shape)
    for copy in copies:
        copy.wait()


def column_block(split, rep, c, reps, cols):
    other = lax.bitwise_xor(rep, c) if split else c
    return pl.ds(pl.multiple_of(other * cols, cols), cols)


def wide_degree(deg_ref, cols):
    return jnp.concatenate([deg_ref[...]] * (cols // deg_ref.shape[1]), axis=1)


def aggregate_body(
    split, rep_ref, feat_ref, inc_ref, high_ref, low_ref, deg_ref, self_ref, neigh_ref,
    own_ref, agg_ref, *refs,
):
    part_refs, table_ref = refs[:-1], refs[-1]
    rows, cols = feat_ref.shape
    feat = feat_ref[...]
    table_ref[:rows] = feat
    table_ref[rows:] = inc_ref[...]
    table = table_ref[...]
    summed = dot(high_ref[...], table) + dot(low_ref[...], table)
    agg = (summed / wide_degree(deg_ref, cols)).astype(BF16)
    agg_ref[...] = agg
    reps = self_ref.shape[1] // cols
    for c in reversed(range(reps)):
        at = column_block(split, rep_ref[0], c, reps, cols)
        value = dot(feat, self_ref[:, at]) + dot(agg, neigh_ref[:, at])
        if not split:
            part_refs[0][c] = value.astype(BF16)

            @pl.when(rep_ref[0] == c)
            def _():
                own_ref[...] = value
        elif c == 0:
            own_ref[...] = value
        else:
            part_refs[c - 1][...] = value.astype(BF16)


def finish_gate(pre, gout_ref, hid_ref, gpre_ref):
    gate = jax.nn.sigmoid(pre)
    hid_ref[...] = (pre * gate).astype(BF16)
    gpre_ref[...] = (gout_ref[...].astype(F32) * (gate + pre * gate * (1.0 - gate))).astype(BF16)


def gate_body(rep_ref, recv_ref, own_ref, gout_ref, hid_ref, gpre_ref):
    pre = own_ref[...]
    for c in range(recv_ref.shape[0]):
        pre = pre + jnp.where(rep_ref[0] == c, 0.0, recv_ref[c].astype(F32))
    finish_gate(pre, gout_ref, hid_ref, gpre_ref)


def gate_blocks_body(own_ref, gout_ref, *refs):
    blocks, (hid_ref, gpre_ref) = refs[:-2], refs[-2:]
    pre = own_ref[...]
    for block in blocks:
        pre = pre + block[...].astype(F32)
    finish_gate(pre, gout_ref, hid_ref, gpre_ref)


def back_body(
    high_ref, low_ref, deg_ref, self_ref, neigh_ref, grad_ref, total_ref, mirror_ref
):
    rows, cols = total_ref.shape
    direct = jnp.zeros((rows, cols), F32)
    gagg = jnp.zeros((rows, cols), F32)
    for c in range(grad_ref.shape[0]):
        grad = grad_ref[c]
        at = slice(c * cols, (c + 1) * cols)
        gagg += dot(grad, neigh_ref[:, at], COLS)
        direct += dot(grad, self_ref[:, at], COLS)
    gagg = (gagg / wide_degree(deg_ref, cols)).astype(BF16)
    table = dot(high_ref[...], gagg, ROWS) + dot(low_ref[...], gagg, ROWS)
    total_ref[...] = direct + table[:rows]
    mirror_ref[...] = table[rows:].astype(BF16)


def weight_body(feat_ref, agg_ref, gfull_ref, out_ref):
    cols = feat_ref.shape[1]
    parts = out_ref.shape[0]
    piece = out_ref.shape[1] // 2
    for k, ref in enumerate((feat_ref, agg_ref)):
        left = ref[...]
        for c in range(gfull_ref.shape[0]):
            value = dot(left, gfull_ref[c], ROWS)
            out_ref[:, k * piece:(k + 1) * piece, c * cols:(c + 1) * cols] = value.reshape(
                parts, piece, cols
            ).astype(BF16)


def sum_body(scale, recv_ref, self_ref, neigh_ref):
    piece = self_ref.shape[0]
    for k, ref in enumerate((self_ref, neigh_ref)):
        total = jnp.zeros(ref.shape, F32)
        for d in range(recv_ref.shape[0]):
            total += recv_ref[d, k * piece:(k + 1) * piece].astype(F32)
        ref[...] = (total * scale).astype(BF16)


def group_weight_body(dom_ref, own_ref, other_ref, *refs):
    rows, mine_ref, send_refs, total_ref = refs[:4], refs[4], refs[5:-1], refs[-1]
    lanes = mine_ref.shape[2]
    layer, side = dom_ref[0] // 2, dom_ref[0] % 2
    count = other_ref.shape[0]
    for k in range(2):
        own, other = rows[2 * k][...], rows[2 * k + 1][...]
        for c in range(count):
            cols = own.shape[1]
            total_ref[:, c * cols:(c + 1) * cols] = dot(
                own, own_ref[side * count + c], ROWS
            ) + dot(other, other_ref[c], ROWS)
        mine_ref[k] = total_ref[:, block_rows(layer, 0, lanes)]
        for offset, ref in enumerate(send_refs):
            ref[k] = total_ref[:, block_rows(layer, offset + 1, lanes)].astype(BF16)


def join_body(scale, mine_ref, *refs):
    total = mine_ref[...]
    for ref in refs[:-1]:
        total = total + ref[...].astype(F32)
    refs[-1][...] = (total * scale).astype(BF16)


def place_body(dom_ref, *refs):
    blocks, (self_ref, neigh_ref) = refs[:-2], refs[-2:]
    lanes = blocks[0].shape[2]
    for offset, block in enumerate(blocks):
        place = lax.bitwise_xor(dom_ref[0], offset)
        at = (place % 2) * (len(blocks) // 2) + place // 2
        at = pl.ds(pl.multiple_of(at * lanes, lanes), lanes)
        self_ref[:, at] = block[0]
        neigh_ref[:, at] = block[1]


def scatter_body(onehot_ref, total_ref, ret_ref, out_ref):
    out_ref[...] = (total_ref[...] + dot(onehot_ref[...], ret_ref[...])).astype(BF16)


def swap(array, axis, offset):
    return lax.ppermute(array, axis, [(i, i ^ offset) for i in range(lax.axis_size(axis))])


def swap_all(blocks, axis):
    return [blocks[0]] + [swap(blocks[k], axis, k) for k in range(1, len(blocks))]


def gather_pieces(array, peers):
    out = {offset: swap(array, "dom", offset) for offset in range(peers - 2, 0, -2)}
    out[0] = array
    for offset in range(0, peers, 2):
        out[offset + 1] = swap(out[offset], "dom", 1)
    return [out[offset] for offset in range(peers)]


def local(
    features, w_self, w_neigh, grad_out, mirror_list, mirror_count, tile_dst, tile_src, tiles
):
    rows, cols = features.shape
    width = w_self.shape[1]
    peers, slots = mirror_list.shape
    mirrors = peers * slots
    table_rows = rows + mirrors
    reps = width // cols
    struct = jax.ShapeDtypeStruct
    block = struct((rows, cols), BF16)
    rep = lax.axis_index("rep").astype(jnp.int32).reshape(1)
    dom = lax.axis_index("dom").astype(jnp.int32).reshape(1)
    lanes = width // peers
    halves = peers // reps
    split = peers == 8 and reps == 4 and slots % 16 == 0 and lanes % 128 == 0
    mirror_out = struct((mirrors, cols), BF16)

    def exchange(array):
        return lax.all_to_all(
            array.reshape(peers, slots, cols), "dom", split_axis=0, concat_axis=0, tiled=True
        ).reshape(mirrors, cols)

    onehot, outgoing = call(
        pick_body, (struct((rows, mirrors), BF16), mirror_out),
        [("h", mirror_count), ("h", mirror_list), ("h", features)],
        scratch=[
            pltpu.SMEM(mirror_count.shape, jnp.int32), pltpu.VMEM(mirror_list.shape, jnp.int32),
            pltpu.VMEM((rows, cols), BF16), pltpu.SemaphoreType.DMA((3,)),
        ],
        vmem=58,
        flops=2 * mirrors * rows * cols, moved=600_000,
    )
    incoming = exchange(outgoing)
    tiles_late, feat_late, self_late, neigh_late, _ = lax.optimization_barrier(
        (tiles, features, w_self, w_neigh, outgoing)
    )
    high, low, degree, self_near, neigh_near = call(
        prep_body,
        (
            struct((rows, table_rows), BF16), struct((rows, table_rows), BF16),
            struct((rows, 128), F32), struct(w_self.shape, BF16), struct(w_neigh.shape, BF16),
        ),
        [
            ("s", tile_dst), ("s", tile_src), ("v", tiles_late), ("h", self_late),
            ("h", neigh_late),
        ],
        scratch=[pltpu.VMEM((rows, table_rows), F32), pltpu.SemaphoreType.DMA((2,))],
        flops=1_000_000, moved=3_000_000,
    )
    if split:
        feat_beside = swap(features, "dom", 1)
        incoming, feat_beside = lax.optimization_barrier((incoming, feat_beside))
    own, agg, *parts = call(
        functools.partial(aggregate_body, split),
        (struct((rows, cols), F32), block)
        + ((block,) * (reps - 1) if split else (struct((reps, rows, cols), BF16),)),
        [
            ("s", rep), ("v", feat_late), ("v", incoming), ("v", high), ("v", low),
            ("v", degree), ("v", self_near), ("v", neigh_near),
        ],
        scratch=[pltpu.VMEM((table_rows, cols), BF16)],
        flops=600_000_000, moved=3_000_000,
    )
    scale = float(rows * peers) ** (-0.5)
    if split:
        agg_beside = swap(agg, "dom", 1)
        blocks = swap_all([own] + list(parts), "rep")
        hidden, grad_pre = call(
            gate_blocks_body, (block, block),
            [("v", own), ("v", grad_out)] + [("v", got) for got in blocks[1:]],
            flops=2_000_000, moved=1_300_000,
        )
    else:
        recv = lax.all_to_all(parts[0], "rep", split_axis=0, concat_axis=0, tiled=True)
        hidden, grad_pre = call(
            gate_body, (block, block),
            [("s", rep), ("v", recv), ("v", own), ("v", grad_out)],
            flops=2_000_000, moved=1_300_000,
        )
    grad_full = lax.all_gather(grad_pre, "rep", axis=0, tiled=False)
    total, mirror_grad = call(
        back_body, (struct((rows, cols), F32), mirror_out),
        [
            ("v", high), ("v", low), ("v", degree), ("v", self_near), ("v", neigh_near),
            ("v", grad_full),
        ],
        flops=600_000_000, moved=3_000_000,
    )
    if split:
        start = (1 - dom[0] % 2) * (reps // 2)
        half = lax.dynamic_slice_in_dim(grad_full, start, reps // 2, 0)
        piece = struct((2, rows, lanes), BF16)
        mine, *sends = call(
            group_weight_body, (struct((2, rows, lanes), F32),) + (piece,) * (reps - 1),
            [
                ("s", dom), ("v", grad_full), ("v", swap(half, "dom", 1)), ("v", features),
                ("v", feat_beside), ("v", agg), ("v", agg_beside),
            ],
            scratch=[pltpu.VMEM((rows, width // 2), F32)],
            flops=600_000_000, moved=3_000_000,
        )
        layers = [swap(send, "dom", 2 * k + 2) for k, send in enumerate(sends)]
        mine = call(
            functools.partial(join_body, scale), piece,
            [("v", mine)] + [("v", got) for got in layers], flops=200_000, moved=500_000,
        )
        pieces = gather_pieces(mine, peers)
    returned = exchange(mirror_grad)
    grad_features = call(
        scatter_body, block, [("v", onehot), ("v", total), ("v", returned)],
        flops=2 * mirrors * rows * cols, moved=700_000,
    )
    if split:
        out_self, out_neigh = call(
            place_body, (struct((rows, width), BF16), struct((rows, width), BF16)),
            [("s", dom)] + [("v", part) for part in pieces], moved=2_000_000,
        )
    else:
        piece = cols // peers
        partial = call(
            weight_body, struct((peers, 2 * piece, width), BF16),
            [("v", features), ("v", agg), ("v", grad_full)],
            flops=600_000_000, moved=2_000_000,
        )
        gathered = lax.all_to_all(partial, "dom", split_axis=0, concat_axis=0, tiled=True)
        mine_self, mine_neigh = call(
            functools.partial(sum_body, scale),
            (struct((piece, width), BF16), struct((piece, width), BF16)),
            [("v", gathered)], flops=1_000_000, moved=1_200_000,
        )
        out_self = lax.all_gather(mine_self, "dom", axis=0, tiled=True)
        out_neigh = lax.all_gather(mine_neigh, "dom", axis=0, tiled=True)
    return hidden, grad_features, out_self, out_neigh


def solution(mesh):
    in_specs = (
        P("dom", "rep"),
        P("rep", None),
        P("rep", None),
        P("dom", "rep"),
        P("dom", None),
        P("dom"),
        P("dom"),
        P("dom"),
        P("dom", None, None),
    )
    out_specs = (P("dom", "rep"), P("dom", "rep"), P("rep", None), P("rep", None))
    return jax.shard_map(local, mesh=mesh, in_specs=in_specs, out_specs=out_specs, check_vma=False)
```

```python
import functools

import jax
import jax.numpy as jnp
from jax import lax
from jax.experimental import pallas as pl
from jax.experimental.pallas import tpu as pltpu
from jax.sharding import PartitionSpec as P

F32 = jnp.float32
BF16 = jnp.bfloat16
SPECS = {
    "v": pl.BlockSpec(memory_space=pltpu.VMEM),
    "s": pl.BlockSpec(memory_space=pltpu.SMEM),
    "h": pl.BlockSpec(memory_space=pltpu.HBM),
}
ROWS = (((0,), (0,)), ((), ()))
COLS = (((1,), (1,)), ((), ()))


def call(body, outs, ins, scratch=(), flops=0, moved=0, vmem=16, out="v"):
    return pl.pallas_call(
        body,
        out_shape=outs,
        in_specs=[SPECS[spec] for spec, _ in ins],
        out_specs=jax.tree.map(lambda _: SPECS[out], outs),
        scratch_shapes=list(scratch),
        compiler_params=pltpu.CompilerParams(vmem_limit_bytes=vmem * 1024 * 1024),
        cost_estimate=pl.CostEstimate(flops=flops, bytes_accessed=moved, transcendentals=0),
    )(*[array for _, array in ins])


def dot(left, right, dims=(((1,), (0,)), ((), ()))):
    return lax.dot_general(left, right, dims, preferred_element_type=F32)


def block_rows(place, offset, size):
    return pl.ds(pl.multiple_of(lax.bitwise_xor(place, offset) * size, size), size)


def row_onehot(count_ref, lists, rows):
    peers, slots = lists.shape
    peer = lax.broadcasted_iota(jnp.int32, (peers, slots), 0)
    slot = lax.broadcasted_iota(jnp.int32, (peers, slots), 1)

    def fill(at, used):
        return jnp.where(peer == at, count_ref[at], used)

    used = jnp.zeros((peers, slots), jnp.int32)
    if peers <= 16:
        for at in range(peers):
            used = fill(at, used)
    else:
        used = lax.fori_loop(0, peers, fill, used)
    index = jnp.where(slot < used, lists, -1).astype(F32).astype(BF16)
    flat = peers * slots
    spread = (
        lax.broadcasted_iota(jnp.int32, (slots, flat), 0)
        == lax.broadcasted_iota(jnp.int32, (slots, flat), 1) % slots
    )
    wide = dot(index, spread.astype(F32).astype(BF16))
    mine = (
        lax.broadcasted_iota(jnp.int32, (peers, flat), 0)
        == lax.broadcasted_iota(jnp.int32, (peers, flat), 1) // slots
    )
    line = jnp.sum(jnp.where(mine, wide, 0.0), axis=0, keepdims=True).astype(jnp.int32)
    hit = lax.broadcasted_iota(jnp.int32, (rows, flat), 0) == line
    return hit.astype(F32).astype(BF16)


def pick_body(
    count_hbm, list_hbm, feat_hbm, onehot_ref, out_ref, count_ref, list_ref, feat_ref, sems
):
    copies = [
        pltpu.make_async_copy(src, dst, sems.at[k])
        for k, (src, dst) in enumerate(
            ((count_hbm, count_ref), (list_hbm, list_ref), (feat_hbm, feat_ref))
        )
    ]
    for copy in copies:
        copy.start()
    for copy in copies:
        copy.wait()
    onehot = row_onehot(count_ref, list_ref[...], feat_ref.shape[0])
    onehot_ref[...] = onehot
    out_ref[...] = dot(onehot, feat_ref[...], ROWS).astype(BF16)


def prep_body(
    dst_ref, src_ref, tiles_ref, self_hbm, neigh_hbm,
    high_ref, low_ref, deg_ref, self_ref, neigh_ref, adj_ref, sems,
):
    copies = [
        pltpu.make_async_copy(src, dst, sems.at[k])
        for k, (src, dst) in enumerate(((self_hbm, self_ref), (neigh_hbm, neigh_ref)))
    ]
    for copy in copies:
        copy.start()
    slots, side, _ = tiles_ref.shape
    adj_ref[...] = jnp.zeros(adj_ref.shape, F32)
    for t in range(slots):
        dst = pl.ds(pl.multiple_of(dst_ref[t] * side, side), side)
        src = pl.ds(pl.multiple_of(src_ref[t] * side, side), side)
        adj_ref[dst, src] += tiles_ref[t].astype(F32)
    adj = adj_ref[...]
    high = adj.astype(BF16)
    high_ref[...] = high
    low_ref[...] = (adj - high.astype(F32)).astype(BF16)
    degree = jnp.maximum(jnp.sum(adj, axis=1, keepdims=True), 1.0)
    deg_ref[...] = jnp.broadcast_to(degree, deg_ref.shape)
    for copy in copies:
        copy.wait()


def column_block(split, rep, c, reps, cols):
    other = lax.bitwise_xor(rep, c) if split else c
    return pl.ds(pl.multiple_of(other * cols, cols), cols)


def wide_degree(deg_ref, cols):
    return jnp.concatenate([deg_ref[...]] * (cols // deg_ref.shape[1]), axis=1)


def aggregate_body(
    split, rep_ref, feat_ref, inc_ref, high_ref, low_ref, deg_ref, self_ref, neigh_ref,
    own_ref, agg_ref, *refs,
):
    part_refs, table_ref = refs[:-1], refs[-1]
    rows, cols = feat_ref.shape
    feat = feat_ref[...]
    table_ref[:rows] = feat
    table_ref[rows:] = inc_ref[...]
    table = table_ref[...]
    summed = dot(high_ref[...], table) + dot(low_ref[...], table)
    agg = (summed / wide_degree(deg_ref, cols)).astype(BF16)
    agg_ref[...] = agg
    reps = self_ref.shape[1] // cols
    for c in reversed(range(reps)):
        at = column_block(split, rep_ref[0], c, reps, cols)
        value = dot(feat, self_ref[:, at]) + dot(agg, neigh_ref[:, at])
        if not split:
            part_refs[0][c] = value.astype(BF16)

            @pl.when(rep_ref[0] == c)
            def _():
                own_ref[...] = value
        elif c == 0:
            own_ref[...] = value
        elif c == 2:
            part_refs[0][...] = value
        else:
            part_refs[1][c // 2] = value.astype(BF16)


def finish_gate(pre, gout_ref, hid_ref, gpre_ref):
    gate = jax.nn.sigmoid(pre)
    hid_ref[...] = (pre * gate).astype(BF16)
    gpre_ref[...] = (gout_ref[...].astype(F32) * (gate + pre * gate * (1.0 - gate))).astype(BF16)


def gate_body(rep_ref, recv_ref, own_ref, gout_ref, hid_ref, gpre_ref):
    pre = own_ref[...]
    for c in range(recv_ref.shape[0]):
        pre = pre + jnp.where(rep_ref[0] == c, 0.0, recv_ref[c].astype(F32))
    finish_gate(pre, gout_ref, hid_ref, gpre_ref)


def across_body(mine_ref, beside_ref, out_ref):
    out_ref[...] = (mine_ref[...] + beside_ref[1].astype(F32)).astype(BF16)


def gate_blocks_body(own_ref, gout_ref, beside_ref, across_ref, hid_ref, gpre_ref):
    pre = own_ref[...] + beside_ref[0].astype(F32) + across_ref[...].astype(F32)
    finish_gate(pre, gout_ref, hid_ref, gpre_ref)


def back_body(
    high_ref, low_ref, deg_ref, self_ref, neigh_ref, grad_ref, total_ref, mirror_ref
):
    rows, cols = total_ref.shape
    direct = jnp.zeros((rows, cols), F32)
    gagg = jnp.zeros((rows, cols), F32)
    for c in range(grad_ref.shape[0]):
        grad = grad_ref[c]
        at = slice(c * cols, (c + 1) * cols)
        gagg += dot(grad, neigh_ref[:, at], COLS)
        direct += dot(grad, self_ref[:, at], COLS)
    gagg = (gagg / wide_degree(deg_ref, cols)).astype(BF16)
    table = dot(high_ref[...], gagg, ROWS) + dot(low_ref[...], gagg, ROWS)
    total_ref[...] = direct + table[:rows]
    mirror_ref[...] = table[rows:].astype(BF16)


def weight_body(feat_ref, agg_ref, gfull_ref, out_ref):
    cols = feat_ref.shape[1]
    parts = out_ref.shape[0]
    piece = out_ref.shape[1] // 2
    for k, ref in enumerate((feat_ref, agg_ref)):
        left = ref[...]
        for c in range(gfull_ref.shape[0]):
            value = dot(left, gfull_ref[c], ROWS)
            out_ref[:, k * piece:(k + 1) * piece, c * cols:(c + 1) * cols] = value.reshape(
                parts, piece, cols
            ).astype(BF16)


def sum_body(scale, recv_ref, self_ref, neigh_ref):
    piece = self_ref.shape[0]
    for k, ref in enumerate((self_ref, neigh_ref)):
        total = jnp.zeros(ref.shape, F32)
        for d in range(recv_ref.shape[0]):
            total += recv_ref[d, k * piece:(k + 1) * piece].astype(F32)
        ref[...] = (total * scale).astype(BF16)


def group_weight_body(dom_ref, own_ref, other_ref, *refs):
    rows, mine_ref, send_refs, total_ref = refs[:4], refs[4], refs[5:-1], refs[-1]
    lanes = mine_ref.shape[2]
    layer, side = dom_ref[0] // 2, dom_ref[0] % 2
    count = other_ref.shape[0]
    for k in range(2):
        own, other = rows[2 * k][...], rows[2 * k + 1][...]
        for c in range(count):
            cols = own.shape[1]
            total_ref[:, c * cols:(c + 1) * cols] = dot(
                own, own_ref[side * count + c], ROWS
            ) + dot(other, other_ref[c], ROWS)
        mine_ref[k] = total_ref[:, block_rows(layer, 0, lanes)]
        for offset, ref in enumerate(send_refs):
            ref[k] = total_ref[:, block_rows(layer, offset + 1, lanes)].astype(BF16)


def join_body(scale, mine_ref, *refs):
    total = mine_ref[...]
    for ref in refs[:-1]:
        total = total + ref[...].astype(F32)
    refs[-1][...] = (total * scale).astype(BF16)


def place_body(dom_ref, *refs):
    blocks, outs, sems = refs[:-3], refs[-3:-1], refs[-1]
    copies = []
    lanes = blocks[0].shape[2]
    for offset, block in enumerate(blocks):
        place = lax.bitwise_xor(dom_ref[0], offset)
        at = (place % 2) * (len(blocks) // 2) + place // 2
        at = pl.ds(pl.multiple_of(at * lanes, lanes), lanes)
        for k, out_ref in enumerate(outs):
            copies.append(
                pltpu.make_async_copy(block.at[k], out_ref.at[:, at], sems.at[2 * offset + k])
            )
            copies[-1].start()
    for copy in copies:
        copy.wait()


def scatter_body(onehot_ref, total_ref, ret_ref, out_ref):
    out_ref[...] = (total_ref[...] + dot(onehot_ref[...], ret_ref[...])).astype(BF16)


def swap(array, axis, offset):
    return lax.ppermute(array, axis, [(i, i ^ offset) for i in range(lax.axis_size(axis))])


def gather_pieces(array, peers):
    out = {0: array, 4: swap(array, "dom", 4), 2: swap(array, "dom", 2)}
    out[6] = swap(out[4], "dom", 2)
    for offset in range(0, peers, 2):
        out[offset + 1] = swap(out[offset], "dom", 1)
    return [out[offset] for offset in range(peers)]


def local(
    features, w_self, w_neigh, grad_out, mirror_list, mirror_count, tile_dst, tile_src, tiles
):
    rows, cols = features.shape
    width = w_self.shape[1]
    peers, slots = mirror_list.shape
    mirrors = peers * slots
    table_rows = rows + mirrors
    reps = width // cols
    struct = jax.ShapeDtypeStruct
    block = struct((rows, cols), BF16)
    rep = lax.axis_index("rep").astype(jnp.int32).reshape(1)
    dom = lax.axis_index("dom").astype(jnp.int32).reshape(1)
    lanes = width // peers
    halves = peers // reps
    split = peers == 8 and reps == 4 and slots % 16 == 0 and lanes % 128 == 0
    mirror_out = struct((mirrors, cols), BF16)

    def exchange(array):
        return lax.all_to_all(
            array.reshape(peers, slots, cols), "dom", split_axis=0, concat_axis=0, tiled=True
        ).reshape(mirrors, cols)

    onehot, outgoing = call(
        pick_body, (struct((rows, mirrors), BF16), mirror_out),
        [("h", mirror_count), ("h", mirror_list), ("h", features)],
        scratch=[
            pltpu.SMEM(mirror_count.shape, jnp.int32), pltpu.VMEM(mirror_list.shape, jnp.int32),
            pltpu.VMEM((rows, cols), BF16), pltpu.SemaphoreType.DMA((3,)),
        ],
        vmem=58,
        flops=2 * mirrors * rows * cols, moved=600_000,
    )
    incoming = exchange(outgoing)
    tiles_late, feat_late, self_late, neigh_late, _ = lax.optimization_barrier(
        (tiles, features, w_self, w_neigh, outgoing)
    )
    high, low, degree, self_near, neigh_near = call(
        prep_body,
        (
            struct((rows, table_rows), BF16), struct((rows, table_rows), BF16),
            struct((rows, 128), F32), struct(w_self.shape, BF16), struct(w_neigh.shape, BF16),
        ),
        [
            ("s", tile_dst), ("s", tile_src), ("v", tiles_late), ("h", self_late),
            ("h", neigh_late),
        ],
        scratch=[pltpu.VMEM((rows, table_rows), F32), pltpu.SemaphoreType.DMA((2,))],
        flops=1_000_000, moved=3_000_000,
    )
    if split:
        feat_beside = swap(features, "dom", 1)
        incoming, feat_beside = lax.optimization_barrier((incoming, feat_beside))
    own, agg, *parts = call(
        functools.partial(aggregate_body, split),
        (struct((rows, cols), F32), block)
        + (
            (struct((rows, cols), F32), struct((2, rows, cols), BF16)) if split
            else (struct((reps, rows, cols), BF16),)
        ),
        [
            ("s", rep), ("v", feat_late), ("v", incoming), ("v", high), ("v", low),
            ("v", degree), ("v", self_near), ("v", neigh_near),
        ],
        scratch=[pltpu.VMEM((table_rows, cols), BF16)],
        flops=600_000_000, moved=3_000_000,
    )
    scale = float(rows * peers) ** (-0.5)
    if split:
        agg_beside = swap(agg, "dom", 1)
        grad_out, agg_beside = lax.optimization_barrier((grad_out, agg_beside))
        beside = swap(parts[1], "rep", 1)
        across = call(
            across_body, block, [("v", parts[0]), ("v", beside)], flops=100_000, moved=500_000
        )
        across = swap(across, "rep", 2)
        hidden, grad_pre = call(
            gate_blocks_body, (block, block),
            [("v", own), ("v", grad_out), ("v", beside), ("v", across)],
            flops=2_000_000, moved=1_300_000,
        )
    else:
        recv = lax.all_to_all(parts[0], "rep", split_axis=0, concat_axis=0, tiled=True)
        hidden, grad_pre = call(
            gate_body, (block, block),
            [("s", rep), ("v", recv), ("v", own), ("v", grad_out)],
            flops=2_000_000, moved=1_300_000,
        )
    grad_full = lax.all_gather(grad_pre, "rep", axis=0, tiled=False)
    total, mirror_grad = call(
        back_body, (struct((rows, cols), F32), mirror_out),
        [
            ("v", high), ("v", low), ("v", degree), ("v", self_near), ("v", neigh_near),
            ("v", grad_full),
        ],
        flops=600_000_000, moved=3_000_000,
    )
    if split:
        start = (1 - dom[0] % 2) * (reps // 2)
        half = lax.dynamic_slice_in_dim(grad_full, start, reps // 2, 0)
        piece = struct((2, rows, lanes), BF16)
        mine, *sends = call(
            group_weight_body, (struct((2, rows, lanes), F32),) + (piece,) * (reps - 1),
            [
                ("s", dom), ("v", grad_full), ("v", swap(half, "dom", 1)), ("v", features),
                ("v", feat_beside), ("v", agg), ("v", agg_beside),
            ],
            scratch=[pltpu.VMEM((rows, width // 2), F32)],
            flops=600_000_000, moved=3_000_000,
        )
        layers = [swap(send, "dom", 2 * k + 2) for k, send in enumerate(sends)]
        mine = call(
            functools.partial(join_body, scale), piece,
            [("v", mine)] + [("v", got) for got in layers], flops=200_000, moved=500_000,
        )
        pieces = gather_pieces(mine, peers)
    returned = exchange(mirror_grad)
    grad_features = call(
        scatter_body, block, [("v", onehot), ("v", total), ("v", returned)],
        flops=2 * mirrors * rows * cols, moved=700_000,
    )
    if split:
        out_self, out_neigh = call(
            place_body, (struct((rows, width), BF16), struct((rows, width), BF16)),
            [("s", dom)] + [("v", part) for part in pieces],
            scratch=[pltpu.SemaphoreType.DMA((2 * peers,))], moved=2_000_000, out="h",
        )
    else:
        piece = cols // peers
        partial = call(
            weight_body, struct((peers, 2 * piece, width), BF16),
            [("v", features), ("v", agg), ("v", grad_full)],
            flops=600_000_000, moved=2_000_000,
        )
        gathered = lax.all_to_all(partial, "dom", split_axis=0, concat_axis=0, tiled=True)
        mine_self, mine_neigh = call(
            functools.partial(sum_body, scale),
            (struct((piece, width), BF16), struct((piece, width), BF16)),
            [("v", gathered)], flops=1_000_000, moved=1_200_000,
        )
        out_self = lax.all_gather(mine_self, "dom", axis=0, tiled=True)
        out_neigh = lax.all_gather(mine_neigh, "dom", axis=0, tiled=True)
    return hidden, grad_features, out_self, out_neigh


def solution(mesh):
    in_specs = (
        P("dom", "rep"),
        P("rep", None),
        P("rep", None),
        P("dom", "rep"),
        P("dom", None),
        P("dom"),
        P("dom"),
        P("dom"),
        P("dom", None, None),
    )
    out_specs = (P("dom", "rep"), P("dom", "rep"), P("rep", None), P("rep", None))
    return jax.shard_map(local, mesh=mesh, in_specs=in_specs, out_specs=out_specs, check_vma=False)
```

```python
import functools

import jax
import jax.numpy as jnp
from jax import lax
from jax.experimental import pallas as pl
from jax.experimental.pallas import tpu as pltpu
from jax.sharding import PartitionSpec as P

F32 = jnp.float32
BF16 = jnp.bfloat16
SPECS = {
    "v": pl.BlockSpec(memory_space=pltpu.VMEM),
    "s": pl.BlockSpec(memory_space=pltpu.SMEM),
    "h": pl.BlockSpec(memory_space=pltpu.HBM),
}
ROWS = (((0,), (0,)), ((), ()))
COLS = (((1,), (1,)), ((), ()))


def call(body, outs, ins, scratch=(), flops=0, moved=0, vmem=16, out="v"):
    return pl.pallas_call(
        body,
        out_shape=outs,
        in_specs=[SPECS[spec] for spec, _ in ins],
        out_specs=jax.tree.map(lambda _: SPECS[out], outs),
        scratch_shapes=list(scratch),
        compiler_params=pltpu.CompilerParams(vmem_limit_bytes=vmem * 1024 * 1024),
        cost_estimate=pl.CostEstimate(flops=flops, bytes_accessed=moved, transcendentals=0),
    )(*[array for _, array in ins])


def dot(left, right, dims=(((1,), (0,)), ((), ()))):
    return lax.dot_general(left, right, dims, preferred_element_type=F32)


def block_rows(place, offset, size):
    return pl.ds(pl.multiple_of(lax.bitwise_xor(place, offset) * size, size), size)


def row_onehot(count_ref, lists, rows):
    peers, slots = lists.shape
    peer = lax.broadcasted_iota(jnp.int32, (peers, slots), 0)
    slot = lax.broadcasted_iota(jnp.int32, (peers, slots), 1)

    def fill(at, used):
        return jnp.where(peer == at, count_ref[at], used)

    used = jnp.zeros((peers, slots), jnp.int32)
    if peers <= 16:
        for at in range(peers):
            used = fill(at, used)
    else:
        used = lax.fori_loop(0, peers, fill, used)
    index = jnp.where(slot < used, lists, -1).astype(F32).astype(BF16)
    flat = peers * slots
    spread = (
        lax.broadcasted_iota(jnp.int32, (slots, flat), 0)
        == lax.broadcasted_iota(jnp.int32, (slots, flat), 1) % slots
    )
    wide = dot(index, spread.astype(F32).astype(BF16))
    mine = (
        lax.broadcasted_iota(jnp.int32, (peers, flat), 0)
        == lax.broadcasted_iota(jnp.int32, (peers, flat), 1) // slots
    )
    line = jnp.sum(jnp.where(mine, wide, 0.0), axis=0, keepdims=True).astype(jnp.int32)
    hit = lax.broadcasted_iota(jnp.int32, (rows, flat), 0) == line
    return hit.astype(F32).astype(BF16)


def pick_body(
    count_hbm, list_hbm, feat_hbm, onehot_ref, out_ref, count_ref, list_ref, feat_ref, sems
):
    copies = [
        pltpu.make_async_copy(src, dst, sems.at[k])
        for k, (src, dst) in enumerate(
            ((count_hbm, count_ref), (list_hbm, list_ref), (feat_hbm, feat_ref))
        )
    ]
    for copy in copies:
        copy.start()
    for copy in copies:
        copy.wait()
    onehot = row_onehot(count_ref, list_ref[...], feat_ref.shape[0])
    onehot_ref[...] = onehot
    out_ref[...] = dot(onehot, feat_ref[...], ROWS).astype(BF16)


def prep_body(
    dst_ref, src_ref, tiles_ref, self_hbm, neigh_hbm,
    high_ref, low_ref, deg_ref, self_ref, neigh_ref, adj_ref, sems,
):
    copies = [
        pltpu.make_async_copy(src, dst, sems.at[k])
        for k, (src, dst) in enumerate(((self_hbm, self_ref), (neigh_hbm, neigh_ref)))
    ]
    for copy in copies:
        copy.start()
    slots, side, _ = tiles_ref.shape
    adj_ref[...] = jnp.zeros(adj_ref.shape, F32)
    for t in range(slots):
        dst = pl.ds(pl.multiple_of(dst_ref[t] * side, side), side)
        src = pl.ds(pl.multiple_of(src_ref[t] * side, side), side)
        adj_ref[dst, src] += tiles_ref[t].astype(F32)
    adj = adj_ref[...]
    high = adj.astype(BF16)
    high_ref[...] = high
    low_ref[...] = (adj - high.astype(F32)).astype(BF16)
    degree = jnp.maximum(jnp.sum(adj, axis=1, keepdims=True), 1.0)
    deg_ref[...] = jnp.broadcast_to(degree, deg_ref.shape)
    for copy in copies:
        copy.wait()


def column_block(split, rep, c, reps, cols):
    other = lax.bitwise_xor(rep, c) if split else c
    return pl.ds(pl.multiple_of(other * cols, cols), cols)


def wide_degree(deg_ref, cols):
    return jnp.concatenate([deg_ref[...]] * (cols // deg_ref.shape[1]), axis=1)


def aggregate_body(
    split, rep_ref, feat_ref, inc_ref, high_ref, low_ref, deg_ref, self_ref, neigh_ref,
    own_ref, agg_ref, *refs,
):
    part_refs, table_ref = refs[:-1], refs[-1]
    rows, cols = feat_ref.shape
    feat = feat_ref[...]
    table_ref[:rows] = feat
    table_ref[rows:] = inc_ref[...]
    table = table_ref[...]
    summed = dot(high_ref[...], table) + dot(low_ref[...], table)
    agg = (summed / wide_degree(deg_ref, cols)).astype(BF16)
    if split:
        agg_ref[0] = feat
        agg_ref[1] = agg
    else:
        agg_ref[...] = agg
    reps = self_ref.shape[1] // cols
    for c in reversed(range(reps)):
        at = column_block(split, rep_ref[0], c, reps, cols)
        value = dot(feat, self_ref[:, at]) + dot(agg, neigh_ref[:, at])
        if not split:
            part_refs[0][c] = value.astype(BF16)

            @pl.when(rep_ref[0] == c)
            def _():
                own_ref[...] = value
        elif c == 0:
            own_ref[...] = value
        elif c == 2:
            part_refs[0][...] = value
        else:
            part_refs[1][c // 2] = value.astype(BF16)


def finish_gate(pre, gout_ref, hid_ref, gpre_ref):
    gate = jax.nn.sigmoid(pre)
    hid_ref[...] = (pre * gate).astype(BF16)
    gpre_ref[...] = (gout_ref[...].astype(F32) * (gate + pre * gate * (1.0 - gate))).astype(BF16)


def gate_body(rep_ref, recv_ref, own_ref, gout_ref, hid_ref, gpre_ref):
    pre = own_ref[...]
    for c in range(recv_ref.shape[0]):
        pre = pre + jnp.where(rep_ref[0] == c, 0.0, recv_ref[c].astype(F32))
    finish_gate(pre, gout_ref, hid_ref, gpre_ref)


def across_body(mine_ref, beside_ref, out_ref):
    out_ref[...] = (mine_ref[...] + beside_ref[1].astype(F32)).astype(BF16)


def gate_blocks_body(own_ref, gout_ref, beside_ref, across_ref, hid_ref, gpre_ref):
    pre = own_ref[...] + beside_ref[0].astype(F32) + across_ref[...].astype(F32)
    finish_gate(pre, gout_ref, hid_ref, gpre_ref)


def back_body(
    high_ref, low_ref, deg_ref, self_ref, neigh_ref, grad_ref, total_ref, mirror_ref
):
    rows, cols = total_ref.shape
    direct = jnp.zeros((rows, cols), F32)
    gagg = jnp.zeros((rows, cols), F32)
    for c in range(grad_ref.shape[0]):
        grad = grad_ref[c]
        at = slice(c * cols, (c + 1) * cols)
        gagg += dot(grad, neigh_ref[:, at], COLS)
        direct += dot(grad, self_ref[:, at], COLS)
    gagg = (gagg / wide_degree(deg_ref, cols)).astype(BF16)
    table = dot(high_ref[...], gagg, ROWS) + dot(low_ref[...], gagg, ROWS)
    total_ref[...] = direct + table[:rows]
    mirror_ref[...] = table[rows:].astype(BF16)


def weight_body(feat_ref, agg_ref, gfull_ref, out_ref):
    cols = feat_ref.shape[1]
    parts = out_ref.shape[0]
    piece = out_ref.shape[1] // 2
    for k, ref in enumerate((feat_ref, agg_ref)):
        left = ref[...]
        for c in range(gfull_ref.shape[0]):
            value = dot(left, gfull_ref[c], ROWS)
            out_ref[:, k * piece:(k + 1) * piece, c * cols:(c + 1) * cols] = value.reshape(
                parts, piece, cols
            ).astype(BF16)


def sum_body(scale, recv_ref, self_ref, neigh_ref):
    piece = self_ref.shape[0]
    for k, ref in enumerate((self_ref, neigh_ref)):
        total = jnp.zeros(ref.shape, F32)
        for d in range(recv_ref.shape[0]):
            total += recv_ref[d, k * piece:(k + 1) * piece].astype(F32)
        ref[...] = (total * scale).astype(BF16)


def group_weight_body(dom_ref, rep_ref, *refs):
    count = (len(refs) - 4) // 2
    rows, grads, (mine_ref, send_ref, hold_ref, total_ref) = (
        refs[:count], refs[count:2 * count], refs[2 * count:]
    )
    for offset, ref in enumerate(grads):
        hold_ref[lax.bitwise_xor(rep_ref[0], offset)] = ref[...]
    lanes = mine_ref.shape[2]
    layer, side = dom_ref[0] // 2, dom_ref[0] % 2
    for k in range(2):
        total = jnp.zeros(total_ref.shape, F32)
        for offset in range(count):
            total += dot(rows[offset][k], hold_ref[lax.bitwise_xor(layer, offset)], ROWS)
        total_ref[...] = total
        mine_ref[k] = total_ref[:, block_rows(side, 0, lanes)]
        send_ref[k] = total_ref[:, block_rows(side, 1, lanes)].astype(BF16)


def join_body(scale, mine_ref, *refs):
    total = mine_ref[...]
    for ref in refs[:-1]:
        total = total + ref[...].astype(F32)
    refs[-1][...] = (total * scale).astype(BF16)


def place_body(dom_ref, *refs):
    blocks, outs, sems = refs[:-3], refs[-3:-1], refs[-1]
    copies = []
    lanes = blocks[0].shape[2]
    for offset, block in enumerate(blocks):
        at = block_rows(dom_ref[0], offset, lanes)
        for k, out_ref in enumerate(outs):
            copies.append(
                pltpu.make_async_copy(block.at[k], out_ref.at[:, at], sems.at[2 * offset + k])
            )
            copies[-1].start()
    for copy in copies:
        copy.wait()


def scatter_body(onehot_ref, total_ref, ret_ref, out_ref):
    out_ref[...] = (total_ref[...] + dot(onehot_ref[...], ret_ref[...])).astype(BF16)


def swap(array, axis, offset):
    return lax.ppermute(array, axis, [(i, i ^ offset) for i in range(lax.axis_size(axis))])


def gather_layers(array):
    far = swap(array, "dom", 4)
    return [array, swap(array, "dom", 2), far, swap(far, "dom", 2)]


def gather_pieces(array, peers):
    out = dict(zip(range(0, peers, 2), gather_layers(array)))
    for offset in range(0, peers, 2):
        out[offset + 1] = swap(out[offset], "dom", 1)
    return [out[offset] for offset in range(peers)]


def local(
    features, w_self, w_neigh, grad_out, mirror_list, mirror_count, tile_dst, tile_src, tiles
):
    rows, cols = features.shape
    width = w_self.shape[1]
    peers, slots = mirror_list.shape
    mirrors = peers * slots
    table_rows = rows + mirrors
    reps = width // cols
    struct = jax.ShapeDtypeStruct
    block = struct((rows, cols), BF16)
    rep = lax.axis_index("rep").astype(jnp.int32).reshape(1)
    dom = lax.axis_index("dom").astype(jnp.int32).reshape(1)
    lanes = width // peers
    halves = peers // reps
    split = peers == 8 and reps == 4 and slots % 16 == 0 and lanes % 128 == 0
    mirror_out = struct((mirrors, cols), BF16)

    def exchange(array):
        return lax.all_to_all(
            array.reshape(peers, slots, cols), "dom", split_axis=0, concat_axis=0, tiled=True
        ).reshape(mirrors, cols)

    onehot, outgoing = call(
        pick_body, (struct((rows, mirrors), BF16), mirror_out),
        [("h", mirror_count), ("h", mirror_list), ("h", features)],
        scratch=[
            pltpu.SMEM(mirror_count.shape, jnp.int32), pltpu.VMEM(mirror_list.shape, jnp.int32),
            pltpu.VMEM((rows, cols), BF16), pltpu.SemaphoreType.DMA((3,)),
        ],
        vmem=58,
        flops=2 * mirrors * rows * cols, moved=600_000,
    )
    incoming = exchange(outgoing)
    tiles_late, feat_late, self_late, neigh_late, _ = lax.optimization_barrier(
        (tiles, features, w_self, w_neigh, outgoing)
    )
    high, low, degree, self_near, neigh_near = call(
        prep_body,
        (
            struct((rows, table_rows), BF16), struct((rows, table_rows), BF16),
            struct((rows, 128), F32), struct(w_self.shape, BF16), struct(w_neigh.shape, BF16),
        ),
        [
            ("s", tile_dst), ("s", tile_src), ("v", tiles_late), ("h", self_late),
            ("h", neigh_late),
        ],
        scratch=[pltpu.VMEM((rows, table_rows), F32), pltpu.SemaphoreType.DMA((2,))],
        flops=1_000_000, moved=3_000_000,
    )
    own, agg, *parts = call(
        functools.partial(aggregate_body, split),
        (struct((rows, cols), F32), struct((2, rows, cols), BF16) if split else block)
        + (
            (struct((rows, cols), F32), struct((2, rows, cols), BF16)) if split
            else (struct((reps, rows, cols), BF16),)
        ),
        [
            ("s", rep), ("v", feat_late), ("v", incoming), ("v", high), ("v", low),
            ("v", degree), ("v", self_near), ("v", neigh_near),
        ],
        scratch=[pltpu.VMEM((table_rows, cols), BF16)],
        flops=600_000_000, moved=3_000_000,
    )
    scale = float(rows * peers) ** (-0.5)
    if split:
        kept = gather_layers(agg)
        beside = swap(parts[1], "rep", 1)
        across = call(
            across_body, block, [("v", parts[0]), ("v", beside)], flops=100_000, moved=500_000
        )
        across = swap(across, "rep", 2)
        hidden, grad_pre = call(
            gate_blocks_body, (block, block),
            [("v", own), ("v", grad_out), ("v", beside), ("v", across)],
            flops=2_000_000, moved=1_300_000,
        )
        perm = [
            (p * reps + r, (halves * r + p % halves) * reps + p // halves)
            for p in range(peers) for r in range(reps)
        ]
        layer_grad = lax.ppermute(grad_pre, ("dom", "rep"), perm)
    else:
        recv = lax.all_to_all(parts[0], "rep", split_axis=0, concat_axis=0, tiled=True)
        hidden, grad_pre = call(
            gate_body, (block, block),
            [("s", rep), ("v", recv), ("v", own), ("v", grad_out)],
            flops=2_000_000, moved=1_300_000,
        )
    grad_full = lax.all_gather(grad_pre, "rep", axis=0, tiled=False)
    total, mirror_grad = call(
        back_body, (struct((rows, cols), F32), mirror_out),
        [
            ("v", high), ("v", low), ("v", degree), ("v", self_near), ("v", neigh_near),
            ("v", grad_full),
        ],
        flops=600_000_000, moved=3_000_000,
    )
    if split:
        piece = struct((2, rows, lanes), BF16)
        layer_grad, _ = lax.optimization_barrier((layer_grad, grad_full))
        layer_grads = [layer_grad] + [swap(layer_grad, "rep", k) for k in range(1, reps)]
        mine, send = call(
            group_weight_body, (struct((2, rows, lanes), F32), piece),
            [("s", dom), ("s", rep)] + [("v", part) for part in kept + layer_grads],
            scratch=[pltpu.VMEM((reps, rows, cols), BF16), pltpu.VMEM((rows, cols), F32)],
            flops=600_000_000, moved=3_000_000,
        )
        mine = call(
            functools.partial(join_body, scale), piece,
            [("v", mine), ("v", swap(send, "dom", 1))], flops=200_000, moved=500_000,
        )
        pieces = gather_pieces(mine, peers)
    returned = exchange(mirror_grad)
    grad_features = call(
        scatter_body, block, [("v", onehot), ("v", total), ("v", returned)],
        flops=2 * mirrors * rows * cols, moved=700_000,
    )
    if split:
        out_self, out_neigh = call(
            place_body, (struct((rows, width), BF16), struct((rows, width), BF16)),
            [("s", dom)] + [("v", part) for part in pieces],
            scratch=[pltpu.SemaphoreType.DMA((2 * peers,))], moved=2_000_000, out="h",
        )
    else:
        piece = cols // peers
        partial = call(
            weight_body, struct((peers, 2 * piece, width), BF16),
            [("v", features), ("v", agg), ("v", grad_full)],
            flops=600_000_000, moved=2_000_000,
        )
        gathered = lax.all_to_all(partial, "dom", split_axis=0, concat_axis=0, tiled=True)
        mine_self, mine_neigh = call(
            functools.partial(sum_body, scale),
            (struct((piece, width), BF16), struct((piece, width), BF16)),
            [("v", gathered)], flops=1_000_000, moved=1_200_000,
        )
        out_self = lax.all_gather(mine_self, "dom", axis=0, tiled=True)
        out_neigh = lax.all_gather(mine_neigh, "dom", axis=0, tiled=True)
    return hidden, grad_features, out_self, out_neigh


def solution(mesh):
    in_specs = (
        P("dom", "rep"),
        P("rep", None),
        P("rep", None),
        P("dom", "rep"),
        P("dom", None),
        P("dom"),
        P("dom"),
        P("dom"),
        P("dom", None, None),
    )
    out_specs = (P("dom", "rep"), P("dom", "rep"), P("rep", None), P("rep", None))
    return jax.shard_map(local, mesh=mesh, in_specs=in_specs, out_specs=out_specs, check_vma=False)
```

```python
import functools

import jax
import jax.numpy as jnp
from jax import lax
from jax.experimental import pallas as pl
from jax.experimental.pallas import tpu as pltpu
from jax.sharding import PartitionSpec as P

F32 = jnp.float32
BF16 = jnp.bfloat16
SPECS = {
    "v": pl.BlockSpec(memory_space=pltpu.VMEM),
    "s": pl.BlockSpec(memory_space=pltpu.SMEM),
    "h": pl.BlockSpec(memory_space=pltpu.HBM),
}
ROWS = (((0,), (0,)), ((), ()))
COLS = (((1,), (1,)), ((), ()))


def call(body, outs, ins, scratch=(), flops=0, moved=0, vmem=16, out="v"):
    return pl.pallas_call(
        body,
        out_shape=outs,
        in_specs=[SPECS[spec] for spec, _ in ins],
        out_specs=jax.tree.map(lambda _: SPECS[out], outs),
        scratch_shapes=list(scratch),
        compiler_params=pltpu.CompilerParams(vmem_limit_bytes=vmem * 1024 * 1024),
        cost_estimate=pl.CostEstimate(flops=flops, bytes_accessed=moved, transcendentals=0),
    )(*[array for _, array in ins])


def dot(left, right, dims=(((1,), (0,)), ((), ()))):
    return lax.dot_general(left, right, dims, preferred_element_type=F32)


def block_rows(place, offset, size):
    return pl.ds(pl.multiple_of(lax.bitwise_xor(place, offset) * size, size), size)


def row_onehot(count_ref, lists, rows):
    peers, slots = lists.shape
    peer = lax.broadcasted_iota(jnp.int32, (peers, slots), 0)
    slot = lax.broadcasted_iota(jnp.int32, (peers, slots), 1)

    def fill(at, used):
        return jnp.where(peer == at, count_ref[at], used)

    used = jnp.zeros((peers, slots), jnp.int32)
    if peers <= 16:
        for at in range(peers):
            used = fill(at, used)
    else:
        used = lax.fori_loop(0, peers, fill, used)
    index = jnp.where(slot < used, lists, -1).astype(F32).astype(BF16)
    flat = peers * slots
    spread = (
        lax.broadcasted_iota(jnp.int32, (slots, flat), 0)
        == lax.broadcasted_iota(jnp.int32, (slots, flat), 1) % slots
    )
    wide = dot(index, spread.astype(F32).astype(BF16))
    mine = (
        lax.broadcasted_iota(jnp.int32, (peers, flat), 0)
        == lax.broadcasted_iota(jnp.int32, (peers, flat), 1) // slots
    )
    line = jnp.sum(jnp.where(mine, wide, 0.0), axis=0, keepdims=True).astype(jnp.int32)
    hit = lax.broadcasted_iota(jnp.int32, (rows, flat), 0) == line
    return hit.astype(F32).astype(BF16)


def pick_body(
    count_hbm, list_hbm, feat_hbm, onehot_ref, out_ref, count_ref, list_ref, feat_ref, sems
):
    copies = [
        pltpu.make_async_copy(src, dst, sems.at[k])
        for k, (src, dst) in enumerate(
            ((count_hbm, count_ref), (list_hbm, list_ref), (feat_hbm, feat_ref))
        )
    ]
    for copy in copies:
        copy.start()
    for copy in copies:
        copy.wait()
    onehot = row_onehot(count_ref, list_ref[...], feat_ref.shape[0])
    onehot_ref[...] = onehot
    out_ref[...] = dot(onehot, feat_ref[...], ROWS).astype(BF16)


def prep_body(
    dst_ref, src_ref, tiles_ref, self_hbm, neigh_hbm,
    high_ref, low_ref, deg_ref, self_ref, neigh_ref, adj_ref, sems,
):
    copies = [
        pltpu.make_async_copy(src, dst, sems.at[k])
        for k, (src, dst) in enumerate(((self_hbm, self_ref), (neigh_hbm, neigh_ref)))
    ]
    for copy in copies:
        copy.start()
    slots, side, _ = tiles_ref.shape
    adj_ref[...] = jnp.zeros(adj_ref.shape, F32)
    for t in range(slots):
        dst = pl.ds(pl.multiple_of(dst_ref[t] * side, side), side)
        src = pl.ds(pl.multiple_of(src_ref[t] * side, side), side)
        adj_ref[dst, src] += tiles_ref[t].astype(F32)
    adj = adj_ref[...]
    high = adj.astype(BF16)
    high_ref[...] = high
    low_ref[...] = (adj - high.astype(F32)).astype(BF16)
    degree = jnp.maximum(jnp.sum(adj, axis=1, keepdims=True), 1.0)
    deg_ref[...] = jnp.broadcast_to(degree, deg_ref.shape)
    for copy in copies:
        copy.wait()


def column_block(split, rep, c, reps, cols):
    other = lax.bitwise_xor(rep, c) if split else c
    return pl.ds(pl.multiple_of(other * cols, cols), cols)


def wide_degree(deg_ref, cols):
    return jnp.concatenate([deg_ref[...]] * (cols // deg_ref.shape[1]), axis=1)


def aggregate_body(
    split, rep_ref, feat_ref, inc_ref, high_ref, low_ref, deg_ref, self_ref, neigh_ref,
    own_ref, agg_ref, *refs,
):
    part_refs, table_ref = refs[:-1], refs[-1]
    rows, cols = feat_ref.shape
    feat = feat_ref[...]
    table_ref[:rows] = feat
    table_ref[rows:] = inc_ref[...]
    table = table_ref[...]
    summed = dot(high_ref[...], table) + dot(low_ref[...], table)
    agg = (summed / wide_degree(deg_ref, cols)).astype(BF16)
    agg_ref[...] = agg
    reps = self_ref.shape[1] // cols
    for c in reversed(range(reps)):
        at = column_block(split, rep_ref[0], c, reps, cols)
        value = dot(feat, self_ref[:, at]) + dot(agg, neigh_ref[:, at])
        if not split:
            part_refs[0][c] = value.astype(BF16)

            @pl.when(rep_ref[0] == c)
            def _():
                own_ref[...] = value
        elif c == 0:
            own_ref[...] = value
        elif c == 2:
            part_refs[0][...] = value
        else:
            part_refs[1][c // 2] = value.astype(BF16)


def finish_gate(pre, gout_ref, hid_ref, gpre_ref):
    gate = jax.nn.sigmoid(pre)
    hid_ref[...] = (pre * gate).astype(BF16)
    gpre_ref[...] = (gout_ref[...].astype(F32) * (gate + pre * gate * (1.0 - gate))).astype(BF16)


def gate_body(rep_ref, recv_ref, own_ref, gout_ref, hid_ref, gpre_ref):
    pre = own_ref[...]
    for c in range(recv_ref.shape[0]):
        pre = pre + jnp.where(rep_ref[0] == c, 0.0, recv_ref[c].astype(F32))
    finish_gate(pre, gout_ref, hid_ref, gpre_ref)


def across_body(mine_ref, beside_ref, out_ref):
    out_ref[...] = (mine_ref[...] + beside_ref[1].astype(F32)).astype(BF16)


def gate_blocks_body(own_ref, gout_ref, beside_ref, across_ref, hid_ref, gpre_ref):
    pre = own_ref[...] + beside_ref[0].astype(F32) + across_ref[...].astype(F32)
    finish_gate(pre, gout_ref, hid_ref, gpre_ref)


def back_body(
    high_ref, low_ref, deg_ref, self_ref, neigh_ref, grad_ref, total_ref, mirror_ref
):
    rows, cols = total_ref.shape
    direct = jnp.zeros((rows, cols), F32)
    gagg = jnp.zeros((rows, cols), F32)
    for c in range(grad_ref.shape[0]):
        grad = grad_ref[c]
        at = slice(c * cols, (c + 1) * cols)
        gagg += dot(grad, neigh_ref[:, at], COLS)
        direct += dot(grad, self_ref[:, at], COLS)
    gagg = (gagg / wide_degree(deg_ref, cols)).astype(BF16)
    table = dot(high_ref[...], gagg, ROWS) + dot(low_ref[...], gagg, ROWS)
    total_ref[...] = direct + table[:rows]
    mirror_ref[...] = table[rows:].astype(BF16)


def weight_body(feat_ref, agg_ref, gfull_ref, out_ref):
    cols = feat_ref.shape[1]
    parts = out_ref.shape[0]
    piece = out_ref.shape[1] // 2
    for k, ref in enumerate((feat_ref, agg_ref)):
        left = ref[...]
        for c in range(gfull_ref.shape[0]):
            value = dot(left, gfull_ref[c], ROWS)
            out_ref[:, k * piece:(k + 1) * piece, c * cols:(c + 1) * cols] = value.reshape(
                parts, piece, cols
            ).astype(BF16)


def sum_body(scale, recv_ref, self_ref, neigh_ref):
    piece = self_ref.shape[0]
    for k, ref in enumerate((self_ref, neigh_ref)):
        total = jnp.zeros(ref.shape, F32)
        for d in range(recv_ref.shape[0]):
            total += recv_ref[d, k * piece:(k + 1) * piece].astype(F32)
        ref[...] = (total * scale).astype(BF16)


def group_weight_body(dom_ref, own_ref, other_ref, *refs):
    rows, mine_ref, send_refs, total_ref = refs[:4], refs[4], refs[5:-1], refs[-1]
    lanes = mine_ref.shape[2]
    layer, side = dom_ref[0] // 2, dom_ref[0] % 2
    count = other_ref.shape[0]
    for k in range(2):
        own, other = rows[2 * k][...], rows[2 * k + 1][...]
        for c in range(count):
            cols = own.shape[1]
            total_ref[:, c * cols:(c + 1) * cols] = dot(
                own, own_ref[side * count + c], ROWS
            ) + dot(other, other_ref[c], ROWS)
        mine_ref[k] = total_ref[:, block_rows(layer, 0, lanes)]
        for offset, ref in enumerate(send_refs):
            ref[k] = total_ref[:, block_rows(layer, offset + 1, lanes)].astype(BF16)


def join_body(scale, mine_ref, *refs):
    total = mine_ref[...]
    for ref in refs[:-1]:
        total = total + ref[...].astype(F32)
    refs[-1][...] = (total * scale).astype(BF16)


def place_body(dom_ref, *refs):
    blocks, outs, sems = refs[:-3], refs[-3:-1], refs[-1]
    copies = []
    lanes = blocks[0].shape[2]
    for offset, block in enumerate(blocks):
        place = lax.bitwise_xor(dom_ref[0], offset)
        at = (place % 2) * (len(blocks) // 2) + place // 2
        at = pl.ds(pl.multiple_of(at * lanes, lanes), lanes)
        for k, out_ref in enumerate(outs):
            copies.append(
                pltpu.make_async_copy(block.at[k], out_ref.at[:, at], sems.at[2 * offset + k])
            )
            copies[-1].start()
    for copy in copies:
        copy.wait()


def scatter_body(onehot_ref, total_ref, ret_ref, out_ref):
    out_ref[...] = (total_ref[...] + dot(onehot_ref[...], ret_ref[...])).astype(BF16)


def swap(array, axis, offset):
    return lax.ppermute(array, axis, [(i, i ^ offset) for i in range(lax.axis_size(axis))])


def gather_pieces(array, peers):
    out = {0: array, 4: swap(array, "dom", 4), 2: swap(array, "dom", 2)}
    out[1] = swap(array, "dom", 1)
    out[4], out[1] = lax.optimization_barrier((out[4], out[1]))
    out[6] = swap(out[4], "dom", 2)
    for offset in range(2, peers, 2):
        out[offset + 1] = swap(out[offset], "dom", 1)
    return [out[offset] for offset in range(peers)]


def local(
    features, w_self, w_neigh, grad_out, mirror_list, mirror_count, tile_dst, tile_src, tiles
):
    rows, cols = features.shape
    width = w_self.shape[1]
    peers, slots = mirror_list.shape
    mirrors = peers * slots
    table_rows = rows + mirrors
    reps = width // cols
    struct = jax.ShapeDtypeStruct
    block = struct((rows, cols), BF16)
    rep = lax.axis_index("rep").astype(jnp.int32).reshape(1)
    dom = lax.axis_index("dom").astype(jnp.int32).reshape(1)
    lanes = width // peers
    halves = peers // reps
    split = peers == 8 and reps == 4 and slots % 16 == 0 and lanes % 128 == 0
    mirror_out = struct((mirrors, cols), BF16)

    def exchange(array):
        return lax.all_to_all(
            array.reshape(peers, slots, cols), "dom", split_axis=0, concat_axis=0, tiled=True
        ).reshape(mirrors, cols)

    onehot, outgoing = call(
        pick_body, (struct((rows, mirrors), BF16), mirror_out),
        [("h", mirror_count), ("h", mirror_list), ("h", features)],
        scratch=[
            pltpu.SMEM(mirror_count.shape, jnp.int32), pltpu.VMEM(mirror_list.shape, jnp.int32),
            pltpu.VMEM((rows, cols), BF16), pltpu.SemaphoreType.DMA((3,)),
        ],
        vmem=58,
        flops=2 * mirrors * rows * cols, moved=600_000,
    )
    incoming = exchange(outgoing)
    tiles_late, feat_late, self_late, neigh_late, _ = lax.optimization_barrier(
        (tiles, features, w_self, w_neigh, outgoing)
    )
    high, low, degree, self_near, neigh_near = call(
        prep_body,
        (
            struct((rows, table_rows), BF16), struct((rows, table_rows), BF16),
            struct((rows, 128), F32), struct(w_self.shape, BF16), struct(w_neigh.shape, BF16),
        ),
        [
            ("s", tile_dst), ("s", tile_src), ("v", tiles_late), ("h", self_late),
            ("h", neigh_late),
        ],
        scratch=[pltpu.VMEM((rows, table_rows), F32), pltpu.SemaphoreType.DMA((2,))],
        flops=1_000_000, moved=3_000_000,
    )
    if split:
        feat_beside = swap(features, "dom", 1)
        incoming, feat_beside = lax.optimization_barrier((incoming, feat_beside))
    own, agg, *parts = call(
        functools.partial(aggregate_body, split),
        (struct((rows, cols), F32), block)
        + (
            (struct((rows, cols), F32), struct((2, rows, cols), BF16)) if split
            else (struct((reps, rows, cols), BF16),)
        ),
        [
            ("s", rep), ("v", feat_late), ("v", incoming), ("v", high), ("v", low),
            ("v", degree), ("v", self_near), ("v", neigh_near),
        ],
        scratch=[pltpu.VMEM((table_rows, cols), BF16)],
        flops=600_000_000, moved=3_000_000,
    )
    scale = float(rows * peers) ** (-0.5)
    if split:
        agg_beside = swap(agg, "dom", 1)
        grad_out, agg_beside = lax.optimization_barrier((grad_out, agg_beside))
        beside = swap(parts[1], "rep", 1)
        across = call(
            across_body, block, [("v", parts[0]), ("v", beside)], flops=100_000, moved=500_000
        )
        across = swap(across, "rep", 2)
        hidden, grad_pre = call(
            gate_blocks_body, (block, block),
            [("v", own), ("v", grad_out), ("v", beside), ("v", across)],
            flops=2_000_000, moved=1_300_000,
        )
    else:
        recv = lax.all_to_all(parts[0], "rep", split_axis=0, concat_axis=0, tiled=True)
        hidden, grad_pre = call(
            gate_body, (block, block),
            [("s", rep), ("v", recv), ("v", own), ("v", grad_out)],
            flops=2_000_000, moved=1_300_000,
        )
    grad_full = lax.all_gather(grad_pre, "rep", axis=0, tiled=False)
    total, mirror_grad = call(
        back_body, (struct((rows, cols), F32), mirror_out),
        [
            ("v", high), ("v", low), ("v", degree), ("v", self_near), ("v", neigh_near),
            ("v", grad_full),
        ],
        flops=600_000_000, moved=3_000_000,
    )
    if split:
        start = (1 - dom[0] % 2) * (reps // 2)
        half = swap(lax.dynamic_slice_in_dim(grad_full, start, reps // 2, 0), "dom", 1)
        half, mirror_grad = lax.optimization_barrier((half, mirror_grad))
        piece = struct((2, rows, lanes), BF16)
        mine, *sends = call(
            group_weight_body, (struct((2, rows, lanes), F32),) + (piece,) * (reps - 1),
            [
                ("s", dom), ("v", grad_full), ("v", half), ("v", features),
                ("v", feat_beside), ("v", agg), ("v", agg_beside),
            ],
            scratch=[pltpu.VMEM((rows, width // 2), F32)],
            flops=600_000_000, moved=3_000_000,
        )
        layers = [swap(send, "dom", 2 * k + 2) for k, send in enumerate(sends)]
        mine = call(
            functools.partial(join_body, scale), piece,
            [("v", mine)] + [("v", got) for got in layers], flops=200_000, moved=500_000,
        )
        pieces = gather_pieces(mine, peers)
    returned = exchange(mirror_grad)
    grad_features = call(
        scatter_body, block, [("v", onehot), ("v", total), ("v", returned)],
        flops=2 * mirrors * rows * cols, moved=700_000,
    )
    if split:
        out_self, out_neigh = call(
            place_body, (struct((rows, width), BF16), struct((rows, width), BF16)),
            [("s", dom)] + [("v", part) for part in pieces],
            scratch=[pltpu.SemaphoreType.DMA((2 * peers,))], moved=2_000_000, out="h",
        )
    else:
        piece = cols // peers
        partial = call(
            weight_body, struct((peers, 2 * piece, width), BF16),
            [("v", features), ("v", agg), ("v", grad_full)],
            flops=600_000_000, moved=2_000_000,
        )
        gathered = lax.all_to_all(partial, "dom", split_axis=0, concat_axis=0, tiled=True)
        mine_self, mine_neigh = call(
            functools.partial(sum_body, scale),
            (struct((piece, width), BF16), struct((piece, width), BF16)),
            [("v", gathered)], flops=1_000_000, moved=1_200_000,
        )
        out_self = lax.all_gather(mine_self, "dom", axis=0, tiled=True)
        out_neigh = lax.all_gather(mine_neigh, "dom", axis=0, tiled=True)
    return hidden, grad_features, out_self, out_neigh


def solution(mesh):
    in_specs = (
        P("dom", "rep"),
        P("rep", None),
        P("rep", None),
        P("dom", "rep"),
        P("dom", None),
        P("dom"),
        P("dom"),
        P("dom"),
        P("dom", None, None),
    )
    out_specs = (P("dom", "rep"), P("dom", "rep"), P("rep", None), P("rep", None))
    return jax.shard_map(local, mesh=mesh, in_specs=in_specs, out_specs=out_specs, check_vma=False)
```

```python
import functools

import jax
import jax.numpy as jnp
from jax import lax
from jax.experimental import pallas as pl
from jax.experimental.pallas import tpu as pltpu
from jax.sharding import PartitionSpec as P

F32 = jnp.float32
BF16 = jnp.bfloat16
SPECS = {
    "v": pl.BlockSpec(memory_space=pltpu.VMEM),
    "s": pl.BlockSpec(memory_space=pltpu.SMEM),
    "h": pl.BlockSpec(memory_space=pltpu.HBM),
}
ROWS = (((0,), (0,)), ((), ()))
COLS = (((1,), (1,)), ((), ()))


def call(body, outs, ins, scratch=(), flops=0, moved=0, vmem=16, out="v"):
    return pl.pallas_call(
        body,
        out_shape=outs,
        in_specs=[SPECS[spec] for spec, _ in ins],
        out_specs=jax.tree.map(lambda _: SPECS[out], outs),
        scratch_shapes=list(scratch),
        compiler_params=pltpu.CompilerParams(vmem_limit_bytes=vmem * 1024 * 1024),
        cost_estimate=pl.CostEstimate(flops=flops, bytes_accessed=moved, transcendentals=0),
    )(*[array for _, array in ins])


def dot(left, right, dims=(((1,), (0,)), ((), ()))):
    return lax.dot_general(left, right, dims, preferred_element_type=F32)


def block_rows(place, offset, size):
    return pl.ds(pl.multiple_of(lax.bitwise_xor(place, offset) * size, size), size)


def row_onehot(count_ref, lists, rows):
    peers, slots = lists.shape
    peer = lax.broadcasted_iota(jnp.int32, (peers, slots), 0)
    slot = lax.broadcasted_iota(jnp.int32, (peers, slots), 1)

    def fill(at, used):
        return jnp.where(peer == at, count_ref[at], used)

    used = jnp.zeros((peers, slots), jnp.int32)
    if peers <= 16:
        for at in range(peers):
            used = fill(at, used)
    else:
        used = lax.fori_loop(0, peers, fill, used)
    index = jnp.where(slot < used, lists, -1).astype(F32).astype(BF16)
    flat = peers * slots
    spread = (
        lax.broadcasted_iota(jnp.int32, (slots, flat), 0)
        == lax.broadcasted_iota(jnp.int32, (slots, flat), 1) % slots
    )
    wide = dot(index, spread.astype(F32).astype(BF16))
    mine = (
        lax.broadcasted_iota(jnp.int32, (peers, flat), 0)
        == lax.broadcasted_iota(jnp.int32, (peers, flat), 1) // slots
    )
    line = jnp.sum(jnp.where(mine, wide, 0.0), axis=0, keepdims=True).astype(jnp.int32)
    hit = lax.broadcasted_iota(jnp.int32, (rows, flat), 0) == line
    return hit.astype(F32).astype(BF16)


def pick_body(
    count_hbm, list_hbm, feat_hbm, onehot_ref, out_ref, count_ref, list_ref, feat_ref, sems
):
    copies = [
        pltpu.make_async_copy(src, dst, sems.at[k])
        for k, (src, dst) in enumerate(
            ((count_hbm, count_ref), (list_hbm, list_ref), (feat_hbm, feat_ref))
        )
    ]
    for copy in copies:
        copy.start()
    for copy in copies:
        copy.wait()
    onehot = row_onehot(count_ref, list_ref[...], feat_ref.shape[0])
    onehot_ref[...] = onehot
    out_ref[...] = dot(onehot, feat_ref[...], ROWS).astype(BF16)


def prep_body(
    dst_ref, src_ref, tiles_ref, self_hbm, neigh_hbm,
    high_ref, low_ref, deg_ref, self_ref, neigh_ref, adj_ref, sems,
):
    copies = [
        pltpu.make_async_copy(src, dst, sems.at[k])
        for k, (src, dst) in enumerate(((self_hbm, self_ref), (neigh_hbm, neigh_ref)))
    ]
    for copy in copies:
        copy.start()
    slots, side, _ = tiles_ref.shape
    adj_ref[...] = jnp.zeros(adj_ref.shape, F32)
    for t in range(slots):
        dst = pl.ds(pl.multiple_of(dst_ref[t] * side, side), side)
        src = pl.ds(pl.multiple_of(src_ref[t] * side, side), side)
        adj_ref[dst, src] += tiles_ref[t].astype(F32)
    adj = adj_ref[...]
    high = adj.astype(BF16)
    high_ref[...] = high
    low_ref[...] = (adj - high.astype(F32)).astype(BF16)
    degree = jnp.maximum(jnp.sum(adj, axis=1, keepdims=True), 1.0)
    deg_ref[...] = jnp.broadcast_to(degree, deg_ref.shape)
    for copy in copies:
        copy.wait()


def column_block(split, rep, c, reps, cols):
    other = lax.bitwise_xor(rep, c) if split else c
    return pl.ds(pl.multiple_of(other * cols, cols), cols)


def wide_degree(deg_ref, cols):
    return jnp.concatenate([deg_ref[...]] * (cols // deg_ref.shape[1]), axis=1)


def aggregate_body(
    split, rep_ref, feat_ref, inc_ref, high_ref, low_ref, deg_ref, self_ref, neigh_ref,
    own_ref, agg_ref, *refs,
):
    part_refs, table_ref = refs[:-1], refs[-1]
    rows, cols = feat_ref.shape
    feat = feat_ref[...]
    table_ref[:rows] = feat
    table_ref[rows:] = inc_ref[...]
    table = table_ref[...]
    summed = dot(high_ref[...], table) + dot(low_ref[...], table)
    agg = (summed / wide_degree(deg_ref, cols)).astype(BF16)
    agg_ref[...] = agg
    reps = self_ref.shape[1] // cols
    for c in reversed(range(reps)):
        at = column_block(split, rep_ref[0], c, reps, cols)
        value = dot(feat, self_ref[:, at]) + dot(agg, neigh_ref[:, at])
        if not split:
            part_refs[0][c] = value.astype(BF16)

            @pl.when(rep_ref[0] == c)
            def _():
                own_ref[...] = value
        elif c == 0:
            own_ref[...] = value
        elif c == 2:
            part_refs[0][...] = value
        else:
            part_refs[1][c // 2] = value.astype(BF16)


def finish_gate(pre, gout_ref, hid_ref, gpre_ref):
    gate = jax.nn.sigmoid(pre)
    hid_ref[...] = (pre * gate).astype(BF16)
    gpre_ref[...] = (gout_ref[...].astype(F32) * (gate + pre * gate * (1.0 - gate))).astype(BF16)


def gate_body(rep_ref, recv_ref, own_ref, gout_ref, hid_ref, gpre_ref):
    pre = own_ref[...]
    for c in range(recv_ref.shape[0]):
        pre = pre + jnp.where(rep_ref[0] == c, 0.0, recv_ref[c].astype(F32))
    finish_gate(pre, gout_ref, hid_ref, gpre_ref)


def across_body(mine_ref, beside_ref, out_ref):
    out_ref[...] = (mine_ref[...] + beside_ref[1].astype(F32)).astype(BF16)


def gate_blocks_body(dom_ref, own_ref, gout_ref, beside_ref, across_ref, hid_ref, gpre_ref, send_ref):
    pre = own_ref[...] + beside_ref[0].astype(F32) + across_ref[...].astype(F32)
    finish_gate(pre, gout_ref, hid_ref, gpre_ref)
    send_ref[...] = gpre_ref[:, block_rows(dom_ref[0] % 2, 1, send_ref.shape[1])]


def back_body(
    split, rep_ref, high_ref, low_ref, deg_ref, self_ref, neigh_ref, *refs,
):
    grads, (total_ref, mirror_ref) = refs[:-2], refs[-2:]
    rows, cols = total_ref.shape
    reps = self_ref.shape[1] // cols
    direct = jnp.zeros((rows, cols), F32)
    gagg = jnp.zeros((rows, cols), F32)
    for c in range(reps):
        grad = grads[c][...] if split else grads[0][c]
        at = column_block(split, rep_ref[0], c, reps, cols)
        gagg += dot(grad, neigh_ref[:, at], COLS)
        direct += dot(grad, self_ref[:, at], COLS)
    gagg = (gagg / wide_degree(deg_ref, cols)).astype(BF16)
    table = dot(high_ref[...], gagg, ROWS) + dot(low_ref[...], gagg, ROWS)
    total_ref[...] = direct + table[:rows]
    mirror_ref[...] = table[rows:].astype(BF16)


def weight_body(feat_ref, agg_ref, gfull_ref, out_ref):
    cols = feat_ref.shape[1]
    parts = out_ref.shape[0]
    piece = out_ref.shape[1] // 2
    for k, ref in enumerate((feat_ref, agg_ref)):
        left = ref[...]
        for c in range(gfull_ref.shape[0]):
            value = dot(left, gfull_ref[c], ROWS)
            out_ref[:, k * piece:(k + 1) * piece, c * cols:(c + 1) * cols] = value.reshape(
                parts, piece, cols
            ).astype(BF16)


def sum_body(scale, recv_ref, self_ref, neigh_ref):
    piece = self_ref.shape[0]
    for k, ref in enumerate((self_ref, neigh_ref)):
        total = jnp.zeros(ref.shape, F32)
        for d in range(recv_ref.shape[0]):
            total += recv_ref[d, k * piece:(k + 1) * piece].astype(F32)
        ref[...] = (total * scale).astype(BF16)


def group_weight_body(dom_ref, rep_ref, *refs):
    rows, (mine_ref, far_ref, send_ref, hold_ref) = refs[:4], refs[-4:]
    grads = refs[4:-4]
    count = len(grads) // 2
    lanes = mine_ref.shape[2]
    layer, side = dom_ref[0] // 2, dom_ref[0] % 2
    for c in range(count):
        at = lax.bitwise_xor(rep_ref[0], c)
        hold_ref[0, at] = grads[c][:, block_rows(side, 0, lanes)]
        hold_ref[1, at] = grads[count + c][...]
    for k in range(2):
        own, other = rows[2 * k][...], rows[2 * k + 1][...]
        for offset in range(count):
            at = lax.bitwise_xor(layer, offset)
            value = dot(own, hold_ref[0, at], ROWS) + dot(other, hold_ref[1, at], ROWS)
            if offset == 0:
                mine_ref[k] = value
            elif offset == 2:
                far_ref[k] = value
            else:
                send_ref[offset // 2, k] = value.astype(BF16)


def join_body(scale, mine_ref, next_ref, far_ref, out_ref):
    total = mine_ref[...] + next_ref[0].astype(F32) + far_ref[...].astype(F32)
    out_ref[...] = (total * scale).astype(BF16)


def place_body(dom_ref, *refs):
    blocks, outs, sems = refs[:-3], refs[-3:-1], refs[-1]
    copies = []
    lanes = blocks[0].shape[2]
    for offset, block in enumerate(blocks):
        at = block_rows(dom_ref[0], offset, lanes)
        for k, out_ref in enumerate(outs):
            copies.append(
                pltpu.make_async_copy(block.at[k], out_ref.at[:, at], sems.at[2 * offset + k])
            )
            copies[-1].start()
    for copy in copies:
        copy.wait()


def scatter_body(onehot_ref, total_ref, ret_ref, out_ref):
    out_ref[...] = (total_ref[...] + dot(onehot_ref[...], ret_ref[...])).astype(BF16)


def swap(array, axis, offset):
    return lax.ppermute(array, axis, [(i, i ^ offset) for i in range(lax.axis_size(axis))])


def gather_columns(array):
    across = swap(array, "rep", 2)
    return [array, swap(array, "rep", 1), across, swap(across, "rep", 1)]


def gather_pieces(array, peers):
    out = {0: array, 4: swap(array, "dom", 4), 2: swap(array, "dom", 2)}
    out[1] = swap(array, "dom", 1)
    out[4], out[1] = lax.optimization_barrier((out[4], out[1]))
    out[6] = swap(out[4], "dom", 2)
    for offset in range(2, peers, 2):
        out[offset + 1] = swap(out[offset], "dom", 1)
    return [out[offset] for offset in range(peers)]


def local(
    features, w_self, w_neigh, grad_out, mirror_list, mirror_count, tile_dst, tile_src, tiles
):
    rows, cols = features.shape
    width = w_self.shape[1]
    peers, slots = mirror_list.shape
    mirrors = peers * slots
    table_rows = rows + mirrors
    reps = width // cols
    struct = jax.ShapeDtypeStruct
    block = struct((rows, cols), BF16)
    rep = lax.axis_index("rep").astype(jnp.int32).reshape(1)
    dom = lax.axis_index("dom").astype(jnp.int32).reshape(1)
    lanes = width // peers
    split = peers == 8 and reps == 4 and slots % 16 == 0 and lanes % 128 == 0
    mirror_out = struct((mirrors, cols), BF16)

    def exchange(array):
        return lax.all_to_all(
            array.reshape(peers, slots, cols), "dom", split_axis=0, concat_axis=0, tiled=True
        ).reshape(mirrors, cols)

    onehot, outgoing = call(
        pick_body, (struct((rows, mirrors), BF16), mirror_out),
        [("h", mirror_count), ("h", mirror_list), ("h", features)],
        scratch=[
            pltpu.SMEM(mirror_count.shape, jnp.int32), pltpu.VMEM(mirror_list.shape, jnp.int32),
            pltpu.VMEM((rows, cols), BF16), pltpu.SemaphoreType.DMA((3,)),
        ],
        vmem=58,
        flops=2 * mirrors * rows * cols, moved=600_000,
    )
    incoming = exchange(outgoing)
    tiles_late, feat_late, self_late, neigh_late, _ = lax.optimization_barrier(
        (tiles, features, w_self, w_neigh, outgoing)
    )
    high, low, degree, self_near, neigh_near = call(
        prep_body,
        (
            struct((rows, table_rows), BF16), struct((rows, table_rows), BF16),
            struct((rows, 128), F32), struct(w_self.shape, BF16), struct(w_neigh.shape, BF16),
        ),
        [
            ("s", tile_dst), ("s", tile_src), ("v", tiles_late), ("h", self_late),
            ("h", neigh_late),
        ],
        scratch=[pltpu.VMEM((rows, table_rows), F32), pltpu.SemaphoreType.DMA((2,))],
        flops=1_000_000, moved=3_000_000,
    )
    if split:
        feat_beside = swap(features, "dom", 1)
        incoming, feat_beside = lax.optimization_barrier((incoming, feat_beside))
    own, agg, *parts = call(
        functools.partial(aggregate_body, split),
        (struct((rows, cols), F32), block)
        + (
            (struct((rows, cols), F32), struct((2, rows, cols), BF16)) if split
            else (struct((reps, rows, cols), BF16),)
        ),
        [
            ("s", rep), ("v", feat_late), ("v", incoming), ("v", high), ("v", low),
            ("v", degree), ("v", self_near), ("v", neigh_near),
        ],
        scratch=[pltpu.VMEM((table_rows, cols), BF16)],
        flops=600_000_000, moved=3_000_000,
    )
    scale = float(rows * peers) ** (-0.5)
    if split:
        agg_beside = swap(agg, "dom", 1)
        grad_out, agg_beside = lax.optimization_barrier((grad_out, agg_beside))
        beside = swap(parts[1], "rep", 1)
        across = call(
            across_body, block, [("v", parts[0]), ("v", beside)], flops=100_000, moved=500_000
        )
        across = swap(across, "rep", 2)
        hidden, grad_pre, half = call(
            gate_blocks_body, (block, block, struct((rows, lanes), BF16)),
            [("s", dom), ("v", own), ("v", grad_out), ("v", beside), ("v", across)],
            flops=2_000_000, moved=1_300_000,
        )
        grad_full = gather_columns(grad_pre)
        halves = gather_columns(swap(half, "dom", 1))
    else:
        recv = lax.all_to_all(parts[0], "rep", split_axis=0, concat_axis=0, tiled=True)
        hidden, grad_pre = call(
            gate_body, (block, block),
            [("s", rep), ("v", recv), ("v", own), ("v", grad_out)],
            flops=2_000_000, moved=1_300_000,
        )
        grad_full = [lax.all_gather(grad_pre, "rep", axis=0, tiled=False)]
    total, mirror_grad = call(
        functools.partial(back_body, split), (struct((rows, cols), F32), mirror_out),
        [
            ("s", rep), ("v", high), ("v", low), ("v", degree), ("v", self_near),
            ("v", neigh_near),
        ] + [("v", got) for got in grad_full],
        flops=600_000_000, moved=3_000_000,
    )
    if split:
        piece = struct((2, rows, lanes), F32)
        mine, far, send = call(
            group_weight_body, (piece, piece, struct((2, 2, rows, lanes), BF16)),
            [
                ("s", dom), ("s", rep), ("v", features), ("v", feat_beside), ("v", agg),
                ("v", agg_beside),
            ] + [("v", got) for got in grad_full + halves],
            scratch=[pltpu.VMEM((2, reps, rows, lanes), BF16)],
            flops=600_000_000, moved=3_000_000,
        )
        piece = struct((2, rows, lanes), BF16)
        beside = swap(send, "dom", 2)
        far = call(across_body, piece, [("v", far), ("v", beside)], flops=100_000, moved=500_000)
        mine = call(
            functools.partial(join_body, scale), piece,
            [("v", mine), ("v", beside), ("v", swap(far, "dom", 4))],
            flops=200_000, moved=500_000,
        )
        pieces = gather_pieces(mine, peers)
    returned = exchange(mirror_grad)
    grad_features = call(
        scatter_body, block, [("v", onehot), ("v", total), ("v", returned)],
        flops=2 * mirrors * rows * cols, moved=700_000,
    )
    if split:
        out_self, out_neigh = call(
            place_body, (struct((rows, width), BF16), struct((rows, width), BF16)),
            [("s", dom)] + [("v", part) for part in pieces],
            scratch=[pltpu.SemaphoreType.DMA((2 * peers,))], moved=2_000_000, out="h",
        )
    else:
        piece = cols // peers
        partial = call(
            weight_body, struct((peers, 2 * piece, width), BF16),
            [("v", features), ("v", agg), ("v", grad_full[0])],
            flops=600_000_000, moved=2_000_000,
        )
        gathered = lax.all_to_all(partial, "dom", split_axis=0, concat_axis=0, tiled=True)
        mine_self, mine_neigh = call(
            functools.partial(sum_body, scale),
            (struct((piece, width), BF16), struct((piece, width), BF16)),
            [("v", gathered)], flops=1_000_000, moved=1_200_000,
        )
        out_self = lax.all_gather(mine_self, "dom", axis=0, tiled=True)
        out_neigh = lax.all_gather(mine_neigh, "dom", axis=0, tiled=True)
    return hidden, grad_features, out_self, out_neigh


def solution(mesh):
    in_specs = (
        P("dom", "rep"),
        P("rep", None),
        P("rep", None),
        P("dom", "rep"),
        P("dom", None),
        P("dom"),
        P("dom"),
        P("dom"),
        P("dom", None, None),
    )
    out_specs = (P("dom", "rep"), P("dom", "rep"), P("rep", None), P("rep", None))
    return jax.shard_map(local, mesh=mesh, in_specs=in_specs, out_specs=out_specs, check_vma=False)
```

```python
import functools

import jax
import jax.numpy as jnp
from jax import lax
from jax.experimental import pallas as pl
from jax.experimental.pallas import tpu as pltpu
from jax.sharding import PartitionSpec as P

F32 = jnp.float32
BF16 = jnp.bfloat16
SPECS = {
    "v": pl.BlockSpec(memory_space=pltpu.VMEM),
    "s": pl.BlockSpec(memory_space=pltpu.SMEM),
    "h": pl.BlockSpec(memory_space=pltpu.HBM),
}
ROWS = (((0,), (0,)), ((), ()))
COLS = (((1,), (1,)), ((), ()))


def call(body, outs, ins, scratch=(), flops=0, moved=0, vmem=16, out="v"):
    return pl.pallas_call(
        body,
        out_shape=outs,
        in_specs=[SPECS[spec] for spec, _ in ins],
        out_specs=jax.tree.map(lambda _: SPECS[out], outs),
        scratch_shapes=list(scratch),
        compiler_params=pltpu.CompilerParams(vmem_limit_bytes=vmem * 1024 * 1024),
        cost_estimate=pl.CostEstimate(flops=flops, bytes_accessed=moved, transcendentals=0),
    )(*[array for _, array in ins])


def dot(left, right, dims=(((1,), (0,)), ((), ()))):
    return lax.dot_general(left, right, dims, preferred_element_type=F32)


def block_rows(place, offset, size):
    return pl.ds(pl.multiple_of(lax.bitwise_xor(place, offset) * size, size), size)


def row_onehot(count_ref, lists, rows):
    peers, slots = lists.shape
    peer = lax.broadcasted_iota(jnp.int32, (peers, slots), 0)
    slot = lax.broadcasted_iota(jnp.int32, (peers, slots), 1)

    def fill(at, used):
        return jnp.where(peer == at, count_ref[at], used)

    used = jnp.zeros((peers, slots), jnp.int32)
    if peers <= 16:
        for at in range(peers):
            used = fill(at, used)
    else:
        used = lax.fori_loop(0, peers, fill, used)
    index = jnp.where(slot < used, lists, -1).astype(F32).astype(BF16)
    flat = peers * slots
    spread = (
        lax.broadcasted_iota(jnp.int32, (slots, flat), 0)
        == lax.broadcasted_iota(jnp.int32, (slots, flat), 1) % slots
    )
    wide = dot(index, spread.astype(F32).astype(BF16))
    mine = (
        lax.broadcasted_iota(jnp.int32, (peers, flat), 0)
        == lax.broadcasted_iota(jnp.int32, (peers, flat), 1) // slots
    )
    line = jnp.sum(jnp.where(mine, wide, 0.0), axis=0, keepdims=True).astype(jnp.int32)
    hit = lax.broadcasted_iota(jnp.int32, (rows, flat), 0) == line
    return hit.astype(F32).astype(BF16)


def pick_body(
    count_hbm, list_hbm, feat_hbm, onehot_ref, out_ref, count_ref, list_ref, feat_ref, sems
):
    copies = [
        pltpu.make_async_copy(src, dst, sems.at[k])
        for k, (src, dst) in enumerate(
            ((count_hbm, count_ref), (list_hbm, list_ref), (feat_hbm, feat_ref))
        )
    ]
    for copy in copies:
        copy.start()
    for copy in copies:
        copy.wait()
    onehot = row_onehot(count_ref, list_ref[...], feat_ref.shape[0])
    onehot_ref[...] = onehot
    out_ref[...] = dot(onehot, feat_ref[...], ROWS).astype(BF16)


def prep_body(
    dst_ref, src_ref, tiles_ref, self_hbm, neigh_hbm,
    high_ref, low_ref, deg_ref, self_ref, neigh_ref, adj_ref, sems,
):
    copies = [
        pltpu.make_async_copy(src, dst, sems.at[k])
        for k, (src, dst) in enumerate(((self_hbm, self_ref), (neigh_hbm, neigh_ref)))
    ]
    for copy in copies:
        copy.start()
    slots, side, _ = tiles_ref.shape
    adj_ref[...] = jnp.zeros(adj_ref.shape, F32)
    for t in range(slots):
        dst = pl.ds(pl.multiple_of(dst_ref[t] * side, side), side)
        src = pl.ds(pl.multiple_of(src_ref[t] * side, side), side)
        adj_ref[dst, src] += tiles_ref[t].astype(F32)
    adj = adj_ref[...]
    high = adj.astype(BF16)
    high_ref[...] = high
    low_ref[...] = (adj - high.astype(F32)).astype(BF16)
    degree = jnp.maximum(jnp.sum(adj, axis=1, keepdims=True), 1.0)
    deg_ref[...] = jnp.broadcast_to(degree, deg_ref.shape)
    for copy in copies:
        copy.wait()


def column_block(split, rep, c, reps, cols):
    other = lax.bitwise_xor(rep, c) if split else c
    return pl.ds(pl.multiple_of(other * cols, cols), cols)


def wide_degree(deg_ref, cols):
    return jnp.concatenate([deg_ref[...]] * (cols // deg_ref.shape[1]), axis=1)


def aggregate_body(
    split, rep_ref, feat_ref, inc_ref, high_ref, low_ref, deg_ref, self_ref, neigh_ref,
    own_ref, agg_ref, *refs,
):
    part_refs, table_ref = refs[:-1], refs[-1]
    rows, cols = feat_ref.shape
    feat = feat_ref[...]
    table_ref[:rows] = feat
    table_ref[rows:] = inc_ref[...]
    table = table_ref[...]
    summed = dot(high_ref[...], table) + dot(low_ref[...], table)
    agg = (summed / wide_degree(deg_ref, cols)).astype(BF16)
    agg_ref[...] = agg
    reps = self_ref.shape[1] // cols
    for c in reversed(range(reps)):
        at = column_block(split, rep_ref[0], c, reps, cols)
        value = dot(feat, self_ref[:, at]) + dot(agg, neigh_ref[:, at])
        if not split:
            part_refs[0][c] = value.astype(BF16)

            @pl.when(rep_ref[0] == c)
            def _():
                own_ref[...] = value
        elif c == 0:
            own_ref[...] = value
        elif c == 2:
            part_refs[0][...] = value
        else:
            part_refs[1][c // 2] = value.astype(BF16)


def finish_gate(pre, gout_ref, hid_ref, gpre_ref):
    gate = jax.nn.sigmoid(pre)
    hid_ref[...] = (pre * gate).astype(BF16)
    gpre_ref[...] = (gout_ref[...].astype(F32) * (gate + pre * gate * (1.0 - gate))).astype(BF16)


def gate_body(rep_ref, recv_ref, own_ref, gout_ref, hid_ref, gpre_ref):
    pre = own_ref[...]
    for c in range(recv_ref.shape[0]):
        pre = pre + jnp.where(rep_ref[0] == c, 0.0, recv_ref[c].astype(F32))
    finish_gate(pre, gout_ref, hid_ref, gpre_ref)


def across_body(mine_ref, beside_ref, out_ref):
    out_ref[...] = (mine_ref[...] + beside_ref[1].astype(F32)).astype(BF16)


def gate_blocks_body(dom_ref, own_ref, gout_ref, beside_ref, across_ref, hid_ref, gpre_ref, send_ref):
    pre = own_ref[...] + beside_ref[0].astype(F32) + across_ref[...].astype(F32)
    finish_gate(pre, gout_ref, hid_ref, gpre_ref)
    send_ref[...] = gpre_ref[:, block_rows(dom_ref[0] % 2, 1, send_ref.shape[1])]


def back_body(
    split, rep_ref, high_ref, low_ref, deg_ref, self_ref, neigh_ref, *refs,
):
    grads, (total_ref, mirror_ref) = refs[:-2], refs[-2:]
    rows, cols = total_ref.shape
    reps = self_ref.shape[1] // cols
    direct = jnp.zeros((rows, cols), F32)
    gagg = jnp.zeros((rows, cols), F32)
    for c in range(reps):
        grad = grads[c][...] if split else grads[0][c]
        at = column_block(split, rep_ref[0], c, reps, cols)
        gagg += dot(grad, neigh_ref[:, at], COLS)
        direct += dot(grad, self_ref[:, at], COLS)
    gagg = (gagg / wide_degree(deg_ref, cols)).astype(BF16)
    table = dot(high_ref[...], gagg, ROWS) + dot(low_ref[...], gagg, ROWS)
    total_ref[...] = direct + table[:rows]
    mirror_ref[...] = table[rows:].astype(BF16)


def weight_body(feat_ref, agg_ref, gfull_ref, out_ref):
    cols = feat_ref.shape[1]
    parts = out_ref.shape[0]
    piece = out_ref.shape[1] // 2
    for k, ref in enumerate((feat_ref, agg_ref)):
        left = ref[...]
        for c in range(gfull_ref.shape[0]):
            value = dot(left, gfull_ref[c], ROWS)
            out_ref[:, k * piece:(k + 1) * piece, c * cols:(c + 1) * cols] = value.reshape(
                parts, piece, cols
            ).astype(BF16)


def sum_body(scale, recv_ref, self_ref, neigh_ref):
    piece = self_ref.shape[0]
    for k, ref in enumerate((self_ref, neigh_ref)):
        total = jnp.zeros(ref.shape, F32)
        for d in range(recv_ref.shape[0]):
            total += recv_ref[d, k * piece:(k + 1) * piece].astype(F32)
        ref[...] = (total * scale).astype(BF16)


def group_weight_body(dom_ref, rep_ref, *refs):
    rows, (mine_ref, far_ref, send_ref, hold_ref) = refs[:4], refs[-4:]
    grads = refs[4:-4]
    count = len(grads) // 2
    lanes = mine_ref.shape[2]
    layer, side = dom_ref[0] // 2, dom_ref[0] % 2
    for c in range(count):
        at = lax.bitwise_xor(rep_ref[0], c)
        hold_ref[0, at] = grads[c][:, block_rows(side, 0, lanes)]
        hold_ref[1, at] = grads[count + c][...]
    for k in range(2):
        own, other = rows[2 * k][...], rows[2 * k + 1][...]
        for offset in range(count):
            at = lax.bitwise_xor(layer, offset)
            value = dot(own, hold_ref[0, at], ROWS) + dot(other, hold_ref[1, at], ROWS)
            if offset == 0:
                mine_ref[k] = value
            elif offset == 2:
                far_ref[k] = value
            else:
                send_ref[offset // 2, k] = value.astype(BF16)


def join_body(scale, mine_ref, next_ref, far_ref, out_ref):
    total = mine_ref[...] + next_ref[0].astype(F32) + far_ref[...].astype(F32)
    out_ref[...] = (total * scale).astype(BF16)


def place_body(dom_ref, *refs):
    blocks, outs, sems = refs[:-3], refs[-3:-1], refs[-1]
    copies = []
    lanes = blocks[0].shape[2]
    for offset, block in enumerate(blocks):
        at = block_rows(dom_ref[0], offset, lanes)
        for k, out_ref in enumerate(outs):
            copies.append(
                pltpu.make_async_copy(block.at[k], out_ref.at[:, at], sems.at[2 * offset + k])
            )
            copies[-1].start()
    for copy in copies:
        copy.wait()


def scatter_body(onehot_ref, total_ref, ret_ref, out_ref):
    out_ref[...] = (total_ref[...] + dot(onehot_ref[...], ret_ref[...])).astype(BF16)


def swap(array, axis, offset):
    return lax.ppermute(array, axis, [(i, i ^ offset) for i in range(lax.axis_size(axis))])


def gather_columns(array):
    across = swap(array, "rep", 2)
    return [array, swap(array, "rep", 1), across, swap(across, "rep", 1)]


def gather_pieces(array, peers):
    out = {0: array, 4: swap(array, "dom", 4), 2: swap(array, "dom", 2)}
    out[1] = swap(array, "dom", 1)
    out[3] = swap(out[2], "dom", 1)
    out[4], out[1], out[3] = lax.optimization_barrier((out[4], out[1], out[3]))
    out[6] = swap(out[4], "dom", 2)
    for offset in range(4, peers, 2):
        out[offset + 1] = swap(out[offset], "dom", 1)
    return [out[offset] for offset in range(peers)]


def local(
    features, w_self, w_neigh, grad_out, mirror_list, mirror_count, tile_dst, tile_src, tiles
):
    rows, cols = features.shape
    width = w_self.shape[1]
    peers, slots = mirror_list.shape
    mirrors = peers * slots
    table_rows = rows + mirrors
    reps = width // cols
    struct = jax.ShapeDtypeStruct
    block = struct((rows, cols), BF16)
    rep = lax.axis_index("rep").astype(jnp.int32).reshape(1)
    dom = lax.axis_index("dom").astype(jnp.int32).reshape(1)
    lanes = width // peers
    split = peers == 8 and reps == 4 and slots % 16 == 0 and lanes % 128 == 0
    mirror_out = struct((mirrors, cols), BF16)

    def exchange(array):
        return lax.all_to_all(
            array.reshape(peers, slots, cols), "dom", split_axis=0, concat_axis=0, tiled=True
        ).reshape(mirrors, cols)

    onehot, outgoing = call(
        pick_body, (struct((rows, mirrors), BF16), mirror_out),
        [("h", mirror_count), ("h", mirror_list), ("h", features)],
        scratch=[
            pltpu.SMEM(mirror_count.shape, jnp.int32), pltpu.VMEM(mirror_list.shape, jnp.int32),
            pltpu.VMEM((rows, cols), BF16), pltpu.SemaphoreType.DMA((3,)),
        ],
        vmem=58,
        flops=2 * mirrors * rows * cols, moved=600_000,
    )
    incoming = exchange(outgoing)
    tiles_late, feat_late, self_late, neigh_late, _ = lax.optimization_barrier(
        (tiles, features, w_self, w_neigh, outgoing)
    )
    high, low, degree, self_near, neigh_near = call(
        prep_body,
        (
            struct((rows, table_rows), BF16), struct((rows, table_rows), BF16),
            struct((rows, 128), F32), struct(w_self.shape, BF16), struct(w_neigh.shape, BF16),
        ),
        [
            ("s", tile_dst), ("s", tile_src), ("v", tiles_late), ("h", self_late),
            ("h", neigh_late),
        ],
        scratch=[pltpu.VMEM((rows, table_rows), F32), pltpu.SemaphoreType.DMA((2,))],
        flops=1_000_000, moved=3_000_000,
    )
    if split:
        feat_beside = swap(features, "dom", 1)
        incoming, feat_beside = lax.optimization_barrier((incoming, feat_beside))
    own, agg, *parts = call(
        functools.partial(aggregate_body, split),
        (struct((rows, cols), F32), block)
        + (
            (struct((rows, cols), F32), struct((2, rows, cols), BF16)) if split
            else (struct((reps, rows, cols), BF16),)
        ),
        [
            ("s", rep), ("v", feat_late), ("v", incoming), ("v", high), ("v", low),
            ("v", degree), ("v", self_near), ("v", neigh_near),
        ],
        scratch=[pltpu.VMEM((table_rows, cols), BF16)],
        flops=600_000_000, moved=3_000_000,
    )
    scale = float(rows * peers) ** (-0.5)
    if split:
        agg_beside = swap(agg, "dom", 1)
        grad_out, agg_beside = lax.optimization_barrier((grad_out, agg_beside))
        beside = swap(parts[1], "rep", 1)
        across = call(
            across_body, block, [("v", parts[0]), ("v", beside)], flops=100_000, moved=500_000
        )
        across = swap(across, "rep", 2)
        hidden, grad_pre, half = call(
            gate_blocks_body, (block, block, struct((rows, lanes), BF16)),
            [("s", dom), ("v", own), ("v", grad_out), ("v", beside), ("v", across)],
            flops=2_000_000, moved=1_300_000,
        )
        grad_full = gather_columns(grad_pre)
        halves = gather_columns(swap(half, "dom", 1))
    else:
        recv = lax.all_to_all(parts[0], "rep", split_axis=0, concat_axis=0, tiled=True)
        hidden, grad_pre = call(
            gate_body, (block, block),
            [("s", rep), ("v", recv), ("v", own), ("v", grad_out)],
            flops=2_000_000, moved=1_300_000,
        )
        grad_full = [lax.all_gather(grad_pre, "rep", axis=0, tiled=False)]
    total, mirror_grad = call(
        functools.partial(back_body, split), (struct((rows, cols), F32), mirror_out),
        [
            ("s", rep), ("v", high), ("v", low), ("v", degree), ("v", self_near),
            ("v", neigh_near),
        ] + [("v", got) for got in grad_full],
        flops=600_000_000, moved=3_000_000,
    )
    if split:
        piece = struct((2, rows, lanes), F32)
        mine, far, send = call(
            group_weight_body, (piece, piece, struct((2, 2, rows, lanes), BF16)),
            [
                ("s", dom), ("s", rep), ("v", features), ("v", feat_beside), ("v", agg),
                ("v", agg_beside),
            ] + [("v", got) for got in grad_full + halves],
            scratch=[pltpu.VMEM((2, reps, rows, lanes), BF16)],
            flops=600_000_000, moved=3_000_000,
        )
        piece = struct((2, rows, lanes), BF16)
        beside = swap(send, "dom", 2)
        beside, mirror_grad = lax.optimization_barrier((beside, mirror_grad))
        returned = exchange(mirror_grad)
        far = call(across_body, piece, [("v", far), ("v", beside)], flops=100_000, moved=500_000)
        far, returned = lax.optimization_barrier((swap(far, "dom", 4), returned))
        mine = call(
            functools.partial(join_body, scale), piece,
            [("v", mine), ("v", beside), ("v", far)],
            flops=200_000, moved=500_000,
        )
        pieces = gather_pieces(mine, peers)
    else:
        returned = exchange(mirror_grad)
    grad_features = call(
        scatter_body, block, [("v", onehot), ("v", total), ("v", returned)],
        flops=2 * mirrors * rows * cols, moved=700_000,
    )
    if split:
        out_self, out_neigh = call(
            place_body, (struct((rows, width), BF16), struct((rows, width), BF16)),
            [("s", dom)] + [("v", part) for part in pieces],
            scratch=[pltpu.SemaphoreType.DMA((2 * peers,))], moved=2_000_000, out="h",
        )
    else:
        piece = cols // peers
        partial = call(
            weight_body, struct((peers, 2 * piece, width), BF16),
            [("v", features), ("v", agg), ("v", grad_full[0])],
            flops=600_000_000, moved=2_000_000,
        )
        gathered = lax.all_to_all(partial, "dom", split_axis=0, concat_axis=0, tiled=True)
        mine_self, mine_neigh = call(
            functools.partial(sum_body, scale),
            (struct((piece, width), BF16), struct((piece, width), BF16)),
            [("v", gathered)], flops=1_000_000, moved=1_200_000,
        )
        out_self = lax.all_gather(mine_self, "dom", axis=0, tiled=True)
        out_neigh = lax.all_gather(mine_neigh, "dom", axis=0, tiled=True)
    return hidden, grad_features, out_self, out_neigh


def solution(mesh):
    in_specs = (
        P("dom", "rep"),
        P("rep", None),
        P("rep", None),
        P("dom", "rep"),
        P("dom", None),
        P("dom"),
        P("dom"),
        P("dom"),
        P("dom", None, None),
    )
    out_specs = (P("dom", "rep"), P("dom", "rep"), P("rep", None), P("rep", None))
    return jax.shard_map(local, mesh=mesh, in_specs=in_specs, out_specs=out_specs, check_vma=False)
```

```python
import functools

import jax
import jax.numpy as jnp
from jax import lax
from jax.experimental import pallas as pl
from jax.experimental.pallas import tpu as pltpu
from jax.sharding import PartitionSpec as P

F32 = jnp.float32
BF16 = jnp.bfloat16
SPECS = {
    "v": pl.BlockSpec(memory_space=pltpu.VMEM),
    "s": pl.BlockSpec(memory_space=pltpu.SMEM),
    "h": pl.BlockSpec(memory_space=pltpu.HBM),
}
ROWS = (((0,), (0,)), ((), ()))
COLS = (((1,), (1,)), ((), ()))


def call(body, outs, ins, scratch=(), flops=0, moved=0, vmem=16, out="v"):
    return pl.pallas_call(
        body,
        out_shape=outs,
        in_specs=[SPECS[spec] for spec, _ in ins],
        out_specs=jax.tree.map(lambda _: SPECS[out], outs),
        scratch_shapes=list(scratch),
        compiler_params=pltpu.CompilerParams(vmem_limit_bytes=vmem * 1024 * 1024),
        cost_estimate=pl.CostEstimate(flops=flops, bytes_accessed=moved, transcendentals=0),
    )(*[array for _, array in ins])


def dot(left, right, dims=(((1,), (0,)), ((), ()))):
    return lax.dot_general(left, right, dims, preferred_element_type=F32)


def block_rows(place, offset, size):
    return pl.ds(pl.multiple_of(lax.bitwise_xor(place, offset) * size, size), size)


def row_onehot(count_ref, lists, rows):
    peers, slots = lists.shape
    peer = lax.broadcasted_iota(jnp.int32, (peers, slots), 0)
    slot = lax.broadcasted_iota(jnp.int32, (peers, slots), 1)

    def fill(at, used):
        return jnp.where(peer == at, count_ref[at], used)

    used = jnp.zeros((peers, slots), jnp.int32)
    if peers <= 16:
        for at in range(peers):
            used = fill(at, used)
    else:
        used = lax.fori_loop(0, peers, fill, used)
    index = jnp.where(slot < used, lists, -1).astype(F32).astype(BF16)
    flat = peers * slots
    spread = (
        lax.broadcasted_iota(jnp.int32, (slots, flat), 0)
        == lax.broadcasted_iota(jnp.int32, (slots, flat), 1) % slots
    )
    wide = dot(index, spread.astype(F32).astype(BF16))
    mine = (
        lax.broadcasted_iota(jnp.int32, (peers, flat), 0)
        == lax.broadcasted_iota(jnp.int32, (peers, flat), 1) // slots
    )
    line = jnp.sum(jnp.where(mine, wide, 0.0), axis=0, keepdims=True).astype(jnp.int32)
    hit = lax.broadcasted_iota(jnp.int32, (rows, flat), 0) == line
    return hit.astype(F32).astype(BF16)


def pick_body(
    count_hbm, list_hbm, feat_hbm, onehot_ref, out_ref, count_ref, list_ref, feat_ref, sems
):
    copies = [
        pltpu.make_async_copy(src, dst, sems.at[k])
        for k, (src, dst) in enumerate(
            ((count_hbm, count_ref), (list_hbm, list_ref), (feat_hbm, feat_ref))
        )
    ]
    for copy in copies:
        copy.start()
    for copy in copies:
        copy.wait()
    onehot = row_onehot(count_ref, list_ref[...], feat_ref.shape[0])
    onehot_ref[...] = onehot
    out_ref[...] = dot(onehot, feat_ref[...], ROWS).astype(BF16)


def prep_body(
    dst_ref, src_ref, tiles_ref, self_hbm, neigh_hbm,
    high_ref, low_ref, deg_ref, self_ref, neigh_ref, adj_ref, sems,
):
    copies = [
        pltpu.make_async_copy(src, dst, sems.at[k])
        for k, (src, dst) in enumerate(((self_hbm, self_ref), (neigh_hbm, neigh_ref)))
    ]
    for copy in copies:
        copy.start()
    slots, side, _ = tiles_ref.shape
    adj_ref[...] = jnp.zeros(adj_ref.shape, F32)
    for t in range(slots):
        dst = pl.ds(pl.multiple_of(dst_ref[t] * side, side), side)
        src = pl.ds(pl.multiple_of(src_ref[t] * side, side), side)
        adj_ref[dst, src] += tiles_ref[t].astype(F32)
    adj = adj_ref[...]
    high = adj.astype(BF16)
    high_ref[...] = high
    low_ref[...] = (adj - high.astype(F32)).astype(BF16)
    degree = jnp.maximum(jnp.sum(adj, axis=1, keepdims=True), 1.0)
    deg_ref[...] = jnp.broadcast_to(degree, deg_ref.shape)
    for copy in copies:
        copy.wait()


def column_block(split, rep, c, reps, cols):
    other = lax.bitwise_xor(rep, c) if split else c
    return pl.ds(pl.multiple_of(other * cols, cols), cols)


def wide_degree(deg_ref, cols):
    return jnp.concatenate([deg_ref[...]] * (cols // deg_ref.shape[1]), axis=1)


def aggregate_body(
    split, rep_ref, feat_ref, inc_ref, high_ref, low_ref, deg_ref, self_ref, neigh_ref,
    own_ref, agg_ref, *refs,
):
    part_refs, table_ref = refs[:-1], refs[-1]
    rows, cols = feat_ref.shape
    feat = feat_ref[...]
    table_ref[:rows] = feat
    table_ref[rows:] = inc_ref[...]
    table = table_ref[...]
    summed = dot(high_ref[...], table) + dot(low_ref[...], table)
    agg = (summed / wide_degree(deg_ref, cols)).astype(BF16)
    agg_ref[...] = agg
    reps = self_ref.shape[1] // cols
    for c in reversed(range(reps)):
        at = column_block(split, rep_ref[0], c, reps, cols)
        value = dot(feat, self_ref[:, at]) + dot(agg, neigh_ref[:, at])
        if not split:
            part_refs[0][c] = value.astype(BF16)

            @pl.when(rep_ref[0] == c)
            def _():
                own_ref[...] = value
        elif c == 0:
            own_ref[...] = value
        elif c == 2:
            part_refs[0][...] = value
        else:
            part_refs[1][c // 2] = value.astype(BF16)


def finish_gate(pre, gout_ref, hid_ref, gpre_ref):
    gate = jax.nn.sigmoid(pre)
    hid_ref[...] = (pre * gate).astype(BF16)
    gpre_ref[...] = (gout_ref[...].astype(F32) * (gate + pre * gate * (1.0 - gate))).astype(BF16)


def gate_body(rep_ref, recv_ref, own_ref, gout_ref, hid_ref, gpre_ref):
    pre = own_ref[...]
    for c in range(recv_ref.shape[0]):
        pre = pre + jnp.where(rep_ref[0] == c, 0.0, recv_ref[c].astype(F32))
    finish_gate(pre, gout_ref, hid_ref, gpre_ref)


def across_body(mine_ref, beside_ref, out_ref):
    out_ref[...] = (mine_ref[...] + beside_ref[1].astype(F32)).astype(BF16)


def gate_blocks_body(dom_ref, own_ref, gout_ref, beside_ref, across_ref, hid_ref, gpre_ref, send_ref):
    pre = own_ref[...] + beside_ref[0].astype(F32) + across_ref[...].astype(F32)
    finish_gate(pre, gout_ref, hid_ref, gpre_ref)
    send_ref[...] = gpre_ref[:, block_rows(dom_ref[0] % 2, 1, send_ref.shape[1])]


def back_body(
    split, rep_ref, high_ref, low_ref, deg_ref, self_ref, neigh_ref, *refs,
):
    grads, (total_ref, mirror_ref) = refs[:-2], refs[-2:]
    rows, cols = total_ref.shape
    reps = self_ref.shape[1] // cols
    direct = jnp.zeros((rows, cols), F32)
    gagg = jnp.zeros((rows, cols), F32)
    for c in range(reps):
        grad = grads[c][...] if split else grads[0][c]
        at = column_block(split, rep_ref[0], c, reps, cols)
        gagg += dot(grad, neigh_ref[:, at], COLS)
        direct += dot(grad, self_ref[:, at], COLS)
    gagg = (gagg / wide_degree(deg_ref, cols)).astype(BF16)
    table = dot(high_ref[...], gagg, ROWS) + dot(low_ref[...], gagg, ROWS)
    total_ref[...] = direct + table[:rows]
    mirror_ref[...] = table[rows:].astype(BF16)


def weight_body(feat_ref, agg_ref, gfull_ref, out_ref):
    cols = feat_ref.shape[1]
    parts = out_ref.shape[0]
    piece = out_ref.shape[1] // 2
    for k, ref in enumerate((feat_ref, agg_ref)):
        left = ref[...]
        for c in range(gfull_ref.shape[0]):
            value = dot(left, gfull_ref[c], ROWS)
            out_ref[:, k * piece:(k + 1) * piece, c * cols:(c + 1) * cols] = value.reshape(
                parts, piece, cols
            ).astype(BF16)


def sum_body(scale, recv_ref, self_ref, neigh_ref):
    piece = self_ref.shape[0]
    for k, ref in enumerate((self_ref, neigh_ref)):
        total = jnp.zeros(ref.shape, F32)
        for d in range(recv_ref.shape[0]):
            total += recv_ref[d, k * piece:(k + 1) * piece].astype(F32)
        ref[...] = (total * scale).astype(BF16)


def group_weight_body(dom_ref, rep_ref, *refs):
    rows, (mine_ref, far_ref, send_ref, hold_ref) = refs[:4], refs[-4:]
    grads = refs[4:-4]
    count = len(grads) // 2
    lanes = mine_ref.shape[2]
    layer, side = dom_ref[0] // 2, dom_ref[0] % 2
    for c in range(count):
        at = lax.bitwise_xor(rep_ref[0], c)
        hold_ref[0, at] = grads[c][:, block_rows(side, 0, lanes)]
        hold_ref[1, at] = grads[count + c][...]
    for k in range(2):
        own, other = rows[2 * k][...], rows[2 * k + 1][...]
        for offset in range(count):
            at = lax.bitwise_xor(layer, offset)
            value = dot(own, hold_ref[0, at], ROWS) + dot(other, hold_ref[1, at], ROWS)
            if offset == 0:
                mine_ref[k] = value
            elif offset == 2:
                far_ref[k] = value
            else:
                send_ref[offset // 2, k] = value.astype(BF16)


def join_body(scale, mine_ref, next_ref, far_ref, out_ref):
    total = mine_ref[...] + next_ref[0].astype(F32) + far_ref[...].astype(F32)
    out_ref[...] = (total * scale).astype(BF16)


def place_body(dom_ref, *refs):
    blocks, outs, sems = refs[:-3], refs[-3:-1], refs[-1]
    copies = []
    lanes = blocks[0].shape[2]
    for offset, block in enumerate(blocks):
        at = block_rows(dom_ref[0], offset, lanes)
        for k, out_ref in enumerate(outs):
            copies.append(
                pltpu.make_async_copy(block.at[k], out_ref.at[:, at], sems.at[2 * offset + k])
            )
            copies[-1].start()
    for copy in copies:
        copy.wait()


def scatter_body(onehot_ref, total_ref, ret_ref, out_ref):
    out_ref[...] = (total_ref[...] + dot(onehot_ref[...], ret_ref[...])).astype(BF16)


def swap(array, axis, offset):
    return lax.ppermute(array, axis, [(i, i ^ offset) for i in range(lax.axis_size(axis))])


def gather_columns(array):
    across = swap(array, "rep", 2)
    return [array, swap(array, "rep", 1), across, swap(across, "rep", 1)]


def gather_pieces(array, peers):
    out = {0: array, 4: swap(array, "dom", 4), 2: swap(array, "dom", 2)}
    out[1] = swap(array, "dom", 1)
    out[4], out[1] = lax.optimization_barrier((out[4], out[1]))
    out[6] = swap(out[4], "dom", 2)
    for offset in range(2, peers, 2):
        out[offset + 1] = swap(out[offset], "dom", 1)
    return [out[offset] for offset in range(peers)]


def local(
    features, w_self, w_neigh, grad_out, mirror_list, mirror_count, tile_dst, tile_src, tiles
):
    rows, cols = features.shape
    width = w_self.shape[1]
    peers, slots = mirror_list.shape
    mirrors = peers * slots
    table_rows = rows + mirrors
    reps = width // cols
    struct = jax.ShapeDtypeStruct
    block = struct((rows, cols), BF16)
    rep = lax.axis_index("rep").astype(jnp.int32).reshape(1)
    dom = lax.axis_index("dom").astype(jnp.int32).reshape(1)
    lanes = width // peers
    split = peers == 8 and reps == 4 and slots % 16 == 0 and lanes % 128 == 0
    mirror_out = struct((mirrors, cols), BF16)

    def exchange(array):
        return lax.all_to_all(
            array.reshape(peers, slots, cols), "dom", split_axis=0, concat_axis=0, tiled=True
        ).reshape(mirrors, cols)

    onehot, outgoing = call(
        pick_body, (struct((rows, mirrors), BF16), mirror_out),
        [("h", mirror_count), ("h", mirror_list), ("h", features)],
        scratch=[
            pltpu.SMEM(mirror_count.shape, jnp.int32), pltpu.VMEM(mirror_list.shape, jnp.int32),
            pltpu.VMEM((rows, cols), BF16), pltpu.SemaphoreType.DMA((3,)),
        ],
        vmem=58,
        flops=2 * mirrors * rows * cols, moved=600_000,
    )
    incoming = exchange(outgoing)
    tiles_late, feat_late, self_late, neigh_late, _ = lax.optimization_barrier(
        (tiles, features, w_self, w_neigh, outgoing)
    )
    high, low, degree, self_near, neigh_near = call(
        prep_body,
        (
            struct((rows, table_rows), BF16), struct((rows, table_rows), BF16),
            struct((rows, 128), F32), struct(w_self.shape, BF16), struct(w_neigh.shape, BF16),
        ),
        [
            ("s", tile_dst), ("s", tile_src), ("v", tiles_late), ("h", self_late),
            ("h", neigh_late),
        ],
        scratch=[pltpu.VMEM((rows, table_rows), F32), pltpu.SemaphoreType.DMA((2,))],
        flops=1_000_000, moved=3_000_000,
    )
    if split:
        feat_beside = swap(features, "dom", 1)
        incoming, feat_beside = lax.optimization_barrier((incoming, feat_beside))
    own, agg, *parts = call(
        functools.partial(aggregate_body, split),
        (struct((rows, cols), F32), block)
        + (
            (struct((rows, cols), F32), struct((2, rows, cols), BF16)) if split
            else (struct((reps, rows, cols), BF16),)
        ),
        [
            ("s", rep), ("v", feat_late), ("v", incoming), ("v", high), ("v", low),
            ("v", degree), ("v", self_near), ("v", neigh_near),
        ],
        scratch=[pltpu.VMEM((table_rows, cols), BF16)],
        flops=600_000_000, moved=3_000_000,
    )
    scale = float(rows * peers) ** (-0.5)
    if split:
        agg_beside = swap(agg, "dom", 1)
        grad_out, agg_beside = lax.optimization_barrier((grad_out, agg_beside))
        beside = swap(parts[1], "rep", 1)
        across = call(
            across_body, block, [("v", parts[0]), ("v", beside)], flops=100_000, moved=500_000
        )
        across = swap(across, "rep", 2)
        hidden, grad_pre, half = call(
            gate_blocks_body, (block, block, struct((rows, lanes), BF16)),
            [("s", dom), ("v", own), ("v", grad_out), ("v", beside), ("v", across)],
            flops=2_000_000, moved=1_300_000,
        )
        grad_full = gather_columns(grad_pre)
        halves = gather_columns(swap(half, "dom", 1))
    else:
        recv = lax.all_to_all(parts[0], "rep", split_axis=0, concat_axis=0, tiled=True)
        hidden, grad_pre = call(
            gate_body, (block, block),
            [("s", rep), ("v", recv), ("v", own), ("v", grad_out)],
            flops=2_000_000, moved=1_300_000,
        )
        grad_full = [lax.all_gather(grad_pre, "rep", axis=0, tiled=False)]
    total, mirror_grad = call(
        functools.partial(back_body, split), (struct((rows, cols), F32), mirror_out),
        [
            ("s", rep), ("v", high), ("v", low), ("v", degree), ("v", self_near),
            ("v", neigh_near),
        ] + [("v", got) for got in grad_full],
        flops=600_000_000, moved=3_000_000,
    )
    if split:
        piece = struct((2, rows, lanes), F32)
        mine, far, send = call(
            group_weight_body, (piece, piece, struct((2, 2, rows, lanes), BF16)),
            [
                ("s", dom), ("s", rep), ("v", features), ("v", feat_beside), ("v", agg),
                ("v", agg_beside),
            ] + [("v", got) for got in grad_full + halves],
            scratch=[pltpu.VMEM((2, reps, rows, lanes), BF16)],
            flops=600_000_000, moved=3_000_000,
        )
        piece = struct((2, rows, lanes), BF16)
        beside = swap(send, "dom", 2)
        returned = exchange(mirror_grad)
        far = call(across_body, piece, [("v", far), ("v", beside)], flops=100_000, moved=500_000)
        far, returned = lax.optimization_barrier((swap(far, "dom", 4), returned))
        mine = call(
            functools.partial(join_body, scale), piece,
            [("v", mine), ("v", beside), ("v", far)],
            flops=200_000, moved=500_000,
        )
        pieces = gather_pieces(mine, peers)
    else:
        returned = exchange(mirror_grad)
    grad_features = call(
        scatter_body, block, [("v", onehot), ("v", total), ("v", returned)],
        flops=2 * mirrors * rows * cols, moved=700_000,
    )
    if split:
        out_self, out_neigh = call(
            place_body, (struct((rows, width), BF16), struct((rows, width), BF16)),
            [("s", dom)] + [("v", part) for part in pieces],
            scratch=[pltpu.SemaphoreType.DMA((2 * peers,))], moved=2_000_000, out="h",
        )
    else:
        piece = cols // peers
        partial = call(
            weight_body, struct((peers, 2 * piece, width), BF16),
            [("v", features), ("v", agg), ("v", grad_full[0])],
            flops=600_000_000, moved=2_000_000,
        )
        gathered = lax.all_to_all(partial, "dom", split_axis=0, concat_axis=0, tiled=True)
        mine_self, mine_neigh = call(
            functools.partial(sum_body, scale),
            (struct((piece, width), BF16), struct((piece, width), BF16)),
            [("v", gathered)], flops=1_000_000, moved=1_200_000,
        )
        out_self = lax.all_gather(mine_self, "dom", axis=0, tiled=True)
        out_neigh = lax.all_gather(mine_neigh, "dom", axis=0, tiled=True)
    return hidden, grad_features, out_self, out_neigh


def solution(mesh):
    in_specs = (
        P("dom", "rep"),
        P("rep", None),
        P("rep", None),
        P("dom", "rep"),
        P("dom", None),
        P("dom"),
        P("dom"),
        P("dom"),
        P("dom", None, None),
    )
    out_specs = (P("dom", "rep"), P("dom", "rep"), P("rep", None), P("rep", None))
    return jax.shard_map(local, mesh=mesh, in_specs=in_specs, out_specs=out_specs, check_vma=False)
```

```python
import functools

import jax
import jax.numpy as jnp
from jax import lax
from jax.experimental import pallas as pl
from jax.experimental.pallas import tpu as pltpu
from jax.sharding import PartitionSpec as P

F32 = jnp.float32
BF16 = jnp.bfloat16
SPECS = {
    "v": pl.BlockSpec(memory_space=pltpu.VMEM),
    "s": pl.BlockSpec(memory_space=pltpu.SMEM),
    "h": pl.BlockSpec(memory_space=pltpu.HBM),
}
ROWS = (((0,), (0,)), ((), ()))
COLS = (((1,), (1,)), ((), ()))


def call(body, outs, ins, scratch=(), flops=0, moved=0, vmem=16, out="v"):
    return pl.pallas_call(
        body,
        out_shape=outs,
        in_specs=[SPECS[spec] for spec, _ in ins],
        out_specs=jax.tree.map(lambda _: SPECS[out], outs),
        scratch_shapes=list(scratch),
        compiler_params=pltpu.CompilerParams(vmem_limit_bytes=vmem * 1024 * 1024),
        cost_estimate=pl.CostEstimate(flops=flops, bytes_accessed=moved, transcendentals=0),
    )(*[array for _, array in ins])


def dot(left, right, dims=(((1,), (0,)), ((), ()))):
    return lax.dot_general(left, right, dims, preferred_element_type=F32)


def block_rows(place, offset, size):
    return pl.ds(pl.multiple_of(lax.bitwise_xor(place, offset) * size, size), size)


def row_onehot(count_ref, lists, rows):
    peers, slots = lists.shape
    peer = lax.broadcasted_iota(jnp.int32, (peers, slots), 0)
    slot = lax.broadcasted_iota(jnp.int32, (peers, slots), 1)

    def fill(at, used):
        return jnp.where(peer == at, count_ref[at], used)

    used = jnp.zeros((peers, slots), jnp.int32)
    if peers <= 16:
        for at in range(peers):
            used = fill(at, used)
    else:
        used = lax.fori_loop(0, peers, fill, used)
    index = jnp.where(slot < used, lists, -1).astype(F32).astype(BF16)
    flat = peers * slots
    spread = (
        lax.broadcasted_iota(jnp.int32, (slots, flat), 0)
        == lax.broadcasted_iota(jnp.int32, (slots, flat), 1) % slots
    )
    wide = dot(index, spread.astype(F32).astype(BF16))
    mine = (
        lax.broadcasted_iota(jnp.int32, (peers, flat), 0)
        == lax.broadcasted_iota(jnp.int32, (peers, flat), 1) // slots
    )
    line = jnp.sum(jnp.where(mine, wide, 0.0), axis=0, keepdims=True).astype(jnp.int32)
    hit = lax.broadcasted_iota(jnp.int32, (rows, flat), 0) == line
    return hit.astype(F32).astype(BF16)


def pick_body(
    count_hbm, list_hbm, feat_hbm, onehot_ref, out_ref, count_ref, list_ref, feat_ref, sems
):
    copies = [
        pltpu.make_async_copy(src, dst, sems.at[k])
        for k, (src, dst) in enumerate(
            ((count_hbm, count_ref), (list_hbm, list_ref), (feat_hbm, feat_ref))
        )
    ]
    for copy in copies:
        copy.start()
    for copy in copies:
        copy.wait()
    onehot = row_onehot(count_ref, list_ref[...], feat_ref.shape[0])
    onehot_ref[...] = onehot
    out_ref[...] = dot(onehot, feat_ref[...], ROWS).astype(BF16)


def prep_body(
    dst_ref, src_ref, tiles_ref, self_hbm, neigh_hbm,
    high_ref, low_ref, deg_ref, self_ref, neigh_ref, adj_ref, sems,
):
    copies = [
        pltpu.make_async_copy(src, dst, sems.at[k])
        for k, (src, dst) in enumerate(((self_hbm, self_ref), (neigh_hbm, neigh_ref)))
    ]
    for copy in copies:
        copy.start()
    slots, side, _ = tiles_ref.shape
    adj_ref[...] = jnp.zeros(adj_ref.shape, F32)
    for t in range(slots):
        dst = pl.ds(pl.multiple_of(dst_ref[t] * side, side), side)
        src = pl.ds(pl.multiple_of(src_ref[t] * side, side), side)
        adj_ref[dst, src] += tiles_ref[t].astype(F32)
    adj = adj_ref[...]
    high = adj.astype(BF16)
    high_ref[...] = high
    low_ref[...] = (adj - high.astype(F32)).astype(BF16)
    degree = jnp.maximum(jnp.sum(adj, axis=1, keepdims=True), 1.0)
    deg_ref[...] = jnp.broadcast_to(degree, deg_ref.shape)
    for copy in copies:
        copy.wait()


def column_block(split, rep, c, reps, cols):
    other = lax.bitwise_xor(rep, c) if split else c
    return pl.ds(pl.multiple_of(other * cols, cols), cols)


def wide_degree(deg_ref, cols):
    return jnp.concatenate([deg_ref[...]] * (cols // deg_ref.shape[1]), axis=1)


def aggregate_body(
    split, rep_ref, feat_ref, inc_ref, high_ref, low_ref, deg_ref, self_ref, neigh_ref,
    own_ref, agg_ref, *refs,
):
    part_refs, table_ref = refs[:-1], refs[-1]
    rows, cols = feat_ref.shape
    feat = feat_ref[...]
    table_ref[:rows] = feat
    table_ref[rows:] = inc_ref[...]
    table = table_ref[...]
    summed = dot(high_ref[...], table) + dot(low_ref[...], table)
    agg = (summed / wide_degree(deg_ref, cols)).astype(BF16)
    agg_ref[...] = agg
    reps = self_ref.shape[1] // cols
    for c in reversed(range(reps)):
        at = column_block(split, rep_ref[0], c, reps, cols)
        value = dot(feat, self_ref[:, at]) + dot(agg, neigh_ref[:, at])
        if not split:
            part_refs[0][c] = value.astype(BF16)

            @pl.when(rep_ref[0] == c)
            def _():
                own_ref[...] = value
        elif c == 0:
            own_ref[...] = value
        elif c == 2:
            part_refs[0][...] = value
        else:
            part_refs[1][c // 2] = value.astype(BF16)


def finish_gate(pre, gout_ref, hid_ref, gpre_ref):
    gate = jax.nn.sigmoid(pre)
    hid_ref[...] = (pre * gate).astype(BF16)
    gpre_ref[...] = (gout_ref[...].astype(F32) * (gate + pre * gate * (1.0 - gate))).astype(BF16)


def gate_body(rep_ref, recv_ref, own_ref, gout_ref, hid_ref, gpre_ref):
    pre = own_ref[...]
    for c in range(recv_ref.shape[0]):
        pre = pre + jnp.where(rep_ref[0] == c, 0.0, recv_ref[c].astype(F32))
    finish_gate(pre, gout_ref, hid_ref, gpre_ref)


def across_body(mine_ref, beside_ref, out_ref):
    out_ref[...] = (mine_ref[...] + beside_ref[1].astype(F32)).astype(BF16)


def gate_blocks_body(dom_ref, own_ref, gout_ref, beside_ref, across_ref, hid_ref, gpre_ref, send_ref):
    pre = own_ref[...] + beside_ref[0].astype(F32) + across_ref[...].astype(F32)
    finish_gate(pre, gout_ref, hid_ref, gpre_ref)
    send_ref[...] = gpre_ref[:, block_rows(dom_ref[0] % 2, 1, send_ref.shape[1])]


def back_body(
    split, rep_ref, high_ref, low_ref, deg_ref, self_ref, neigh_ref, *refs,
):
    grads, (total_ref, mirror_ref) = refs[:-2], refs[-2:]
    rows, cols = total_ref.shape
    reps = self_ref.shape[1] // cols
    direct = jnp.zeros((rows, cols), F32)
    gagg = jnp.zeros((rows, cols), F32)
    for c in range(reps):
        grad = grads[c][...] if split else grads[0][c]
        at = column_block(split, rep_ref[0], c, reps, cols)
        gagg += dot(grad, neigh_ref[:, at], COLS)
        direct += dot(grad, self_ref[:, at], COLS)
    gagg = (gagg / wide_degree(deg_ref, cols)).astype(BF16)
    table = dot(high_ref[...], gagg, ROWS) + dot(low_ref[...], gagg, ROWS)
    total_ref[...] = direct + table[:rows]
    mirror_ref[...] = table[rows:].astype(BF16)


def weight_body(feat_ref, agg_ref, gfull_ref, out_ref):
    cols = feat_ref.shape[1]
    parts = out_ref.shape[0]
    piece = out_ref.shape[1] // 2
    for k, ref in enumerate((feat_ref, agg_ref)):
        left = ref[...]
        for c in range(gfull_ref.shape[0]):
            value = dot(left, gfull_ref[c], ROWS)
            out_ref[:, k * piece:(k + 1) * piece, c * cols:(c + 1) * cols] = value.reshape(
                parts, piece, cols
            ).astype(BF16)


def sum_body(scale, recv_ref, self_ref, neigh_ref):
    piece = self_ref.shape[0]
    for k, ref in enumerate((self_ref, neigh_ref)):
        total = jnp.zeros(ref.shape, F32)
        for d in range(recv_ref.shape[0]):
            total += recv_ref[d, k * piece:(k + 1) * piece].astype(F32)
        ref[...] = (total * scale).astype(BF16)


def group_weight_body(dom_ref, rep_ref, *refs):
    rows, grads, (keep_ref, send_ref, hold_ref) = refs[:4], refs[4:-3], refs[-3:]
    count = len(grads) // 2
    lanes = keep_ref.shape[3]
    layer, side = dom_ref[0] // 2, dom_ref[0] % 2
    for c in range(count):
        at = lax.bitwise_xor(rep_ref[0], c)
        hold_ref[0, at] = grads[c][:, block_rows(side, 0, lanes)]
        hold_ref[1, at] = grads[count + c][...]
    for k in range(2):
        own, other = rows[2 * k][...], rows[2 * k + 1][...]
        for offset in range(count):
            at = lax.bitwise_xor(layer, offset)
            value = dot(own, hold_ref[0, at], ROWS) + dot(other, hold_ref[1, at], ROWS)
            if offset % 2 == 0:
                keep_ref[offset // 2, k] = value
            else:
                send_ref[offset // 2, k] = value.astype(BF16)


def pair_body(keep_ref, next_ref, out_ref):
    out_ref[...] = (keep_ref[...] + next_ref[...].astype(F32)).astype(BF16)


def join_body(scale, pair_ref, far_ref, out_ref):
    for k in range(2):
        total = pair_ref[k].astype(F32) + far_ref[1 - k].astype(F32)
        out_ref[k] = (total * scale).astype(BF16)


def place_body(dom_ref, *refs):
    blocks, outs, sems = refs[:-3], refs[-3:-1], refs[-1]
    lanes = blocks[0].shape[3]
    copies = []
    for offset, block in enumerate(blocks):
        for far in range(2):
            at = block_rows(dom_ref[0], offset + 4 * far, lanes)
            for k, out_ref in enumerate(outs):
                copies.append(
                    pltpu.make_async_copy(
                        block.at[far, k], out_ref.at[:, at], sems.at[len(copies)]
                    )
                )
                copies[-1].start()
    for copy in copies:
        copy.wait()


def scatter_body(onehot_ref, total_ref, ret_ref, out_ref):
    out_ref[...] = (total_ref[...] + dot(onehot_ref[...], ret_ref[...])).astype(BF16)


def swap(array, axis, offset):
    return lax.ppermute(array, axis, [(i, i ^ offset) for i in range(lax.axis_size(axis))])


def gather_columns(array):
    across = swap(array, "rep", 2)
    return [array, swap(array, "rep", 1), across, swap(across, "rep", 1)]


def local(
    features, w_self, w_neigh, grad_out, mirror_list, mirror_count, tile_dst, tile_src, tiles
):
    rows, cols = features.shape
    width = w_self.shape[1]
    peers, slots = mirror_list.shape
    mirrors = peers * slots
    table_rows = rows + mirrors
    reps = width // cols
    struct = jax.ShapeDtypeStruct
    block = struct((rows, cols), BF16)
    rep = lax.axis_index("rep").astype(jnp.int32).reshape(1)
    dom = lax.axis_index("dom").astype(jnp.int32).reshape(1)
    lanes = width // peers
    split = peers == 8 and reps == 4 and slots % 16 == 0 and lanes % 128 == 0
    mirror_out = struct((mirrors, cols), BF16)

    def exchange(array):
        return lax.all_to_all(
            array.reshape(peers, slots, cols), "dom", split_axis=0, concat_axis=0, tiled=True
        ).reshape(mirrors, cols)

    onehot, outgoing = call(
        pick_body, (struct((rows, mirrors), BF16), mirror_out),
        [("h", mirror_count), ("h", mirror_list), ("h", features)],
        scratch=[
            pltpu.SMEM(mirror_count.shape, jnp.int32), pltpu.VMEM(mirror_list.shape, jnp.int32),
            pltpu.VMEM((rows, cols), BF16), pltpu.SemaphoreType.DMA((3,)),
        ],
        vmem=58,
        flops=2 * mirrors * rows * cols, moved=600_000,
    )
    incoming = exchange(outgoing)
    tiles_late, feat_late, self_late, neigh_late, _ = lax.optimization_barrier(
        (tiles, features, w_self, w_neigh, outgoing)
    )
    high, low, degree, self_near, neigh_near = call(
        prep_body,
        (
            struct((rows, table_rows), BF16), struct((rows, table_rows), BF16),
            struct((rows, 128), F32), struct(w_self.shape, BF16), struct(w_neigh.shape, BF16),
        ),
        [
            ("s", tile_dst), ("s", tile_src), ("v", tiles_late), ("h", self_late),
            ("h", neigh_late),
        ],
        scratch=[pltpu.VMEM((rows, table_rows), F32), pltpu.SemaphoreType.DMA((2,))],
        flops=1_000_000, moved=3_000_000,
    )
    if split:
        feat_beside = swap(features, "dom", 1)
        incoming, feat_beside = lax.optimization_barrier((incoming, feat_beside))
    own, agg, *parts = call(
        functools.partial(aggregate_body, split),
        (struct((rows, cols), F32), block)
        + (
            (struct((rows, cols), F32), struct((2, rows, cols), BF16)) if split
            else (struct((reps, rows, cols), BF16),)
        ),
        [
            ("s", rep), ("v", feat_late), ("v", incoming), ("v", high), ("v", low),
            ("v", degree), ("v", self_near), ("v", neigh_near),
        ],
        scratch=[pltpu.VMEM((table_rows, cols), BF16)],
        flops=600_000_000, moved=3_000_000,
    )
    scale = float(rows * peers) ** (-0.5)
    if split:
        agg_beside = swap(agg, "dom", 1)
        grad_out, agg_beside = lax.optimization_barrier((grad_out, agg_beside))
        beside = swap(parts[1], "rep", 1)
        across = call(
            across_body, block, [("v", parts[0]), ("v", beside)], flops=100_000, moved=500_000
        )
        across = swap(across, "rep", 2)
        hidden, grad_pre, half = call(
            gate_blocks_body, (block, block, struct((rows, lanes), BF16)),
            [("s", dom), ("v", own), ("v", grad_out), ("v", beside), ("v", across)],
            flops=2_000_000, moved=1_300_000,
        )
        grad_full = gather_columns(grad_pre)
        halves = gather_columns(swap(half, "dom", 1))
    else:
        recv = lax.all_to_all(parts[0], "rep", split_axis=0, concat_axis=0, tiled=True)
        hidden, grad_pre = call(
            gate_body, (block, block),
            [("s", rep), ("v", recv), ("v", own), ("v", grad_out)],
            flops=2_000_000, moved=1_300_000,
        )
        grad_full = [lax.all_gather(grad_pre, "rep", axis=0, tiled=False)]
    total, mirror_grad = call(
        functools.partial(back_body, split), (struct((rows, cols), F32), mirror_out),
        [
            ("s", rep), ("v", high), ("v", low), ("v", degree), ("v", self_near),
            ("v", neigh_near),
        ] + [("v", got) for got in grad_full],
        flops=600_000_000, moved=3_000_000,
    )
    if split:
        pieces = (2, 2, rows, lanes)
        keep, send = call(
            group_weight_body, (struct(pieces, F32), struct(pieces, BF16)),
            [
                ("s", dom), ("s", rep), ("v", features), ("v", feat_beside), ("v", agg),
                ("v", agg_beside),
            ] + [("v", got) for got in grad_full + halves],
            scratch=[pltpu.VMEM((2, reps, rows, lanes), BF16)],
            flops=600_000_000, moved=3_000_000,
        )
        pair = call(
            pair_body, struct(pieces, BF16), [("v", keep), ("v", swap(send, "dom", 2))],
            flops=200_000, moved=1_000_000,
        )
        done = call(
            functools.partial(join_body, scale), struct(pieces, BF16),
            [("v", pair), ("v", swap(pair, "dom", 4))], flops=200_000, moved=1_000_000,
        )
        layer = swap(done, "dom", 2)
        pieces = [done, swap(done, "dom", 1), layer, swap(layer, "dom", 1)]
    returned = exchange(mirror_grad)
    grad_features = call(
        scatter_body, block, [("v", onehot), ("v", total), ("v", returned)],
        flops=2 * mirrors * rows * cols, moved=700_000,
    )
    if split:
        out_self, out_neigh = call(
            place_body, (struct((rows, width), BF16), struct((rows, width), BF16)),
            [("s", dom)] + [("v", part) for part in pieces],
            scratch=[pltpu.SemaphoreType.DMA((2 * peers,))], moved=2_000_000, out="h",
        )
    else:
        piece = cols // peers
        partial = call(
            weight_body, struct((peers, 2 * piece, width), BF16),
            [("v", features), ("v", agg), ("v", grad_full[0])],
            flops=600_000_000, moved=2_000_000,
        )
        gathered = lax.all_to_all(partial, "dom", split_axis=0, concat_axis=0, tiled=True)
        mine_self, mine_neigh = call(
            functools.partial(sum_body, scale),
            (struct((piece, width), BF16), struct((piece, width), BF16)),
            [("v", gathered)], flops=1_000_000, moved=1_200_000,
        )
        out_self = lax.all_gather(mine_self, "dom", axis=0, tiled=True)
        out_neigh = lax.all_gather(mine_neigh, "dom", axis=0, tiled=True)
    return hidden, grad_features, out_self, out_neigh


def solution(mesh):
    in_specs = (
        P("dom", "rep"),
        P("rep", None),
        P("rep", None),
        P("dom", "rep"),
        P("dom", None),
        P("dom"),
        P("dom"),
        P("dom"),
        P("dom", None, None),
    )
    out_specs = (P("dom", "rep"), P("dom", "rep"), P("rep", None), P("rep", None))
    return jax.shard_map(local, mesh=mesh, in_specs=in_specs, out_specs=out_specs, check_vma=False)
```

```python
import functools

import jax
import jax.numpy as jnp
from jax import lax
from jax.experimental import pallas as pl
from jax.experimental.pallas import tpu as pltpu
from jax.sharding import PartitionSpec as P

F32 = jnp.float32
BF16 = jnp.bfloat16
SPECS = {
    "v": pl.BlockSpec(memory_space=pltpu.VMEM),
    "s": pl.BlockSpec(memory_space=pltpu.SMEM),
    "h": pl.BlockSpec(memory_space=pltpu.HBM),
}
ROWS = (((0,), (0,)), ((), ()))
COLS = (((1,), (1,)), ((), ()))


def call(body, outs, ins, scratch=(), flops=0, moved=0, vmem=16, out="v"):
    return pl.pallas_call(
        body,
        out_shape=outs,
        in_specs=[SPECS[spec] for spec, _ in ins],
        out_specs=jax.tree.map(lambda _: SPECS[out], outs),
        scratch_shapes=list(scratch),
        compiler_params=pltpu.CompilerParams(vmem_limit_bytes=vmem * 1024 * 1024),
        cost_estimate=pl.CostEstimate(flops=flops, bytes_accessed=moved, transcendentals=0),
    )(*[array for _, array in ins])


def dot(left, right, dims=(((1,), (0,)), ((), ()))):
    return lax.dot_general(left, right, dims, preferred_element_type=F32)


def block_rows(place, offset, size):
    return pl.ds(pl.multiple_of(lax.bitwise_xor(place, offset) * size, size), size)


def row_onehot(count_ref, lists, rows):
    peers, slots = lists.shape
    peer = lax.broadcasted_iota(jnp.int32, (peers, slots), 0)
    slot = lax.broadcasted_iota(jnp.int32, (peers, slots), 1)

    def fill(at, used):
        return jnp.where(peer == at, count_ref[at], used)

    used = jnp.zeros((peers, slots), jnp.int32)
    if peers <= 16:
        for at in range(peers):
            used = fill(at, used)
    else:
        used = lax.fori_loop(0, peers, fill, used)
    index = jnp.where(slot < used, lists, -1).astype(F32).astype(BF16)
    flat = peers * slots
    spread = (
        lax.broadcasted_iota(jnp.int32, (slots, flat), 0)
        == lax.broadcasted_iota(jnp.int32, (slots, flat), 1) % slots
    )
    wide = dot(index, spread.astype(F32).astype(BF16))
    mine = (
        lax.broadcasted_iota(jnp.int32, (peers, flat), 0)
        == lax.broadcasted_iota(jnp.int32, (peers, flat), 1) // slots
    )
    line = jnp.sum(jnp.where(mine, wide, 0.0), axis=0, keepdims=True).astype(jnp.int32)
    hit = lax.broadcasted_iota(jnp.int32, (rows, flat), 0) == line
    return hit.astype(F32).astype(BF16)


def pick_body(
    count_hbm, list_hbm, feat_hbm, onehot_ref, out_ref, count_ref, list_ref, feat_ref, sems
):
    copies = [
        pltpu.make_async_copy(src, dst, sems.at[k])
        for k, (src, dst) in enumerate(
            ((count_hbm, count_ref), (list_hbm, list_ref), (feat_hbm, feat_ref))
        )
    ]
    for copy in copies:
        copy.start()
    for copy in copies:
        copy.wait()
    onehot = row_onehot(count_ref, list_ref[...], feat_ref.shape[0])
    onehot_ref[...] = onehot
    out_ref[...] = dot(onehot, feat_ref[...], ROWS).astype(BF16)


def prep_body(
    dst_ref, src_ref, tiles_ref, self_hbm, neigh_hbm,
    high_ref, low_ref, deg_ref, self_ref, neigh_ref, adj_ref, sems,
):
    copies = [
        pltpu.make_async_copy(src, dst, sems.at[k])
        for k, (src, dst) in enumerate(((self_hbm, self_ref), (neigh_hbm, neigh_ref)))
    ]
    for copy in copies:
        copy.start()
    slots, side, _ = tiles_ref.shape
    adj_ref[...] = jnp.zeros(adj_ref.shape, F32)
    for t in range(slots):
        dst = pl.ds(pl.multiple_of(dst_ref[t] * side, side), side)
        src = pl.ds(pl.multiple_of(src_ref[t] * side, side), side)
        adj_ref[dst, src] += tiles_ref[t].astype(F32)
    adj = adj_ref[...]
    high = adj.astype(BF16)
    high_ref[...] = high
    low_ref[...] = (adj - high.astype(F32)).astype(BF16)
    degree = jnp.maximum(jnp.sum(adj, axis=1, keepdims=True), 1.0)
    deg_ref[...] = jnp.broadcast_to(degree, deg_ref.shape)
    for copy in copies:
        copy.wait()


def column_block(split, rep, c, reps, cols):
    other = lax.bitwise_xor(rep, c) if split else c
    return pl.ds(pl.multiple_of(other * cols, cols), cols)


def wide_degree(deg_ref, cols):
    return jnp.concatenate([deg_ref[...]] * (cols // deg_ref.shape[1]), axis=1)


def aggregate_body(
    split, rep_ref, feat_ref, inc_ref, high_ref, low_ref, deg_ref, self_ref, neigh_ref,
    own_ref, agg_ref, *refs,
):
    part_refs, table_ref = refs[:-1], refs[-1]
    rows, cols = feat_ref.shape
    feat = feat_ref[...]
    table_ref[:rows] = feat
    table_ref[rows:] = inc_ref[...]
    table = table_ref[...]
    summed = dot(high_ref[...], table) + dot(low_ref[...], table)
    agg = (summed / wide_degree(deg_ref, cols)).astype(BF16)
    agg_ref[...] = agg
    reps = self_ref.shape[1] // cols
    for c in reversed(range(reps)):
        at = column_block(split, rep_ref[0], c, reps, cols)
        value = dot(feat, self_ref[:, at]) + dot(agg, neigh_ref[:, at])
        if not split:
            part_refs[0][c] = value.astype(BF16)

            @pl.when(rep_ref[0] == c)
            def _():
                own_ref[...] = value
        elif c == 0:
            own_ref[...] = value
        elif c == 2:
            part_refs[0][...] = value
        else:
            part_refs[1][c // 2] = value.astype(BF16)


def finish_gate(pre, gout_ref, hid_ref, gpre_ref):
    gate = jax.nn.sigmoid(pre)
    hid_ref[...] = (pre * gate).astype(BF16)
    gpre_ref[...] = (gout_ref[...].astype(F32) * (gate + pre * gate * (1.0 - gate))).astype(BF16)


def gate_body(rep_ref, recv_ref, own_ref, gout_ref, hid_ref, gpre_ref):
    pre = own_ref[...]
    for c in range(recv_ref.shape[0]):
        pre = pre + jnp.where(rep_ref[0] == c, 0.0, recv_ref[c].astype(F32))
    finish_gate(pre, gout_ref, hid_ref, gpre_ref)


def across_body(mine_ref, beside_ref, out_ref):
    out_ref[...] = (mine_ref[...] + beside_ref[1].astype(F32)).astype(BF16)


def gate_blocks_body(dom_ref, own_ref, gout_ref, beside_ref, across_ref, hid_ref, gpre_ref, send_ref):
    pre = own_ref[...] + beside_ref[0].astype(F32) + across_ref[...].astype(F32)
    finish_gate(pre, gout_ref, hid_ref, gpre_ref)
    send_ref[...] = gpre_ref[:, block_rows(dom_ref[0] % 2, 1, send_ref.shape[1])]


def back_body(
    split, rep_ref, high_ref, low_ref, deg_ref, self_ref, neigh_ref, *refs,
):
    grads, (total_ref, mirror_ref) = refs[:-2], refs[-2:]
    rows, cols = total_ref.shape
    reps = self_ref.shape[1] // cols
    direct = jnp.zeros((rows, cols), F32)
    gagg = jnp.zeros((rows, cols), F32)
    for c in range(reps):
        grad = grads[c][...] if split else grads[0][c]
        at = column_block(split, rep_ref[0], c, reps, cols)
        gagg += dot(grad, neigh_ref[:, at], COLS)
        direct += dot(grad, self_ref[:, at], COLS)
    gagg = (gagg / wide_degree(deg_ref, cols)).astype(BF16)
    table = dot(high_ref[...], gagg, ROWS) + dot(low_ref[...], gagg, ROWS)
    total_ref[...] = direct + table[:rows]
    mirror_ref[...] = table[rows:].astype(BF16)


def weight_body(feat_ref, agg_ref, gfull_ref, out_ref):
    cols = feat_ref.shape[1]
    parts = out_ref.shape[0]
    piece = out_ref.shape[1] // 2
    for k, ref in enumerate((feat_ref, agg_ref)):
        left = ref[...]
        for c in range(gfull_ref.shape[0]):
            value = dot(left, gfull_ref[c], ROWS)
            out_ref[:, k * piece:(k + 1) * piece, c * cols:(c + 1) * cols] = value.reshape(
                parts, piece, cols
            ).astype(BF16)


def sum_body(scale, recv_ref, self_ref, neigh_ref):
    piece = self_ref.shape[0]
    for k, ref in enumerate((self_ref, neigh_ref)):
        total = jnp.zeros(ref.shape, F32)
        for d in range(recv_ref.shape[0]):
            total += recv_ref[d, k * piece:(k + 1) * piece].astype(F32)
        ref[...] = (total * scale).astype(BF16)


def group_weight_body(dom_ref, rep_ref, *refs):
    rows, grads, (keep_ref, send_ref, hold_ref) = refs[:4], refs[4:-3], refs[-3:]
    count = len(grads) // 2
    lanes = keep_ref.shape[3]
    layer, side = dom_ref[0] // 2, dom_ref[0] % 2
    for c in range(count):
        at = lax.bitwise_xor(rep_ref[0], c)
        hold_ref[0, at] = grads[c][:, block_rows(side, 0, lanes)]
        hold_ref[1, at] = grads[count + c][...]
    for k in range(2):
        own, other = rows[2 * k][...], rows[2 * k + 1][...]
        for offset in range(count):
            at = lax.bitwise_xor(layer, offset)
            value = dot(own, hold_ref[0, at], ROWS) + dot(other, hold_ref[1, at], ROWS)
            if offset % 2 == 0:
                keep_ref[offset // 2, k] = value
            else:
                send_ref[offset // 2, k] = value.astype(BF16)


def pair_body(keep_ref, next_ref, out_ref):
    out_ref[...] = (keep_ref[...] + next_ref[...].astype(F32)).astype(BF16)


def join_body(scale, pair_ref, far_ref, out_ref):
    for k in range(2):
        total = pair_ref[k].astype(F32) + far_ref[1 - k].astype(F32)
        out_ref[k] = (total * scale).astype(BF16)


def place_body(dom_ref, *refs):
    blocks, outs, sems = refs[:-3], refs[-3:-1], refs[-1]
    lanes = blocks[0].shape[3]
    copies = []
    for offset, block in enumerate(blocks):
        for far in range(2):
            at = block_rows(dom_ref[0], offset + 4 * far, lanes)
            for k, out_ref in enumerate(outs):
                copies.append(
                    pltpu.make_async_copy(
                        block.at[far, k], out_ref.at[:, at], sems.at[len(copies)]
                    )
                )
                copies[-1].start()
    for copy in copies:
        copy.wait()


def scatter_body(onehot_ref, total_ref, ret_ref, out_ref):
    out_ref[...] = (total_ref[...] + dot(onehot_ref[...], ret_ref[...])).astype(BF16)


def swap(array, axis, offset):
    return lax.ppermute(array, axis, [(i, i ^ offset) for i in range(lax.axis_size(axis))])


def gather_columns(array):
    across = swap(array, "rep", 2)
    return [array, swap(array, "rep", 1), across, swap(across, "rep", 1)]


def local(
    features, w_self, w_neigh, grad_out, mirror_list, mirror_count, tile_dst, tile_src, tiles
):
    rows, cols = features.shape
    width = w_self.shape[1]
    peers, slots = mirror_list.shape
    mirrors = peers * slots
    table_rows = rows + mirrors
    reps = width // cols
    struct = jax.ShapeDtypeStruct
    block = struct((rows, cols), BF16)
    rep = lax.axis_index("rep").astype(jnp.int32).reshape(1)
    dom = lax.axis_index("dom").astype(jnp.int32).reshape(1)
    lanes = width // peers
    split = peers == 8 and reps == 4 and slots % 16 == 0 and lanes % 128 == 0
    mirror_out = struct((mirrors, cols), BF16)

    def exchange(array):
        return lax.all_to_all(
            array.reshape(peers, slots, cols), "dom", split_axis=0, concat_axis=0, tiled=True
        ).reshape(mirrors, cols)

    onehot, outgoing = call(
        pick_body, (struct((rows, mirrors), BF16), mirror_out),
        [("h", mirror_count), ("h", mirror_list), ("h", features)],
        scratch=[
            pltpu.SMEM(mirror_count.shape, jnp.int32), pltpu.VMEM(mirror_list.shape, jnp.int32),
            pltpu.VMEM((rows, cols), BF16), pltpu.SemaphoreType.DMA((3,)),
        ],
        vmem=58,
        flops=2 * mirrors * rows * cols, moved=600_000,
    )
    incoming = exchange(outgoing)
    tiles_late, feat_late, self_late, neigh_late, _ = lax.optimization_barrier(
        (tiles, features, w_self, w_neigh, outgoing)
    )
    high, low, degree, self_near, neigh_near = call(
        prep_body,
        (
            struct((rows, table_rows), BF16), struct((rows, table_rows), BF16),
            struct((rows, 128), F32), struct(w_self.shape, BF16), struct(w_neigh.shape, BF16),
        ),
        [
            ("s", tile_dst), ("s", tile_src), ("v", tiles_late), ("h", self_late),
            ("h", neigh_late),
        ],
        scratch=[pltpu.VMEM((rows, table_rows), F32), pltpu.SemaphoreType.DMA((2,))],
        flops=1_000_000, moved=3_000_000,
    )
    if split:
        feat_beside = swap(features, "dom", 1)
        incoming, feat_beside = lax.optimization_barrier((incoming, feat_beside))
    own, agg, *parts = call(
        functools.partial(aggregate_body, split),
        (struct((rows, cols), F32), block)
        + (
            (struct((rows, cols), F32), struct((2, rows, cols), BF16)) if split
            else (struct((reps, rows, cols), BF16),)
        ),
        [
            ("s", rep), ("v", feat_late), ("v", incoming), ("v", high), ("v", low),
            ("v", degree), ("v", self_near), ("v", neigh_near),
        ],
        scratch=[pltpu.VMEM((table_rows, cols), BF16)],
        flops=600_000_000, moved=3_000_000,
    )
    scale = float(rows * peers) ** (-0.5)
    if split:
        agg_beside = swap(agg, "dom", 1)
        grad_out, agg_beside = lax.optimization_barrier((grad_out, agg_beside))
        beside = swap(parts[1], "rep", 1)
        across = call(
            across_body, block, [("v", parts[0]), ("v", beside)], flops=100_000, moved=500_000
        )
        across = swap(across, "rep", 2)
        hidden, grad_pre, half = call(
            gate_blocks_body, (block, block, struct((rows, lanes), BF16)),
            [("s", dom), ("v", own), ("v", grad_out), ("v", beside), ("v", across)],
            flops=2_000_000, moved=1_300_000,
        )
        grad_full = gather_columns(grad_pre)
        halves = gather_columns(swap(half, "dom", 1))
    else:
        recv = lax.all_to_all(parts[0], "rep", split_axis=0, concat_axis=0, tiled=True)
        hidden, grad_pre = call(
            gate_body, (block, block),
            [("s", rep), ("v", recv), ("v", own), ("v", grad_out)],
            flops=2_000_000, moved=1_300_000,
        )
        grad_full = [lax.all_gather(grad_pre, "rep", axis=0, tiled=False)]
    def back(high):
        return call(
            functools.partial(back_body, split), (struct((rows, cols), F32), mirror_out),
            [
                ("s", rep), ("v", high), ("v", low), ("v", degree), ("v", self_near),
                ("v", neigh_near),
            ] + [("v", got) for got in grad_full],
            flops=600_000_000, moved=3_000_000,
        )

    if split:
        pieces = (2, 2, rows, lanes)
        keep, send = call(
            group_weight_body, (struct(pieces, F32), struct(pieces, BF16)),
            [
                ("s", dom), ("s", rep), ("v", features), ("v", feat_beside), ("v", agg),
                ("v", agg_beside),
            ] + [("v", got) for got in grad_full + halves],
            scratch=[pltpu.VMEM((2, reps, rows, lanes), BF16)],
            flops=600_000_000, moved=3_000_000,
        )
        late, _ = lax.optimization_barrier((high, send))
        total, mirror_grad = back(late)
        returned = exchange(mirror_grad)
        pair = call(
            pair_body, struct(pieces, BF16), [("v", keep), ("v", swap(send, "dom", 2))],
            flops=200_000, moved=1_000_000,
        )
        far, returned = lax.optimization_barrier((swap(pair, "dom", 4), returned))
        done = call(
            functools.partial(join_body, scale), struct(pieces, BF16),
            [("v", pair), ("v", far)], flops=200_000, moved=1_000_000,
        )
        layer = swap(done, "dom", 2)
        pieces = [done, swap(done, "dom", 1), layer, swap(layer, "dom", 1)]
    else:
        total, mirror_grad = back(high)
        returned = exchange(mirror_grad)
    grad_features = call(
        scatter_body, block, [("v", onehot), ("v", total), ("v", returned)],
        flops=2 * mirrors * rows * cols, moved=700_000,
    )
    if split:
        out_self, out_neigh = call(
            place_body, (struct((rows, width), BF16), struct((rows, width), BF16)),
            [("s", dom)] + [("v", part) for part in pieces],
            scratch=[pltpu.SemaphoreType.DMA((2 * peers,))], moved=2_000_000, out="h",
        )
    else:
        piece = cols // peers
        partial = call(
            weight_body, struct((peers, 2 * piece, width), BF16),
            [("v", features), ("v", agg), ("v", grad_full[0])],
            flops=600_000_000, moved=2_000_000,
        )
        gathered = lax.all_to_all(partial, "dom", split_axis=0, concat_axis=0, tiled=True)
        mine_self, mine_neigh = call(
            functools.partial(sum_body, scale),
            (struct((piece, width), BF16), struct((piece, width), BF16)),
            [("v", gathered)], flops=1_000_000, moved=1_200_000,
        )
        out_self = lax.all_gather(mine_self, "dom", axis=0, tiled=True)
        out_neigh = lax.all_gather(mine_neigh, "dom", axis=0, tiled=True)
    return hidden, grad_features, out_self, out_neigh


def solution(mesh):
    in_specs = (
        P("dom", "rep"),
        P("rep", None),
        P("rep", None),
        P("dom", "rep"),
        P("dom", None),
        P("dom"),
        P("dom"),
        P("dom"),
        P("dom", None, None),
    )
    out_specs = (P("dom", "rep"), P("dom", "rep"), P("rep", None), P("rep", None))
    return jax.shard_map(local, mesh=mesh, in_specs=in_specs, out_specs=out_specs, check_vma=False)
```

```python
import functools

import jax
import jax.numpy as jnp
from jax import lax
from jax.experimental import pallas as pl
from jax.experimental.pallas import tpu as pltpu
from jax.sharding import PartitionSpec as P

F32 = jnp.float32
BF16 = jnp.bfloat16
SPECS = {
    "v": pl.BlockSpec(memory_space=pltpu.VMEM),
    "s": pl.BlockSpec(memory_space=pltpu.SMEM),
    "h": pl.BlockSpec(memory_space=pltpu.HBM),
}
ROWS = (((0,), (0,)), ((), ()))
COLS = (((1,), (1,)), ((), ()))


def call(body, outs, ins, scratch=(), flops=0, moved=0, vmem=16, out="v"):
    return pl.pallas_call(
        body,
        out_shape=outs,
        in_specs=[SPECS[spec] for spec, _ in ins],
        out_specs=jax.tree.map(lambda _: SPECS[out], outs),
        scratch_shapes=list(scratch),
        compiler_params=pltpu.CompilerParams(vmem_limit_bytes=vmem * 1024 * 1024),
        cost_estimate=pl.CostEstimate(flops=flops, bytes_accessed=moved, transcendentals=0),
    )(*[array for _, array in ins])


def dot(left, right, dims=(((1,), (0,)), ((), ()))):
    return lax.dot_general(left, right, dims, preferred_element_type=F32)


def block_rows(place, offset, size):
    return pl.ds(pl.multiple_of(lax.bitwise_xor(place, offset) * size, size), size)


def row_onehot(count_ref, lists, rows):
    peers, slots = lists.shape
    peer = lax.broadcasted_iota(jnp.int32, (peers, slots), 0)
    slot = lax.broadcasted_iota(jnp.int32, (peers, slots), 1)

    def fill(at, used):
        return jnp.where(peer == at, count_ref[at], used)

    used = jnp.zeros((peers, slots), jnp.int32)
    if peers <= 16:
        for at in range(peers):
            used = fill(at, used)
    else:
        used = lax.fori_loop(0, peers, fill, used)
    index = jnp.where(slot < used, lists, -1).astype(F32).astype(BF16)
    flat = peers * slots
    spread = (
        lax.broadcasted_iota(jnp.int32, (slots, flat), 0)
        == lax.broadcasted_iota(jnp.int32, (slots, flat), 1) % slots
    )
    wide = dot(index, spread.astype(F32).astype(BF16))
    mine = (
        lax.broadcasted_iota(jnp.int32, (peers, flat), 0)
        == lax.broadcasted_iota(jnp.int32, (peers, flat), 1) // slots
    )
    line = jnp.sum(jnp.where(mine, wide, 0.0), axis=0, keepdims=True).astype(jnp.int32)
    hit = lax.broadcasted_iota(jnp.int32, (rows, flat), 0) == line
    return hit.astype(F32).astype(BF16)


def pick_body(
    count_hbm, list_hbm, feat_hbm, onehot_ref, out_ref, count_ref, list_ref, feat_ref, sems
):
    copies = [
        pltpu.make_async_copy(src, dst, sems.at[k])
        for k, (src, dst) in enumerate(
            ((count_hbm, count_ref), (list_hbm, list_ref), (feat_hbm, feat_ref))
        )
    ]
    for copy in copies:
        copy.start()
    for copy in copies:
        copy.wait()
    onehot = row_onehot(count_ref, list_ref[...], feat_ref.shape[0])
    onehot_ref[...] = onehot
    out_ref[...] = dot(onehot, feat_ref[...], ROWS).astype(BF16)


def prep_body(
    dst_ref, src_ref, tiles_ref, self_hbm, neigh_hbm,
    high_ref, low_ref, deg_ref, self_ref, neigh_ref, adj_ref, sems,
):
    copies = [
        pltpu.make_async_copy(src, dst, sems.at[k])
        for k, (src, dst) in enumerate(((self_hbm, self_ref), (neigh_hbm, neigh_ref)))
    ]
    for copy in copies:
        copy.start()
    slots, side, _ = tiles_ref.shape
    adj_ref[...] = jnp.zeros(adj_ref.shape, F32)
    for t in range(slots):
        dst = pl.ds(pl.multiple_of(dst_ref[t] * side, side), side)
        src = pl.ds(pl.multiple_of(src_ref[t] * side, side), side)
        adj_ref[dst, src] += tiles_ref[t].astype(F32)
    adj = adj_ref[...]
    high = adj.astype(BF16)
    high_ref[...] = high
    low_ref[...] = (adj - high.astype(F32)).astype(BF16)
    degree = jnp.maximum(jnp.sum(adj, axis=1, keepdims=True), 1.0)
    deg_ref[...] = jnp.broadcast_to(degree, deg_ref.shape)
    for copy in copies:
        copy.wait()


def column_block(split, rep, c, reps, cols):
    other = lax.bitwise_xor(rep, c) if split else c
    return pl.ds(pl.multiple_of(other * cols, cols), cols)


def wide_degree(deg_ref, cols):
    return jnp.concatenate([deg_ref[...]] * (cols // deg_ref.shape[1]), axis=1)


def aggregate_body(
    split, rep_ref, feat_ref, inc_ref, high_ref, low_ref, deg_ref, self_ref, neigh_ref,
    own_ref, agg_ref, *refs,
):
    part_refs, table_ref = refs[:-1], refs[-1]
    rows, cols = feat_ref.shape
    feat = feat_ref[...]
    table_ref[:rows] = feat
    table_ref[rows:] = inc_ref[...]
    table = table_ref[...]
    summed = dot(high_ref[...], table) + dot(low_ref[...], table)
    agg = (summed / wide_degree(deg_ref, cols)).astype(BF16)
    agg_ref[...] = agg
    reps = self_ref.shape[1] // cols
    for c in reversed(range(reps)):
        at = column_block(split, rep_ref[0], c, reps, cols)
        value = dot(feat, self_ref[:, at]) + dot(agg, neigh_ref[:, at])
        if not split:
            part_refs[0][c] = value.astype(BF16)

            @pl.when(rep_ref[0] == c)
            def _():
                own_ref[...] = value
        elif c == 0:
            own_ref[...] = value
        elif c == 2:
            part_refs[0][...] = value
        else:
            part_refs[1][c // 2] = value.astype(BF16)


def finish_gate(pre, gout_ref, hid_ref, gpre_ref):
    gate = jax.nn.sigmoid(pre)
    hid_ref[...] = (pre * gate).astype(BF16)
    gpre_ref[...] = (gout_ref[...].astype(F32) * (gate + pre * gate * (1.0 - gate))).astype(BF16)


def gate_body(rep_ref, recv_ref, own_ref, gout_ref, hid_ref, gpre_ref):
    pre = own_ref[...]
    for c in range(recv_ref.shape[0]):
        pre = pre + jnp.where(rep_ref[0] == c, 0.0, recv_ref[c].astype(F32))
    finish_gate(pre, gout_ref, hid_ref, gpre_ref)


def across_body(mine_ref, beside_ref, out_ref):
    out_ref[...] = (mine_ref[...] + beside_ref[1].astype(F32)).astype(BF16)


def gate_blocks_body(dom_ref, own_ref, gout_ref, beside_ref, across_ref, hid_ref, gpre_ref, send_ref):
    pre = own_ref[...] + beside_ref[0].astype(F32) + across_ref[...].astype(F32)
    finish_gate(pre, gout_ref, hid_ref, gpre_ref)
    send_ref[...] = gpre_ref[:, block_rows(dom_ref[0] % 2, 1, send_ref.shape[1])]


def back_body(
    split, rep_ref, high_ref, low_ref, deg_ref, self_ref, neigh_ref, *refs,
):
    grads, (total_ref, mirror_ref) = refs[:-2], refs[-2:]
    rows, cols = total_ref.shape
    reps = self_ref.shape[1] // cols
    direct = jnp.zeros((rows, cols), F32)
    gagg = jnp.zeros((rows, cols), F32)
    for c in range(reps):
        grad = grads[c][...] if split else grads[0][c]
        at = column_block(split, rep_ref[0], c, reps, cols)
        gagg += dot(grad, neigh_ref[:, at], COLS)
        direct += dot(grad, self_ref[:, at], COLS)
    gagg = (gagg / wide_degree(deg_ref, cols)).astype(BF16)
    table = dot(high_ref[...], gagg, ROWS) + dot(low_ref[...], gagg, ROWS)
    total_ref[...] = direct + table[:rows]
    mirror_ref[...] = table[rows:].astype(BF16)


def weight_body(feat_ref, agg_ref, gfull_ref, out_ref):
    cols = feat_ref.shape[1]
    parts = out_ref.shape[0]
    piece = out_ref.shape[1] // 2
    for k, ref in enumerate((feat_ref, agg_ref)):
        left = ref[...]
        for c in range(gfull_ref.shape[0]):
            value = dot(left, gfull_ref[c], ROWS)
            out_ref[:, k * piece:(k + 1) * piece, c * cols:(c + 1) * cols] = value.reshape(
                parts, piece, cols
            ).astype(BF16)


def sum_body(scale, recv_ref, self_ref, neigh_ref):
    piece = self_ref.shape[0]
    for k, ref in enumerate((self_ref, neigh_ref)):
        total = jnp.zeros(ref.shape, F32)
        for d in range(recv_ref.shape[0]):
            total += recv_ref[d, k * piece:(k + 1) * piece].astype(F32)
        ref[...] = (total * scale).astype(BF16)


def group_weight_body(dom_ref, rep_ref, *refs):
    rows, (mine_ref, far_ref, send_ref, hold_ref) = refs[:4], refs[-4:]
    grads = refs[4:-4]
    count = len(grads) // 2
    lanes = mine_ref.shape[2]
    layer, side = dom_ref[0] // 2, dom_ref[0] % 2
    for c in range(count):
        at = lax.bitwise_xor(rep_ref[0], c)
        hold_ref[0, at] = grads[c][:, block_rows(side, 0, lanes)]
        hold_ref[1, at] = grads[count + c][...]
    for k in range(2):
        own, other = rows[2 * k][...], rows[2 * k + 1][...]
        for offset in range(count):
            at = lax.bitwise_xor(layer, offset)
            value = dot(own, hold_ref[0, at], ROWS) + dot(other, hold_ref[1, at], ROWS)
            if offset == 0:
                mine_ref[k] = value
            elif offset == 2:
                far_ref[k] = value
            else:
                send_ref[offset // 2, k] = value.astype(BF16)


def join_body(scale, mine_ref, next_ref, far_ref, out_ref):
    total = mine_ref[...] + next_ref[0].astype(F32) + far_ref[...].astype(F32)
    out_ref[...] = (total * scale).astype(BF16)


def place_body(dom_ref, *refs):
    blocks, outs, sems = refs[:-3], refs[-3:-1], refs[-1]
    copies = []
    lanes = blocks[0].shape[2]
    for offset, block in enumerate(blocks):
        at = block_rows(dom_ref[0], offset, lanes)
        for k, out_ref in enumerate(outs):
            copies.append(
                pltpu.make_async_copy(block.at[k], out_ref.at[:, at], sems.at[2 * offset + k])
            )
            copies[-1].start()
    for copy in copies:
        copy.wait()


def scatter_body(onehot_ref, total_ref, ret_ref, out_ref):
    out_ref[...] = (total_ref[...] + dot(onehot_ref[...], ret_ref[...])).astype(BF16)


def swap(array, axis, offset):
    return lax.ppermute(array, axis, [(i, i ^ offset) for i in range(lax.axis_size(axis))])


def gather_columns(array):
    across = swap(array, "rep", 2)
    return [array, swap(array, "rep", 1), across, swap(across, "rep", 1)]


def gather_pieces(array, peers):
    out = {0: array, 4: swap(array, "dom", 4), 2: swap(array, "dom", 2)}
    out[1] = swap(array, "dom", 1)
    out[3] = swap(out[2], "dom", 1)
    out[4], out[1] = lax.optimization_barrier((out[4], out[1]))
    out[6] = swap(out[4], "dom", 2)
    late, out[3] = lax.optimization_barrier((out[4], out[3]))
    out[5] = swap(late, "dom", 1)
    out[7] = swap(out[6], "dom", 1)
    return [out[offset] for offset in range(peers)]


def local(
    features, w_self, w_neigh, grad_out, mirror_list, mirror_count, tile_dst, tile_src, tiles
):
    rows, cols = features.shape
    width = w_self.shape[1]
    peers, slots = mirror_list.shape
    mirrors = peers * slots
    table_rows = rows + mirrors
    reps = width // cols
    struct = jax.ShapeDtypeStruct
    block = struct((rows, cols), BF16)
    rep = lax.axis_index("rep").astype(jnp.int32).reshape(1)
    dom = lax.axis_index("dom").astype(jnp.int32).reshape(1)
    lanes = width // peers
    split = peers == 8 and reps == 4 and slots % 16 == 0 and lanes % 128 == 0
    mirror_out = struct((mirrors, cols), BF16)

    def exchange(array):
        return lax.all_to_all(
            array.reshape(peers, slots, cols), "dom", split_axis=0, concat_axis=0, tiled=True
        ).reshape(mirrors, cols)

    onehot, outgoing = call(
        pick_body, (struct((rows, mirrors), BF16), mirror_out),
        [("h", mirror_count), ("h", mirror_list), ("h", features)],
        scratch=[
            pltpu.SMEM(mirror_count.shape, jnp.int32), pltpu.VMEM(mirror_list.shape, jnp.int32),
            pltpu.VMEM((rows, cols), BF16), pltpu.SemaphoreType.DMA((3,)),
        ],
        vmem=58,
        flops=2 * mirrors * rows * cols, moved=600_000,
    )
    incoming = exchange(outgoing)
    tiles_late, feat_late, self_late, neigh_late, _ = lax.optimization_barrier(
        (tiles, features, w_self, w_neigh, outgoing)
    )
    high, low, degree, self_near, neigh_near = call(
        prep_body,
        (
            struct((rows, table_rows), BF16), struct((rows, table_rows), BF16),
            struct((rows, 128), F32), struct(w_self.shape, BF16), struct(w_neigh.shape, BF16),
        ),
        [
            ("s", tile_dst), ("s", tile_src), ("v", tiles_late), ("h", self_late),
            ("h", neigh_late),
        ],
        scratch=[pltpu.VMEM((rows, table_rows), F32), pltpu.SemaphoreType.DMA((2,))],
        flops=1_000_000, moved=3_000_000,
    )
    if split:
        feat_beside = swap(features, "dom", 1)
        incoming, feat_beside = lax.optimization_barrier((incoming, feat_beside))
    own, agg, *parts = call(
        functools.partial(aggregate_body, split),
        (struct((rows, cols), F32), block)
        + (
            (struct((rows, cols), F32), struct((2, rows, cols), BF16)) if split
            else (struct((reps, rows, cols), BF16),)
        ),
        [
            ("s", rep), ("v", feat_late), ("v", incoming), ("v", high), ("v", low),
            ("v", degree), ("v", self_near), ("v", neigh_near),
        ],
        scratch=[pltpu.VMEM((table_rows, cols), BF16)],
        flops=600_000_000, moved=3_000_000,
    )
    scale = float(rows * peers) ** (-0.5)
    if split:
        agg_beside = swap(agg, "dom", 1)
        grad_out, agg_beside = lax.optimization_barrier((grad_out, agg_beside))
        beside = swap(parts[1], "rep", 1)
        across = call(
            across_body, block, [("v", parts[0]), ("v", beside)], flops=100_000, moved=500_000
        )
        across = swap(across, "rep", 2)
        hidden, grad_pre, half = call(
            gate_blocks_body, (block, block, struct((rows, lanes), BF16)),
            [("s", dom), ("v", own), ("v", grad_out), ("v", beside), ("v", across)],
            flops=2_000_000, moved=1_300_000,
        )
        grad_full = gather_columns(grad_pre)
        half = swap(half, "dom", 1)
        halves = [half] + [swap(half, "rep", offset) for offset in (1, 2, 3)]
    else:
        recv = lax.all_to_all(parts[0], "rep", split_axis=0, concat_axis=0, tiled=True)
        hidden, grad_pre = call(
            gate_body, (block, block),
            [("s", rep), ("v", recv), ("v", own), ("v", grad_out)],
            flops=2_000_000, moved=1_300_000,
        )
        grad_full = [lax.all_gather(grad_pre, "rep", axis=0, tiled=False)]
    total, mirror_grad = call(
        functools.partial(back_body, split), (struct((rows, cols), F32), mirror_out),
        [
            ("s", rep), ("v", high), ("v", low), ("v", degree), ("v", self_near),
            ("v", neigh_near),
        ] + [("v", got) for got in grad_full],
        flops=600_000_000, moved=3_000_000,
    )
    if split:
        piece = struct((2, rows, lanes), F32)
        mine, far, send = call(
            group_weight_body, (piece, piece, struct((2, 2, rows, lanes), BF16)),
            [
                ("s", dom), ("s", rep), ("v", features), ("v", feat_beside), ("v", agg),
                ("v", agg_beside),
            ] + [("v", got) for got in grad_full + halves],
            scratch=[pltpu.VMEM((2, reps, rows, lanes), BF16)],
            flops=600_000_000, moved=3_000_000,
        )
        piece = struct((2, rows, lanes), BF16)
        beside = swap(send, "dom", 2)
        far = call(across_body, piece, [("v", far), ("v", beside)], flops=100_000, moved=500_000)
        mine = call(
            functools.partial(join_body, scale), piece,
            [("v", mine), ("v", beside), ("v", swap(far, "dom", 4))],
            flops=200_000, moved=500_000,
        )
        pieces = gather_pieces(mine, peers)
    returned = exchange(mirror_grad)
    grad_features = call(
        scatter_body, block, [("v", onehot), ("v", total), ("v", returned)],
        flops=2 * mirrors * rows * cols, moved=700_000,
    )
    if split:
        out_self, out_neigh = call(
            place_body, (struct((rows, width), BF16), struct((rows, width), BF16)),
            [("s", dom)] + [("v", part) for part in pieces],
            scratch=[pltpu.SemaphoreType.DMA((2 * peers,))], moved=2_000_000, out="h",
        )
    else:
        piece = cols // peers
        partial = call(
            weight_body, struct((peers, 2 * piece, width), BF16),
            [("v", features), ("v", agg), ("v", grad_full[0])],
            flops=600_000_000, moved=2_000_000,
        )
        gathered = lax.all_to_all(partial, "dom", split_axis=0, concat_axis=0, tiled=True)
        mine_self, mine_neigh = call(
            functools.partial(sum_body, scale),
            (struct((piece, width), BF16), struct((piece, width), BF16)),
            [("v", gathered)], flops=1_000_000, moved=1_200_000,
        )
        out_self = lax.all_gather(mine_self, "dom", axis=0, tiled=True)
        out_neigh = lax.all_gather(mine_neigh, "dom", axis=0, tiled=True)
    return hidden, grad_features, out_self, out_neigh


def solution(mesh):
    in_specs = (
        P("dom", "rep"),
        P("rep", None),
        P("rep", None),
        P("dom", "rep"),
        P("dom", None),
        P("dom"),
        P("dom"),
        P("dom"),
        P("dom", None, None),
    )
    out_specs = (P("dom", "rep"), P("dom", "rep"), P("rep", None), P("rep", None))
    return jax.shard_map(local, mesh=mesh, in_specs=in_specs, out_specs=out_specs, check_vma=False)
```

```python
import functools

import jax
import jax.numpy as jnp
from jax import lax
from jax.experimental import pallas as pl
from jax.experimental.pallas import tpu as pltpu
from jax.sharding import PartitionSpec as P

F32 = jnp.float32
BF16 = jnp.bfloat16
SPECS = {
    "v": pl.BlockSpec(memory_space=pltpu.VMEM),
    "s": pl.BlockSpec(memory_space=pltpu.SMEM),
    "h": pl.BlockSpec(memory_space=pltpu.HBM),
}
ROWS = (((0,), (0,)), ((), ()))
COLS = (((1,), (1,)), ((), ()))


def call(body, outs, ins, scratch=(), flops=0, moved=0, vmem=16, out="v"):
    return pl.pallas_call(
        body,
        out_shape=outs,
        in_specs=[SPECS[spec] for spec, _ in ins],
        out_specs=jax.tree.map(lambda _: SPECS[out], outs),
        scratch_shapes=list(scratch),
        compiler_params=pltpu.CompilerParams(vmem_limit_bytes=vmem * 1024 * 1024),
        cost_estimate=pl.CostEstimate(flops=flops, bytes_accessed=moved, transcendentals=0),
    )(*[array for _, array in ins])


def dot(left, right, dims=(((1,), (0,)), ((), ()))):
    return lax.dot_general(left, right, dims, preferred_element_type=F32)


def block_rows(place, offset, size):
    return pl.ds(pl.multiple_of(lax.bitwise_xor(place, offset) * size, size), size)


def row_onehot(count_ref, lists, rows):
    peers, slots = lists.shape
    peer = lax.broadcasted_iota(jnp.int32, (peers, slots), 0)
    slot = lax.broadcasted_iota(jnp.int32, (peers, slots), 1)

    def fill(at, used):
        return jnp.where(peer == at, count_ref[at], used)

    used = jnp.zeros((peers, slots), jnp.int32)
    if peers <= 16:
        for at in range(peers):
            used = fill(at, used)
    else:
        used = lax.fori_loop(0, peers, fill, used)
    index = jnp.where(slot < used, lists, -1).astype(F32).astype(BF16)
    flat = peers * slots
    spread = (
        lax.broadcasted_iota(jnp.int32, (slots, flat), 0)
        == lax.broadcasted_iota(jnp.int32, (slots, flat), 1) % slots
    )
    wide = dot(index, spread.astype(F32).astype(BF16))
    mine = (
        lax.broadcasted_iota(jnp.int32, (peers, flat), 0)
        == lax.broadcasted_iota(jnp.int32, (peers, flat), 1) // slots
    )
    line = jnp.sum(jnp.where(mine, wide, 0.0), axis=0, keepdims=True).astype(jnp.int32)
    hit = lax.broadcasted_iota(jnp.int32, (rows, flat), 0) == line
    return hit.astype(F32).astype(BF16)


def pick_body(
    count_hbm, list_hbm, feat_hbm, out_ref, count_ref, list_ref, feat_ref, sems
):
    copies = [
        pltpu.make_async_copy(src, dst, sems.at[k])
        for k, (src, dst) in enumerate(
            ((count_hbm, count_ref), (list_hbm, list_ref), (feat_hbm, feat_ref))
        )
    ]
    for copy in copies:
        copy.start()
    for copy in copies:
        copy.wait()
    onehot = row_onehot(count_ref, list_ref[...], feat_ref.shape[0])
    out_ref[...] = dot(onehot, feat_ref[...], ROWS).astype(BF16)


def prep_body(
    dst_ref, src_ref, count_ref, list_ref, tiles_ref, self_hbm, neigh_hbm,
    onehot_ref, high_ref, low_ref, deg_ref, self_ref, neigh_ref, adj_ref, sems,
):
    copies = [
        pltpu.make_async_copy(src, dst, sems.at[k])
        for k, (src, dst) in enumerate(((self_hbm, self_ref), (neigh_hbm, neigh_ref)))
    ]
    for copy in copies:
        copy.start()
    onehot_ref[...] = row_onehot(count_ref, list_ref[...], onehot_ref.shape[0])
    slots, side, _ = tiles_ref.shape
    adj_ref[...] = jnp.zeros(adj_ref.shape, F32)
    for t in range(slots):
        dst = pl.ds(pl.multiple_of(dst_ref[t] * side, side), side)
        src = pl.ds(pl.multiple_of(src_ref[t] * side, side), side)
        adj_ref[dst, src] += tiles_ref[t].astype(F32)
    adj = adj_ref[...]
    high = adj.astype(BF16)
    high_ref[...] = high
    low_ref[...] = (adj - high.astype(F32)).astype(BF16)
    degree = jnp.maximum(jnp.sum(adj, axis=1, keepdims=True), 1.0)
    deg_ref[...] = jnp.broadcast_to(degree, deg_ref.shape)
    for copy in copies:
        copy.wait()


def column_block(split, rep, c, reps, cols):
    other = lax.bitwise_xor(rep, c) if split else c
    return pl.ds(pl.multiple_of(other * cols, cols), cols)


def wide_degree(deg_ref, cols):
    return jnp.concatenate([deg_ref[...]] * (cols // deg_ref.shape[1]), axis=1)


def aggregate_body(
    split, rep_ref, feat_ref, inc_ref, high_ref, low_ref, deg_ref, self_ref, neigh_ref,
    own_ref, agg_ref, *refs,
):
    part_refs, table_ref = refs[:-1], refs[-1]
    rows, cols = feat_ref.shape
    feat = feat_ref[...]
    table_ref[:rows] = feat
    table_ref[rows:] = inc_ref[...]
    table = table_ref[...]
    summed = dot(high_ref[...], table) + dot(low_ref[...], table)
    agg = (summed / wide_degree(deg_ref, cols)).astype(BF16)
    agg_ref[...] = agg
    reps = self_ref.shape[1] // cols
    for c in reversed(range(reps)):
        at = column_block(split, rep_ref[0], c, reps, cols)
        value = dot(feat, self_ref[:, at]) + dot(agg, neigh_ref[:, at])
        if not split:
            part_refs[0][c] = value.astype(BF16)

            @pl.when(rep_ref[0] == c)
            def _():
                own_ref[...] = value
        elif c == 0:
            own_ref[...] = value
        elif c == 2:
            part_refs[0][...] = value
        else:
            part_refs[1][c // 2] = value.astype(BF16)


def finish_gate(pre, gout_ref, hid_ref, gpre_ref):
    gate = jax.nn.sigmoid(pre)
    hid_ref[...] = (pre * gate).astype(BF16)
    gpre_ref[...] = (gout_ref[...].astype(F32) * (gate + pre * gate * (1.0 - gate))).astype(BF16)


def gate_body(rep_ref, recv_ref, own_ref, gout_ref, hid_ref, gpre_ref):
    pre = own_ref[...]
    for c in range(recv_ref.shape[0]):
        pre = pre + jnp.where(rep_ref[0] == c, 0.0, recv_ref[c].astype(F32))
    finish_gate(pre, gout_ref, hid_ref, gpre_ref)


def across_body(mine_ref, beside_ref, out_ref):
    out_ref[...] = (mine_ref[...] + beside_ref[1].astype(F32)).astype(BF16)


def gate_blocks_body(dom_ref, own_ref, gout_ref, beside_ref, across_ref, hid_ref, gpre_ref, send_ref):
    pre = own_ref[...] + beside_ref[0].astype(F32) + across_ref[...].astype(F32)
    finish_gate(pre, gout_ref, hid_ref, gpre_ref)
    send_ref[...] = gpre_ref[:, block_rows(dom_ref[0] % 2, 1, send_ref.shape[1])]


def back_body(
    split, rep_ref, high_ref, low_ref, deg_ref, self_ref, neigh_ref, *refs,
):
    grads, (total_ref, mirror_ref) = refs[:-2], refs[-2:]
    rows, cols = total_ref.shape
    reps = self_ref.shape[1] // cols
    direct = jnp.zeros((rows, cols), F32)
    gagg = jnp.zeros((rows, cols), F32)
    for c in range(reps):
        grad = grads[c][...] if split else grads[0][c]
        at = column_block(split, rep_ref[0], c, reps, cols)
        gagg += dot(grad, neigh_ref[:, at], COLS)
        direct += dot(grad, self_ref[:, at], COLS)
    gagg = (gagg / wide_degree(deg_ref, cols)).astype(BF16)
    table = dot(high_ref[...], gagg, ROWS) + dot(low_ref[...], gagg, ROWS)
    total_ref[...] = direct + table[:rows]
    mirror_ref[...] = table[rows:].astype(BF16)


def weight_body(feat_ref, agg_ref, gfull_ref, out_ref):
    cols = feat_ref.shape[1]
    parts = out_ref.shape[0]
    piece = out_ref.shape[1] // 2
    for k, ref in enumerate((feat_ref, agg_ref)):
        left = ref[...]
        for c in range(gfull_ref.shape[0]):
            value = dot(left, gfull_ref[c], ROWS)
            out_ref[:, k * piece:(k + 1) * piece, c * cols:(c + 1) * cols] = value.reshape(
                parts, piece, cols
            ).astype(BF16)


def sum_body(scale, recv_ref, self_ref, neigh_ref):
    piece = self_ref.shape[0]
    for k, ref in enumerate((self_ref, neigh_ref)):
        total = jnp.zeros(ref.shape, F32)
        for d in range(recv_ref.shape[0]):
            total += recv_ref[d, k * piece:(k + 1) * piece].astype(F32)
        ref[...] = (total * scale).astype(BF16)


def group_weight_body(dom_ref, rep_ref, *refs):
    rows, (mine_ref, far_ref, send_ref, hold_ref) = refs[:4], refs[-4:]
    grads = refs[4:-4]
    count = len(grads) // 2
    lanes = mine_ref.shape[2]
    layer, side = dom_ref[0] // 2, dom_ref[0] % 2
    for c in range(count):
        at = lax.bitwise_xor(rep_ref[0], c)
        hold_ref[0, at] = grads[c][:, block_rows(side, 0, lanes)]
        hold_ref[1, at] = grads[count + c][...]
    for k in range(2):
        own, other = rows[2 * k][...], rows[2 * k + 1][...]
        for offset in range(count):
            at = lax.bitwise_xor(layer, offset)
            value = dot(own, hold_ref[0, at], ROWS) + dot(other, hold_ref[1, at], ROWS)
            if offset == 0:
                mine_ref[k] = value
            elif offset == 2:
                far_ref[k] = value
            else:
                send_ref[offset // 2, k] = value.astype(BF16)


def join_body(scale, mine_ref, next_ref, far_ref, out_ref):
    total = mine_ref[...] + next_ref[0].astype(F32) + far_ref[...].astype(F32)
    out_ref[...] = (total * scale).astype(BF16)


def place_body(dom_ref, *refs):
    blocks, outs, sems = refs[:-3], refs[-3:-1], refs[-1]
    copies = []
    lanes = blocks[0].shape[2]
    for offset, block in enumerate(blocks):
        at = block_rows(dom_ref[0], offset, lanes)
        for k, out_ref in enumerate(outs):
            copies.append(
                pltpu.make_async_copy(block.at[k], out_ref.at[:, at], sems.at[2 * offset + k])
            )
            copies[-1].start()
    for copy in copies:
        copy.wait()


def scatter_body(onehot_ref, total_ref, ret_ref, out_ref):
    out_ref[...] = (total_ref[...] + dot(onehot_ref[...], ret_ref[...])).astype(BF16)


def swap(array, axis, offset):
    return lax.ppermute(array, axis, [(i, i ^ offset) for i in range(lax.axis_size(axis))])


def gather_columns(array):
    return [array] + [swap(array, "rep", offset) for offset in (1, 2, 3)]


def gather_pieces(array, peers):
    out = {0: array, 4: swap(array, "dom", 4), 2: swap(array, "dom", 2)}
    out[1] = swap(array, "dom", 1)
    out[3] = swap(out[2], "dom", 1)
    out[4], out[1] = lax.optimization_barrier((out[4], out[1]))
    out[6] = swap(out[4], "dom", 2)
    late, out[3] = lax.optimization_barrier((out[4], out[3]))
    out[5] = swap(late, "dom", 1)
    out[7] = swap(out[6], "dom", 1)
    return [out[offset] for offset in range(peers)]


def local(
    features, w_self, w_neigh, grad_out, mirror_list, mirror_count, tile_dst, tile_src, tiles
):
    rows, cols = features.shape
    width = w_self.shape[1]
    peers, slots = mirror_list.shape
    mirrors = peers * slots
    table_rows = rows + mirrors
    reps = width // cols
    struct = jax.ShapeDtypeStruct
    block = struct((rows, cols), BF16)
    rep = lax.axis_index("rep").astype(jnp.int32).reshape(1)
    dom = lax.axis_index("dom").astype(jnp.int32).reshape(1)
    lanes = width // peers
    split = peers == 8 and reps == 4 and slots % 16 == 0 and lanes % 128 == 0
    mirror_out = struct((mirrors, cols), BF16)

    def exchange(array):
        return lax.all_to_all(
            array.reshape(peers, slots, cols), "dom", split_axis=0, concat_axis=0, tiled=True
        ).reshape(mirrors, cols)

    outgoing = call(
        pick_body, mirror_out,
        [("h", mirror_count), ("h", mirror_list), ("h", features)],
        scratch=[
            pltpu.SMEM(mirror_count.shape, jnp.int32), pltpu.VMEM(mirror_list.shape, jnp.int32),
            pltpu.VMEM((rows, cols), BF16), pltpu.SemaphoreType.DMA((3,)),
        ],
        vmem=58,
        flops=2 * mirrors * rows * cols, moved=600_000,
    )
    incoming = exchange(outgoing)
    tiles_late, feat_late, self_late, neigh_late, _ = lax.optimization_barrier(
        (tiles, features, w_self, w_neigh, outgoing)
    )
    onehot, high, low, degree, self_near, neigh_near = call(
        prep_body,
        (
            struct((rows, mirrors), BF16),
            struct((rows, table_rows), BF16), struct((rows, table_rows), BF16),
            struct((rows, 128), F32), struct(w_self.shape, BF16), struct(w_neigh.shape, BF16),
        ),
        [
            ("s", tile_dst), ("s", tile_src), ("s", mirror_count), ("v", mirror_list),
            ("v", tiles_late), ("h", self_late),
            ("h", neigh_late),
        ],
        scratch=[pltpu.VMEM((rows, table_rows), F32), pltpu.SemaphoreType.DMA((2,))],
        flops=1_000_000, moved=3_000_000,
    )
    if split:
        feat_beside = swap(features, "dom", 1)
        incoming, feat_beside = lax.optimization_barrier((incoming, feat_beside))
    own, agg, *parts = call(
        functools.partial(aggregate_body, split),
        (struct((rows, cols), F32), block)
        + (
            (struct((rows, cols), F32), struct((2, rows, cols), BF16)) if split
            else (struct((reps, rows, cols), BF16),)
        ),
        [
            ("s", rep), ("v", feat_late), ("v", incoming), ("v", high), ("v", low),
            ("v", degree), ("v", self_near), ("v", neigh_near),
        ],
        scratch=[pltpu.VMEM((table_rows, cols), BF16)],
        flops=600_000_000, moved=3_000_000,
    )
    scale = float(rows * peers) ** (-0.5)
    if split:
        agg_beside = swap(agg, "dom", 1)
        grad_out, agg_beside = lax.optimization_barrier((grad_out, agg_beside))
        beside = swap(parts[1], "rep", 1)
        across = call(
            across_body, block, [("v", parts[0]), ("v", beside)], flops=100_000, moved=500_000
        )
        across = swap(across, "rep", 2)
        hidden, grad_pre, half = call(
            gate_blocks_body, (block, block, struct((rows, lanes), BF16)),
            [("s", dom), ("v", own), ("v", grad_out), ("v", beside), ("v", across)],
            flops=2_000_000, moved=1_300_000,
        )
        grad_full = gather_columns(grad_pre)
        halves = gather_columns(swap(half, "dom", 1))
    else:
        recv = lax.all_to_all(parts[0], "rep", split_axis=0, concat_axis=0, tiled=True)
        hidden, grad_pre = call(
            gate_body, (block, block),
            [("s", rep), ("v", recv), ("v", own), ("v", grad_out)],
            flops=2_000_000, moved=1_300_000,
        )
        grad_full = [lax.all_gather(grad_pre, "rep", axis=0, tiled=False)]
    total, mirror_grad = call(
        functools.partial(back_body, split), (struct((rows, cols), F32), mirror_out),
        [
            ("s", rep), ("v", high), ("v", low), ("v", degree), ("v", self_near),
            ("v", neigh_near),
        ] + [("v", got) for got in grad_full],
        flops=600_000_000, moved=3_000_000,
    )
    if split:
        piece = struct((2, rows, lanes), F32)
        mine, far, send = call(
            group_weight_body, (piece, piece, struct((2, 2, rows, lanes), BF16)),
            [
                ("s", dom), ("s", rep), ("v", features), ("v", feat_beside), ("v", agg),
                ("v", agg_beside),
            ] + [("v", got) for got in grad_full + halves],
            scratch=[pltpu.VMEM((2, reps, rows, lanes), BF16)],
            flops=600_000_000, moved=3_000_000,
        )
        piece = struct((2, rows, lanes), BF16)
        beside = swap(send, "dom", 2)
        far = call(across_body, piece, [("v", far), ("v", beside)], flops=100_000, moved=500_000)
        mine = call(
            functools.partial(join_body, scale), piece,
            [("v", mine), ("v", beside), ("v", swap(far, "dom", 4))],
            flops=200_000, moved=500_000,
        )
        pieces = gather_pieces(mine, peers)
    returned = exchange(mirror_grad)
    grad_features = call(
        scatter_body, block, [("v", onehot), ("v", total), ("v", returned)],
        flops=2 * mirrors * rows * cols, moved=700_000,
    )
    if split:
        out_self, out_neigh = call(
            place_body, (struct((rows, width), BF16), struct((rows, width), BF16)),
            [("s", dom)] + [("v", part) for part in pieces],
            scratch=[pltpu.SemaphoreType.DMA((2 * peers,))], moved=2_000_000, out="h",
        )
    else:
        piece = cols // peers
        partial = call(
            weight_body, struct((peers, 2 * piece, width), BF16),
            [("v", features), ("v", agg), ("v", grad_full[0])],
            flops=600_000_000, moved=2_000_000,
        )
        gathered = lax.all_to_all(partial, "dom", split_axis=0, concat_axis=0, tiled=True)
        mine_self, mine_neigh = call(
            functools.partial(sum_body, scale),
            (struct((piece, width), BF16), struct((piece, width), BF16)),
            [("v", gathered)], flops=1_000_000, moved=1_200_000,
        )
        out_self = lax.all_gather(mine_self, "dom", axis=0, tiled=True)
        out_neigh = lax.all_gather(mine_neigh, "dom", axis=0, tiled=True)
    return hidden, grad_features, out_self, out_neigh


def solution(mesh):
    in_specs = (
        P("dom", "rep"),
        P("rep", None),
        P("rep", None),
        P("dom", "rep"),
        P("dom", None),
        P("dom"),
        P("dom"),
        P("dom"),
        P("dom", None, None),
    )
    out_specs = (P("dom", "rep"), P("dom", "rep"), P("rep", None), P("rep", None))
    return jax.shard_map(local, mesh=mesh, in_specs=in_specs, out_specs=out_specs, check_vma=False)
```

```python
import functools

import jax
import jax.numpy as jnp
from jax import lax
from jax.experimental import pallas as pl
from jax.experimental.pallas import tpu as pltpu
from jax.sharding import PartitionSpec as P

F32 = jnp.float32
BF16 = jnp.bfloat16
SPECS = {
    "v": pl.BlockSpec(memory_space=pltpu.VMEM),
    "s": pl.BlockSpec(memory_space=pltpu.SMEM),
    "h": pl.BlockSpec(memory_space=pltpu.HBM),
}
ROWS = (((0,), (0,)), ((), ()))
COLS = (((1,), (1,)), ((), ()))


def call(body, outs, ins, scratch=(), flops=0, moved=0, vmem=16, out="v"):
    return pl.pallas_call(
        body,
        out_shape=outs,
        in_specs=[SPECS[spec] for spec, _ in ins],
        out_specs=jax.tree.map(lambda _: SPECS[out], outs),
        scratch_shapes=list(scratch),
        compiler_params=pltpu.CompilerParams(vmem_limit_bytes=vmem * 1024 * 1024),
        cost_estimate=pl.CostEstimate(flops=flops, bytes_accessed=moved, transcendentals=0),
    )(*[array for _, array in ins])


def dot(left, right, dims=(((1,), (0,)), ((), ()))):
    return lax.dot_general(left, right, dims, preferred_element_type=F32)


def block_rows(place, offset, size):
    return pl.ds(pl.multiple_of(lax.bitwise_xor(place, offset) * size, size), size)


def row_onehot(count_ref, lists, rows):
    peers, slots = lists.shape
    peer = lax.broadcasted_iota(jnp.int32, (peers, slots), 0)
    slot = lax.broadcasted_iota(jnp.int32, (peers, slots), 1)

    def fill(at, used):
        return jnp.where(peer == at, count_ref[at], used)

    used = jnp.zeros((peers, slots), jnp.int32)
    if peers <= 16:
        for at in range(peers):
            used = fill(at, used)
    else:
        used = lax.fori_loop(0, peers, fill, used)
    index = jnp.where(slot < used, lists, -1).astype(F32).astype(BF16)
    flat = peers * slots
    spread = (
        lax.broadcasted_iota(jnp.int32, (slots, flat), 0)
        == lax.broadcasted_iota(jnp.int32, (slots, flat), 1) % slots
    )
    wide = dot(index, spread.astype(F32).astype(BF16))
    mine = (
        lax.broadcasted_iota(jnp.int32, (peers, flat), 0)
        == lax.broadcasted_iota(jnp.int32, (peers, flat), 1) // slots
    )
    line = jnp.sum(jnp.where(mine, wide, 0.0), axis=0, keepdims=True).astype(jnp.int32)
    hit = lax.broadcasted_iota(jnp.int32, (rows, flat), 0) == line
    return hit.astype(F32).astype(BF16)


def pick_body(
    count_hbm, list_hbm, feat_hbm, onehot_ref, out_ref, count_ref, list_ref, feat_ref, sems
):
    copies = [
        pltpu.make_async_copy(src, dst, sems.at[k])
        for k, (src, dst) in enumerate(
            ((count_hbm, count_ref), (list_hbm, list_ref), (feat_hbm, feat_ref))
        )
    ]
    for copy in copies:
        copy.start()
    for copy in copies:
        copy.wait()
    onehot = row_onehot(count_ref, list_ref[...], feat_ref.shape[0])
    onehot_ref[...] = onehot
    out_ref[...] = dot(onehot, feat_ref[...], ROWS).astype(BF16)


def prep_body(
    dst_ref, src_ref, tiles_ref, self_hbm, neigh_hbm,
    high_ref, low_ref, deg_ref, self_ref, neigh_ref, adj_ref, sems,
):
    copies = [
        pltpu.make_async_copy(src, dst, sems.at[k])
        for k, (src, dst) in enumerate(((self_hbm, self_ref), (neigh_hbm, neigh_ref)))
    ]
    for copy in copies:
        copy.start()
    slots, side, _ = tiles_ref.shape
    adj_ref[...] = jnp.zeros(adj_ref.shape, F32)
    for t in range(slots):
        dst = pl.ds(pl.multiple_of(dst_ref[t] * side, side), side)
        src = pl.ds(pl.multiple_of(src_ref[t] * side, side), side)
        adj_ref[dst, src] += tiles_ref[t].astype(F32)
    adj = adj_ref[...]
    high = adj.astype(BF16)
    high_ref[...] = high
    low_ref[...] = (adj - high.astype(F32)).astype(BF16)
    degree = jnp.maximum(jnp.sum(adj, axis=1, keepdims=True), 1.0)
    deg_ref[...] = jnp.broadcast_to(degree, deg_ref.shape)
    for copy in copies:
        copy.wait()


def column_block(split, rep, c, reps, cols):
    other = lax.bitwise_xor(rep, c) if split else c
    return pl.ds(pl.multiple_of(other * cols, cols), cols)


def wide_degree(deg_ref, cols):
    return jnp.concatenate([deg_ref[...]] * (cols // deg_ref.shape[1]), axis=1)


def aggregate_body(
    split, rep_ref, feat_ref, inc_ref, high_ref, low_ref, deg_ref, self_ref, neigh_ref,
    own_ref, agg_ref, *refs,
):
    part_refs, table_ref = refs[:-1], refs[-1]
    rows, cols = feat_ref.shape
    feat = feat_ref[...]
    table_ref[:rows] = feat
    table_ref[rows:] = inc_ref[...]
    table = table_ref[...]
    summed = dot(high_ref[...], table) + dot(low_ref[...], table)
    agg = (summed / wide_degree(deg_ref, cols)).astype(BF16)
    agg_ref[...] = agg
    reps = self_ref.shape[1] // cols
    for c in reversed(range(reps)):
        at = column_block(split, rep_ref[0], c, reps, cols)
        value = dot(feat, self_ref[:, at]) + dot(agg, neigh_ref[:, at])
        if not split:
            part_refs[0][c] = value.astype(BF16)

            @pl.when(rep_ref[0] == c)
            def _():
                own_ref[...] = value
        elif c == 0:
            own_ref[...] = value
        elif c == 2:
            part_refs[0][...] = value
        else:
            part_refs[1][c // 2] = value.astype(BF16)


def finish_gate(pre, gout_ref, hid_ref, gpre_ref):
    gate = jax.nn.sigmoid(pre)
    hid_ref[...] = (pre * gate).astype(BF16)
    gpre_ref[...] = (gout_ref[...].astype(F32) * (gate + pre * gate * (1.0 - gate))).astype(BF16)


def gate_body(rep_ref, recv_ref, own_ref, gout_ref, hid_ref, gpre_ref):
    pre = own_ref[...]
    for c in range(recv_ref.shape[0]):
        pre = pre + jnp.where(rep_ref[0] == c, 0.0, recv_ref[c].astype(F32))
    finish_gate(pre, gout_ref, hid_ref, gpre_ref)


def across_body(mine_ref, beside_ref, out_ref):
    out_ref[...] = (mine_ref[...] + beside_ref[1].astype(F32)).astype(BF16)


def gate_blocks_body(dom_ref, own_ref, gout_ref, beside_ref, across_ref, hid_ref, gpre_ref, send_ref):
    pre = own_ref[...] + beside_ref[0].astype(F32) + across_ref[...].astype(F32)
    finish_gate(pre, gout_ref, hid_ref, gpre_ref)
    send_ref[...] = gpre_ref[:, block_rows(dom_ref[0] % 2, 1, send_ref.shape[1])]


def back_body(
    split, rep_ref, high_ref, low_ref, deg_ref, self_ref, neigh_ref, *refs,
):
    grads, (total_ref, mirror_ref) = refs[:-2], refs[-2:]
    rows, cols = total_ref.shape
    reps = self_ref.shape[1] // cols
    direct = jnp.zeros((rows, cols), F32)
    gagg = jnp.zeros((rows, cols), F32)
    for c in range(reps):
        grad = grads[c][...] if split else grads[0][c]
        at = column_block(split, rep_ref[0], c, reps, cols)
        gagg += dot(grad, neigh_ref[:, at], COLS)
        direct += dot(grad, self_ref[:, at], COLS)
    gagg = (gagg / wide_degree(deg_ref, cols)).astype(BF16)
    table = dot(high_ref[...], gagg, ROWS) + dot(low_ref[...], gagg, ROWS)
    total_ref[...] = direct + table[:rows]
    mirror_ref[...] = table[rows:].astype(BF16)


def weight_body(feat_ref, agg_ref, gfull_ref, out_ref):
    cols = feat_ref.shape[1]
    parts = out_ref.shape[0]
    piece = out_ref.shape[1] // 2
    for k, ref in enumerate((feat_ref, agg_ref)):
        left = ref[...]
        for c in range(gfull_ref.shape[0]):
            value = dot(left, gfull_ref[c], ROWS)
            out_ref[:, k * piece:(k + 1) * piece, c * cols:(c + 1) * cols] = value.reshape(
                parts, piece, cols
            ).astype(BF16)


def sum_body(scale, recv_ref, self_ref, neigh_ref):
    piece = self_ref.shape[0]
    for k, ref in enumerate((self_ref, neigh_ref)):
        total = jnp.zeros(ref.shape, F32)
        for d in range(recv_ref.shape[0]):
            total += recv_ref[d, k * piece:(k + 1) * piece].astype(F32)
        ref[...] = (total * scale).astype(BF16)


def group_weight_body(dom_ref, rep_ref, *refs):
    rows, (mine_ref, far_ref, send_ref, hold_ref) = refs[:4], refs[-4:]
    grads = refs[4:-4]
    count = len(grads) // 2
    lanes = mine_ref.shape[2]
    layer, side = dom_ref[0] // 2, dom_ref[0] % 2
    for c in range(count):
        at = lax.bitwise_xor(rep_ref[0], c)
        hold_ref[0, at] = grads[c][:, block_rows(side, 0, lanes)]
        hold_ref[1, at] = grads[count + c][...]
    for k in range(2):
        own, other = rows[2 * k][...], rows[2 * k + 1][...]
        for offset in range(count):
            at = lax.bitwise_xor(layer, offset)
            value = dot(own, hold_ref[0, at], ROWS) + dot(other, hold_ref[1, at], ROWS)
            if offset == 0:
                mine_ref[k] = value
            elif offset == 2:
                far_ref[k] = value
            else:
                send_ref[offset // 2, k] = value.astype(BF16)


def join_body(scale, mine_ref, next_ref, far_ref, out_ref):
    total = mine_ref[...] + next_ref[0].astype(F32) + far_ref[...].astype(F32)
    out_ref[...] = (total * scale).astype(BF16)


def place_body(dom_ref, *refs):
    blocks, outs, sems = refs[:-3], refs[-3:-1], refs[-1]
    copies = []
    lanes = blocks[0].shape[2]
    for offset, block in enumerate(blocks):
        at = block_rows(dom_ref[0], offset, lanes)
        for k, out_ref in enumerate(outs):
            copies.append(
                pltpu.make_async_copy(block.at[k], out_ref.at[:, at], sems.at[2 * offset + k])
            )
            copies[-1].start()
    for copy in copies:
        copy.wait()


def scatter_body(onehot_ref, total_ref, ret_ref, out_ref):
    out_ref[...] = (total_ref[...] + dot(onehot_ref[...], ret_ref[...])).astype(BF16)


def swap(array, axis, offset):
    return lax.ppermute(array, axis, [(i, i ^ offset) for i in range(lax.axis_size(axis))])


def gather_columns(array):
    across = swap(array, "rep", 2)
    return [array, swap(array, "rep", 1), across, swap(across, "rep", 1)]


def gather_pieces(array, peers):
    out = {offset: swap(array, "dom", offset) for offset in range(peers - 2, 0, -2)}
    out[0] = array
    for offset in range(0, peers, 2):
        out[offset + 1] = swap(out[offset], "dom", 1)
    return [out[offset] for offset in range(peers)]


def local(
    features, w_self, w_neigh, grad_out, mirror_list, mirror_count, tile_dst, tile_src, tiles
):
    rows, cols = features.shape
    width = w_self.shape[1]
    peers, slots = mirror_list.shape
    mirrors = peers * slots
    table_rows = rows + mirrors
    reps = width // cols
    struct = jax.ShapeDtypeStruct
    block = struct((rows, cols), BF16)
    rep = lax.axis_index("rep").astype(jnp.int32).reshape(1)
    dom = lax.axis_index("dom").astype(jnp.int32).reshape(1)
    lanes = width // peers
    split = peers == 8 and reps == 4 and slots % 16 == 0 and lanes % 128 == 0
    mirror_out = struct((mirrors, cols), BF16)

    def exchange(array):
        return lax.all_to_all(
            array.reshape(peers, slots, cols), "dom", split_axis=0, concat_axis=0, tiled=True
        ).reshape(mirrors, cols)

    onehot, outgoing = call(
        pick_body, (struct((rows, mirrors), BF16), mirror_out),
        [("h", mirror_count), ("h", mirror_list), ("h", features)],
        scratch=[
            pltpu.SMEM(mirror_count.shape, jnp.int32), pltpu.VMEM(mirror_list.shape, jnp.int32),
            pltpu.VMEM((rows, cols), BF16), pltpu.SemaphoreType.DMA((3,)),
        ],
        vmem=58,
        flops=2 * mirrors * rows * cols, moved=600_000,
    )
    incoming = exchange(outgoing)
    tiles_late, feat_late, self_late, neigh_late, _ = lax.optimization_barrier(
        (tiles, features, w_self, w_neigh, outgoing)
    )
    high, low, degree, self_near, neigh_near = call(
        prep_body,
        (
            struct((rows, table_rows), BF16), struct((rows, table_rows), BF16),
            struct((rows, 128), F32), struct(w_self.shape, BF16), struct(w_neigh.shape, BF16),
        ),
        [
            ("s", tile_dst), ("s", tile_src), ("v", tiles_late), ("h", self_late),
            ("h", neigh_late),
        ],
        scratch=[pltpu.VMEM((rows, table_rows), F32), pltpu.SemaphoreType.DMA((2,))],
        flops=1_000_000, moved=3_000_000,
    )
    if split:
        feat_beside = swap(features, "dom", 1)
        incoming, feat_beside = lax.optimization_barrier((incoming, feat_beside))
    own, agg, *parts = call(
        functools.partial(aggregate_body, split),
        (struct((rows, cols), F32), block)
        + (
            (struct((rows, cols), F32), struct((2, rows, cols), BF16)) if split
            else (struct((reps, rows, cols), BF16),)
        ),
        [
            ("s", rep), ("v", feat_late), ("v", incoming), ("v", high), ("v", low),
            ("v", degree), ("v", self_near), ("v", neigh_near),
        ],
        scratch=[pltpu.VMEM((table_rows, cols), BF16)],
        flops=600_000_000, moved=3_000_000,
    )
    scale = float(rows * peers) ** (-0.5)
    if split:
        agg_beside = swap(agg, "dom", 1)
        grad_out, agg_beside = lax.optimization_barrier((grad_out, agg_beside))
        beside = swap(parts[1], "rep", 1)
        across = call(
            across_body, block, [("v", parts[0]), ("v", beside)], flops=100_000, moved=500_000
        )
        across = swap(across, "rep", 2)
        hidden, grad_pre, half = call(
            gate_blocks_body, (block, block, struct((rows, lanes), BF16)),
            [("s", dom), ("v", own), ("v", grad_out), ("v", beside), ("v", across)],
            flops=2_000_000, moved=1_300_000,
        )
        grad_full = gather_columns(grad_pre)
        halves = gather_columns(swap(half, "dom", 1))
    else:
        recv = lax.all_to_all(parts[0], "rep", split_axis=0, concat_axis=0, tiled=True)
        hidden, grad_pre = call(
            gate_body, (block, block),
            [("s", rep), ("v", recv), ("v", own), ("v", grad_out)],
            flops=2_000_000, moved=1_300_000,
        )
        grad_full = [lax.all_gather(grad_pre, "rep", axis=0, tiled=False)]
    total, mirror_grad = call(
        functools.partial(back_body, split), (struct((rows, cols), F32), mirror_out),
        [
            ("s", rep), ("v", high), ("v", low), ("v", degree), ("v", self_near),
            ("v", neigh_near),
        ] + [("v", got) for got in grad_full],
        flops=600_000_000, moved=3_000_000,
    )
    if split:
        piece = struct((2, rows, lanes), F32)
        mine, far, send = call(
            group_weight_body, (piece, piece, struct((2, 2, rows, lanes), BF16)),
            [
                ("s", dom), ("s", rep), ("v", features), ("v", feat_beside), ("v", agg),
                ("v", agg_beside),
            ] + [("v", got) for got in grad_full + halves],
            scratch=[pltpu.VMEM((2, reps, rows, lanes), BF16)],
            flops=600_000_000, moved=3_000_000,
        )
        piece = struct((2, rows, lanes), BF16)
        beside = swap(send, "dom", 2)
        far = call(across_body, piece, [("v", far), ("v", beside)], flops=100_000, moved=500_000)
        mine = call(
            functools.partial(join_body, scale), piece,
            [("v", mine), ("v", beside), ("v", swap(far, "dom", 4))],
            flops=200_000, moved=500_000,
        )
        pieces = gather_pieces(mine, peers)
    returned = exchange(mirror_grad)
    grad_features = call(
        scatter_body, block, [("v", onehot), ("v", total), ("v", returned)],
        flops=2 * mirrors * rows * cols, moved=700_000,
    )
    if split:
        out_self, out_neigh = call(
            place_body, (struct((rows, width), BF16), struct((rows, width), BF16)),
            [("s", dom)] + [("v", part) for part in pieces],
            scratch=[pltpu.SemaphoreType.DMA((2 * peers,))], moved=2_000_000, out="h",
        )
    else:
        piece = cols // peers
        partial = call(
            weight_body, struct((peers, 2 * piece, width), BF16),
            [("v", features), ("v", agg), ("v", grad_full[0])],
            flops=600_000_000, moved=2_000_000,
        )
        gathered = lax.all_to_all(partial, "dom", split_axis=0, concat_axis=0, tiled=True)
        mine_self, mine_neigh = call(
            functools.partial(sum_body, scale),
            (struct((piece, width), BF16), struct((piece, width), BF16)),
            [("v", gathered)], flops=1_000_000, moved=1_200_000,
        )
        out_self = lax.all_gather(mine_self, "dom", axis=0, tiled=True)
        out_neigh = lax.all_gather(mine_neigh, "dom", axis=0, tiled=True)
    return hidden, grad_features, out_self, out_neigh


def solution(mesh):
    in_specs = (
        P("dom", "rep"),
        P("rep", None),
        P("rep", None),
        P("dom", "rep"),
        P("dom", None),
        P("dom"),
        P("dom"),
        P("dom"),
        P("dom", None, None),
    )
    out_specs = (P("dom", "rep"), P("dom", "rep"), P("rep", None), P("rep", None))
    return jax.shard_map(local, mesh=mesh, in_specs=in_specs, out_specs=out_specs, check_vma=False)
```

```python
import functools

import jax
import jax.numpy as jnp
from jax import lax
from jax.experimental import pallas as pl
from jax.experimental.pallas import tpu as pltpu
from jax.sharding import PartitionSpec as P

F32 = jnp.float32
BF16 = jnp.bfloat16
SPECS = {
    "v": pl.BlockSpec(memory_space=pltpu.VMEM),
    "s": pl.BlockSpec(memory_space=pltpu.SMEM),
    "h": pl.BlockSpec(memory_space=pltpu.HBM),
}
ROWS = (((0,), (0,)), ((), ()))
COLS = (((1,), (1,)), ((), ()))


def call(body, outs, ins, scratch=(), flops=0, moved=0, vmem=16, out="v", aliases=None):
    return pl.pallas_call(
        body,
        out_shape=outs,
        in_specs=[SPECS[spec] for spec, _ in ins],
        out_specs=jax.tree.map(lambda _: SPECS[out], outs),
        scratch_shapes=list(scratch),
        input_output_aliases=aliases or {},
        compiler_params=pltpu.CompilerParams(vmem_limit_bytes=vmem * 1024 * 1024),
        cost_estimate=pl.CostEstimate(flops=flops, bytes_accessed=moved, transcendentals=0),
    )(*[array for _, array in ins])


def dot(left, right, dims=(((1,), (0,)), ((), ()))):
    return lax.dot_general(left, right, dims, preferred_element_type=F32)


def block_rows(place, offset, size):
    return pl.ds(pl.multiple_of(lax.bitwise_xor(place, offset) * size, size), size)


def row_onehot(count_ref, lists, rows):
    peers, slots = lists.shape
    peer = lax.broadcasted_iota(jnp.int32, (peers, slots), 0)
    slot = lax.broadcasted_iota(jnp.int32, (peers, slots), 1)

    def fill(at, used):
        return jnp.where(peer == at, count_ref[at], used)

    used = jnp.zeros((peers, slots), jnp.int32)
    if peers <= 16:
        for at in range(peers):
            used = fill(at, used)
    else:
        used = lax.fori_loop(0, peers, fill, used)
    index = jnp.where(slot < used, lists, -1).astype(F32).astype(BF16)
    flat = peers * slots
    spread = (
        lax.broadcasted_iota(jnp.int32, (slots, flat), 0)
        == lax.broadcasted_iota(jnp.int32, (slots, flat), 1) % slots
    )
    wide = dot(index, spread.astype(F32).astype(BF16))
    mine = (
        lax.broadcasted_iota(jnp.int32, (peers, flat), 0)
        == lax.broadcasted_iota(jnp.int32, (peers, flat), 1) // slots
    )
    line = jnp.sum(jnp.where(mine, wide, 0.0), axis=0, keepdims=True).astype(jnp.int32)
    hit = lax.broadcasted_iota(jnp.int32, (rows, flat), 0) == line
    return hit.astype(F32).astype(BF16)


def pick_body(
    count_hbm, list_hbm, feat_hbm, onehot_ref, out_ref, count_ref, list_ref, feat_ref, sems
):
    copies = [
        pltpu.make_async_copy(src, dst, sems.at[k])
        for k, (src, dst) in enumerate(
            ((count_hbm, count_ref), (list_hbm, list_ref), (feat_hbm, feat_ref))
        )
    ]
    for copy in copies:
        copy.start()
    for copy in copies:
        copy.wait()
    onehot = row_onehot(count_ref, list_ref[...], feat_ref.shape[0])
    onehot_ref[...] = onehot
    out_ref[...] = dot(onehot, feat_ref[...], ROWS).astype(BF16)


def prep_body(
    dst_ref, src_ref, tiles_ref, self_hbm, neigh_hbm,
    high_ref, low_ref, deg_ref, self_ref, neigh_ref, adj_ref, sems,
):
    copies = [
        pltpu.make_async_copy(src, dst, sems.at[k])
        for k, (src, dst) in enumerate(((self_hbm, self_ref), (neigh_hbm, neigh_ref)))
    ]
    for copy in copies:
        copy.start()
    slots, side, _ = tiles_ref.shape
    adj_ref[...] = jnp.zeros(adj_ref.shape, F32)
    for t in range(slots):
        dst = pl.ds(pl.multiple_of(dst_ref[t] * side, side), side)
        src = pl.ds(pl.multiple_of(src_ref[t] * side, side), side)
        adj_ref[dst, src] += tiles_ref[t].astype(F32)
    adj = adj_ref[...]
    high = adj.astype(BF16)
    high_ref[...] = high
    low_ref[...] = (adj - high.astype(F32)).astype(BF16)
    degree = jnp.maximum(jnp.sum(adj, axis=1, keepdims=True), 1.0)
    deg_ref[...] = jnp.broadcast_to(degree, deg_ref.shape)
    for copy in copies:
        copy.wait()


def column_block(split, rep, c, reps, cols):
    other = lax.bitwise_xor(rep, c) if split else c
    return pl.ds(pl.multiple_of(other * cols, cols), cols)


def wide_degree(deg_ref, cols):
    return jnp.concatenate([deg_ref[...]] * (cols // deg_ref.shape[1]), axis=1)


def aggregate_body(
    split, rep_ref, feat_ref, inc_ref, high_ref, low_ref, deg_ref, self_ref, neigh_ref,
    own_ref, agg_ref, *refs,
):
    part_refs, table_ref = refs[:-1], refs[-1]
    rows, cols = feat_ref.shape
    feat = feat_ref[...]
    table_ref[:rows] = feat
    table_ref[rows:] = inc_ref[...]
    table = table_ref[...]
    summed = dot(high_ref[...], table) + dot(low_ref[...], table)
    agg = (summed / wide_degree(deg_ref, cols)).astype(BF16)
    agg_ref[...] = agg
    reps = self_ref.shape[1] // cols
    for c in reversed(range(reps)):
        at = column_block(split, rep_ref[0], c, reps, cols)
        value = dot(feat, self_ref[:, at]) + dot(agg, neigh_ref[:, at])
        if not split:
            part_refs[0][c] = value.astype(BF16)

            @pl.when(rep_ref[0] == c)
            def _():
                own_ref[...] = value
        elif c == 0:
            own_ref[...] = value
        elif c == 2:
            part_refs[0][...] = value
        else:
            part_refs[1][c // 2] = value.astype(BF16)


def finish_gate(pre, gout_ref, hid_ref, gpre_ref):
    gate = jax.nn.sigmoid(pre)
    hid_ref[...] = (pre * gate).astype(BF16)
    gpre_ref[...] = (gout_ref[...].astype(F32) * (gate + pre * gate * (1.0 - gate))).astype(BF16)


def gate_body(rep_ref, recv_ref, own_ref, gout_ref, hid_ref, gpre_ref):
    pre = own_ref[...]
    for c in range(recv_ref.shape[0]):
        pre = pre + jnp.where(rep_ref[0] == c, 0.0, recv_ref[c].astype(F32))
    finish_gate(pre, gout_ref, hid_ref, gpre_ref)


def across_body(mine_ref, beside_ref, out_ref):
    out_ref[...] = (mine_ref[...] + beside_ref[1].astype(F32)).astype(BF16)


def gate_blocks_body(dom_ref, own_ref, gout_ref, beside_ref, across_ref, hid_ref, gpre_ref, send_ref):
    pre = own_ref[...] + beside_ref[0].astype(F32) + across_ref[...].astype(F32)
    finish_gate(pre, gout_ref, hid_ref, gpre_ref)
    send_ref[...] = gpre_ref[:, block_rows(dom_ref[0] % 2, 1, send_ref.shape[1])]


def back_body(
    split, rep_ref, high_ref, low_ref, deg_ref, self_ref, neigh_ref, *refs,
):
    grads, (total_ref, mirror_ref) = refs[:-2], refs[-2:]
    rows, cols = total_ref.shape
    reps = self_ref.shape[1] // cols
    direct = jnp.zeros((rows, cols), F32)
    gagg = jnp.zeros((rows, cols), F32)
    for c in range(reps):
        grad = grads[c][...] if split else grads[0][c]
        at = column_block(split, rep_ref[0], c, reps, cols)
        gagg += dot(grad, neigh_ref[:, at], COLS)
        direct += dot(grad, self_ref[:, at], COLS)
    gagg = (gagg / wide_degree(deg_ref, cols)).astype(BF16)
    table = dot(high_ref[...], gagg, ROWS) + dot(low_ref[...], gagg, ROWS)
    total_ref[...] = direct + table[:rows]
    mirror_ref[...] = table[rows:].astype(BF16)


def weight_body(feat_ref, agg_ref, gfull_ref, out_ref):
    cols = feat_ref.shape[1]
    parts = out_ref.shape[0]
    piece = out_ref.shape[1] // 2
    for k, ref in enumerate((feat_ref, agg_ref)):
        left = ref[...]
        for c in range(gfull_ref.shape[0]):
            value = dot(left, gfull_ref[c], ROWS)
            out_ref[:, k * piece:(k + 1) * piece, c * cols:(c + 1) * cols] = value.reshape(
                parts, piece, cols
            ).astype(BF16)


def sum_body(scale, recv_ref, self_ref, neigh_ref):
    piece = self_ref.shape[0]
    for k, ref in enumerate((self_ref, neigh_ref)):
        total = jnp.zeros(ref.shape, F32)
        for d in range(recv_ref.shape[0]):
            total += recv_ref[d, k * piece:(k + 1) * piece].astype(F32)
        ref[...] = (total * scale).astype(BF16)


def group_weight_body(dom_ref, rep_ref, *refs):
    rows, (mine_ref, far_ref, send_ref, hold_ref) = refs[:4], refs[-4:]
    grads = refs[4:-4]
    count = len(grads) // 2
    lanes = mine_ref.shape[2]
    layer, side = dom_ref[0] // 2, dom_ref[0] % 2
    for c in range(count):
        at = lax.bitwise_xor(rep_ref[0], c)
        hold_ref[0, at] = grads[c][:, block_rows(side, 0, lanes)]
        hold_ref[1, at] = grads[count + c][...]
    for k in range(2):
        own, other = rows[2 * k][...], rows[2 * k + 1][...]
        for offset in range(count):
            at = lax.bitwise_xor(layer, offset)
            value = dot(own, hold_ref[0, at], ROWS) + dot(other, hold_ref[1, at], ROWS)
            if offset == 0:
                mine_ref[k] = value
            elif offset == 2:
                far_ref[k] = value
            else:
                send_ref[offset // 2, k] = value.astype(BF16)


def join_body(scale, mine_ref, next_ref, far_ref, out_ref):
    total = mine_ref[...] + next_ref[0].astype(F32) + far_ref[...].astype(F32)
    out_ref[...] = (total * scale).astype(BF16)


def place_body(offsets, dom_ref, *refs):
    blocks, outs, sems = refs[:len(offsets)], refs[-3:-1], refs[-1]
    lanes = blocks[0].shape[2]
    copies = []
    for offset, block in zip(offsets, blocks):
        at = block_rows(dom_ref[0], offset, lanes)
        for k, out_ref in enumerate(outs):
            copies.append(
                pltpu.make_async_copy(block.at[k], out_ref.at[:, at], sems.at[len(copies)])
            )
            copies[-1].start()
    for copy in copies:
        copy.wait()


def scatter_body(onehot_ref, total_ref, ret_ref, out_ref):
    out_ref[...] = (total_ref[...] + dot(onehot_ref[...], ret_ref[...])).astype(BF16)


def swap(array, axis, offset):
    return lax.ppermute(array, axis, [(i, i ^ offset) for i in range(lax.axis_size(axis))])


def gather_columns(array):
    across = swap(array, "rep", 2)
    return [array, swap(array, "rep", 1), across, swap(across, "rep", 1)]


def gather_pieces(array, peers):
    out = {0: array, 4: swap(array, "dom", 4), 2: swap(array, "dom", 2)}
    out[1] = swap(array, "dom", 1)
    out[4], out[1] = lax.optimization_barrier((out[4], out[1]))
    out[6] = swap(out[4], "dom", 2)
    for offset in range(2, peers, 2):
        out[offset + 1] = swap(out[offset], "dom", 1)
    return [out[offset] for offset in range(peers)]


def local(
    features, w_self, w_neigh, grad_out, mirror_list, mirror_count, tile_dst, tile_src, tiles
):
    rows, cols = features.shape
    width = w_self.shape[1]
    peers, slots = mirror_list.shape
    mirrors = peers * slots
    table_rows = rows + mirrors
    reps = width // cols
    struct = jax.ShapeDtypeStruct
    block = struct((rows, cols), BF16)
    rep = lax.axis_index("rep").astype(jnp.int32).reshape(1)
    dom = lax.axis_index("dom").astype(jnp.int32).reshape(1)
    lanes = width // peers
    split = peers == 8 and reps == 4 and slots % 16 == 0 and lanes % 128 == 0
    mirror_out = struct((mirrors, cols), BF16)

    def exchange(array):
        return lax.all_to_all(
            array.reshape(peers, slots, cols), "dom", split_axis=0, concat_axis=0, tiled=True
        ).reshape(mirrors, cols)

    onehot, outgoing = call(
        pick_body, (struct((rows, mirrors), BF16), mirror_out),
        [("h", mirror_count), ("h", mirror_list), ("h", features)],
        scratch=[
            pltpu.SMEM(mirror_count.shape, jnp.int32), pltpu.VMEM(mirror_list.shape, jnp.int32),
            pltpu.VMEM((rows, cols), BF16), pltpu.SemaphoreType.DMA((3,)),
        ],
        vmem=58,
        flops=2 * mirrors * rows * cols, moved=600_000,
    )
    incoming = exchange(outgoing)
    tiles_late, feat_late, self_late, neigh_late, _ = lax.optimization_barrier(
        (tiles, features, w_self, w_neigh, outgoing)
    )
    high, low, degree, self_near, neigh_near = call(
        prep_body,
        (
            struct((rows, table_rows), BF16), struct((rows, table_rows), BF16),
            struct((rows, 128), F32), struct(w_self.shape, BF16), struct(w_neigh.shape, BF16),
        ),
        [
            ("s", tile_dst), ("s", tile_src), ("v", tiles_late), ("h", self_late),
            ("h", neigh_late),
        ],
        scratch=[pltpu.VMEM((rows, table_rows), F32), pltpu.SemaphoreType.DMA((2,))],
        flops=1_000_000, moved=3_000_000,
    )
    if split:
        feat_beside = swap(features, "dom", 1)
        incoming, feat_beside = lax.optimization_barrier((incoming, feat_beside))
    own, agg, *parts = call(
        functools.partial(aggregate_body, split),
        (struct((rows, cols), F32), block)
        + (
            (struct((rows, cols), F32), struct((2, rows, cols), BF16)) if split
            else (struct((reps, rows, cols), BF16),)
        ),
        [
            ("s", rep), ("v", feat_late), ("v", incoming), ("v", high), ("v", low),
            ("v", degree), ("v", self_near), ("v", neigh_near),
        ],
        scratch=[pltpu.VMEM((table_rows, cols), BF16)],
        flops=600_000_000, moved=3_000_000,
    )
    scale = float(rows * peers) ** (-0.5)
    if split:
        agg_beside = swap(agg, "dom", 1)
        grad_out, agg_beside = lax.optimization_barrier((grad_out, agg_beside))
        beside = swap(parts[1], "rep", 1)
        across = call(
            across_body, block, [("v", parts[0]), ("v", beside)], flops=100_000, moved=500_000
        )
        across = swap(across, "rep", 2)
        hidden, grad_pre, half = call(
            gate_blocks_body, (block, block, struct((rows, lanes), BF16)),
            [("s", dom), ("v", own), ("v", grad_out), ("v", beside), ("v", across)],
            flops=2_000_000, moved=1_300_000,
        )
        grad_full = gather_columns(grad_pre)
        halves = gather_columns(swap(half, "dom", 1))
    else:
        recv = lax.all_to_all(parts[0], "rep", split_axis=0, concat_axis=0, tiled=True)
        hidden, grad_pre = call(
            gate_body, (block, block),
            [("s", rep), ("v", recv), ("v", own), ("v", grad_out)],
            flops=2_000_000, moved=1_300_000,
        )
        grad_full = [lax.all_gather(grad_pre, "rep", axis=0, tiled=False)]
    total, mirror_grad = call(
        functools.partial(back_body, split), (struct((rows, cols), F32), mirror_out),
        [
            ("s", rep), ("v", high), ("v", low), ("v", degree), ("v", self_near),
            ("v", neigh_near),
        ] + [("v", got) for got in grad_full],
        flops=600_000_000, moved=3_000_000,
    )
    if split:
        piece = struct((2, rows, lanes), F32)
        mine, far, send = call(
            group_weight_body, (piece, piece, struct((2, 2, rows, lanes), BF16)),
            [
                ("s", dom), ("s", rep), ("v", features), ("v", feat_beside), ("v", agg),
                ("v", agg_beside),
            ] + [("v", got) for got in grad_full + halves],
            scratch=[pltpu.VMEM((2, reps, rows, lanes), BF16)],
            flops=600_000_000, moved=3_000_000,
        )
        piece = struct((2, rows, lanes), BF16)
        beside = swap(send, "dom", 2)
        far = call(across_body, piece, [("v", far), ("v", beside)], flops=100_000, moved=500_000)
        mine = call(
            functools.partial(join_body, scale), piece,
            [("v", mine), ("v", beside), ("v", swap(far, "dom", 4))],
            flops=200_000, moved=500_000,
        )
        pieces = gather_pieces(mine, peers)
    returned = exchange(mirror_grad)
    grad_features = call(
        scatter_body, block, [("v", onehot), ("v", total), ("v", returned)],
        flops=2 * mirrors * rows * cols, moved=700_000,
    )
    if split:
        outs = ()
        for offsets in ((0, 1, 2, 4), (3, 5, 6, 7)):
            outs = call(
                functools.partial(place_body, offsets), (struct((rows, width), BF16),) * 2,
                [("s", dom)] + [("v", pieces[k]) for k in offsets] + [("h", out) for out in outs],
                scratch=[pltpu.SemaphoreType.DMA((2 * len(offsets),))], moved=1_000_000, out="h",
                aliases={len(offsets) + 1 + k: k for k in range(len(outs))},
            )
        out_self, out_neigh = outs
    else:
        piece = cols // peers
        partial = call(
            weight_body, struct((peers, 2 * piece, width), BF16),
            [("v", features), ("v", agg), ("v", grad_full[0])],
            flops=600_000_000, moved=2_000_000,
        )
        gathered = lax.all_to_all(partial, "dom", split_axis=0, concat_axis=0, tiled=True)
        mine_self, mine_neigh = call(
            functools.partial(sum_body, scale),
            (struct((piece, width), BF16), struct((piece, width), BF16)),
            [("v", gathered)], flops=1_000_000, moved=1_200_000,
        )
        out_self = lax.all_gather(mine_self, "dom", axis=0, tiled=True)
        out_neigh = lax.all_gather(mine_neigh, "dom", axis=0, tiled=True)
    return hidden, grad_features, out_self, out_neigh


def solution(mesh):
    in_specs = (
        P("dom", "rep"),
        P("rep", None),
        P("rep", None),
        P("dom", "rep"),
        P("dom", None),
        P("dom"),
        P("dom"),
        P("dom"),
        P("dom", None, None),
    )
    out_specs = (P("dom", "rep"), P("dom", "rep"), P("rep", None), P("rep", None))
    return jax.shard_map(local, mesh=mesh, in_specs=in_specs, out_specs=out_specs, check_vma=False)
```

```python
import functools

import jax
import jax.numpy as jnp
from jax import lax
from jax.experimental import pallas as pl
from jax.experimental.pallas import tpu as pltpu
from jax.sharding import PartitionSpec as P

F32 = jnp.float32
BF16 = jnp.bfloat16
SPECS = {
    "v": pl.BlockSpec(memory_space=pltpu.VMEM),
    "s": pl.BlockSpec(memory_space=pltpu.SMEM),
    "h": pl.BlockSpec(memory_space=pltpu.HBM),
}
ROWS = (((0,), (0,)), ((), ()))
COLS = (((1,), (1,)), ((), ()))


def call(body, outs, ins, scratch=(), flops=0, moved=0, vmem=16, out="v", aliases=None):
    return pl.pallas_call(
        body,
        out_shape=outs,
        in_specs=[SPECS[spec] for spec, _ in ins],
        out_specs=jax.tree.map(lambda _: SPECS[out], outs),
        scratch_shapes=list(scratch),
        input_output_aliases=aliases or {},
        compiler_params=pltpu.CompilerParams(vmem_limit_bytes=vmem * 1024 * 1024),
        cost_estimate=pl.CostEstimate(flops=flops, bytes_accessed=moved, transcendentals=0),
    )(*[array for _, array in ins])


def dot(left, right, dims=(((1,), (0,)), ((), ()))):
    return lax.dot_general(left, right, dims, preferred_element_type=F32)


def block_rows(place, offset, size):
    return pl.ds(pl.multiple_of(lax.bitwise_xor(place, offset) * size, size), size)


def row_onehot(count_ref, lists, rows):
    peers, slots = lists.shape
    peer = lax.broadcasted_iota(jnp.int32, (peers, slots), 0)
    slot = lax.broadcasted_iota(jnp.int32, (peers, slots), 1)

    def fill(at, used):
        return jnp.where(peer == at, count_ref[at], used)

    used = jnp.zeros((peers, slots), jnp.int32)
    if peers <= 16:
        for at in range(peers):
            used = fill(at, used)
    else:
        used = lax.fori_loop(0, peers, fill, used)
    index = jnp.where(slot < used, lists, -1).astype(F32).astype(BF16)
    flat = peers * slots
    spread = (
        lax.broadcasted_iota(jnp.int32, (slots, flat), 0)
        == lax.broadcasted_iota(jnp.int32, (slots, flat), 1) % slots
    )
    wide = dot(index, spread.astype(F32).astype(BF16))
    mine = (
        lax.broadcasted_iota(jnp.int32, (peers, flat), 0)
        == lax.broadcasted_iota(jnp.int32, (peers, flat), 1) // slots
    )
    line = jnp.sum(jnp.where(mine, wide, 0.0), axis=0, keepdims=True).astype(jnp.int32)
    hit = lax.broadcasted_iota(jnp.int32, (rows, flat), 0) == line
    return hit.astype(F32).astype(BF16)


def pick_body(
    count_hbm, list_hbm, feat_hbm, onehot_ref, out_ref, count_ref, list_ref, feat_ref, sems
):
    copies = [
        pltpu.make_async_copy(src, dst, sems.at[k])
        for k, (src, dst) in enumerate(
            ((count_hbm, count_ref), (list_hbm, list_ref), (feat_hbm, feat_ref))
        )
    ]
    for copy in copies:
        copy.start()
    for copy in copies:
        copy.wait()
    onehot = row_onehot(count_ref, list_ref[...], feat_ref.shape[0])
    onehot_ref[...] = onehot
    out_ref[...] = dot(onehot, feat_ref[...], ROWS).astype(BF16)


def prep_body(
    dst_ref, src_ref, tiles_ref, self_hbm, neigh_hbm,
    high_ref, low_ref, deg_ref, self_ref, neigh_ref, adj_ref, sems,
):
    copies = [
        pltpu.make_async_copy(src, dst, sems.at[k])
        for k, (src, dst) in enumerate(((self_hbm, self_ref), (neigh_hbm, neigh_ref)))
    ]
    for copy in copies:
        copy.start()
    slots, side, _ = tiles_ref.shape
    adj_ref[...] = jnp.zeros(adj_ref.shape, F32)
    for t in range(slots):
        dst = pl.ds(pl.multiple_of(dst_ref[t] * side, side), side)
        src = pl.ds(pl.multiple_of(src_ref[t] * side, side), side)
        adj_ref[dst, src] += tiles_ref[t].astype(F32)
    adj = adj_ref[...]
    high = adj.astype(BF16)
    high_ref[...] = high
    low_ref[...] = (adj - high.astype(F32)).astype(BF16)
    degree = jnp.maximum(jnp.sum(adj, axis=1, keepdims=True), 1.0)
    deg_ref[...] = jnp.broadcast_to(degree, deg_ref.shape)
    for copy in copies:
        copy.wait()


def column_block(split, rep, c, reps, cols):
    other = lax.bitwise_xor(rep, c) if split else c
    return pl.ds(pl.multiple_of(other * cols, cols), cols)


def wide_degree(deg_ref, cols):
    return jnp.concatenate([deg_ref[...]] * (cols // deg_ref.shape[1]), axis=1)


def aggregate_body(
    split, rep_ref, feat_ref, inc_ref, high_ref, low_ref, deg_ref, self_ref, neigh_ref,
    own_ref, agg_ref, *refs,
):
    part_refs, table_ref = refs[:-1], refs[-1]
    rows, cols = feat_ref.shape
    feat = feat_ref[...]
    table_ref[:rows] = feat
    table_ref[rows:] = inc_ref[...]
    table = table_ref[...]
    summed = dot(high_ref[...], table) + dot(low_ref[...], table)
    agg = (summed / wide_degree(deg_ref, cols)).astype(BF16)
    agg_ref[...] = agg
    reps = self_ref.shape[1] // cols
    for c in reversed(range(reps)):
        at = column_block(split, rep_ref[0], c, reps, cols)
        value = dot(feat, self_ref[:, at]) + dot(agg, neigh_ref[:, at])
        if not split:
            part_refs[0][c] = value.astype(BF16)

            @pl.when(rep_ref[0] == c)
            def _():
                own_ref[...] = value
        elif c == 0:
            own_ref[...] = value
        elif c == 2:
            part_refs[0][...] = value
        else:
            part_refs[1][c // 2] = value.astype(BF16)


def finish_gate(pre, gout_ref, hid_ref, gpre_ref):
    gate = jax.nn.sigmoid(pre)
    hid_ref[...] = (pre * gate).astype(BF16)
    gpre_ref[...] = (gout_ref[...].astype(F32) * (gate + pre * gate * (1.0 - gate))).astype(BF16)


def gate_body(rep_ref, recv_ref, own_ref, gout_ref, hid_ref, gpre_ref):
    pre = own_ref[...]
    for c in range(recv_ref.shape[0]):
        pre = pre + jnp.where(rep_ref[0] == c, 0.0, recv_ref[c].astype(F32))
    finish_gate(pre, gout_ref, hid_ref, gpre_ref)


def across_body(mine_ref, beside_ref, out_ref):
    out_ref[...] = (mine_ref[...] + beside_ref[1].astype(F32)).astype(BF16)


def gate_blocks_body(dom_ref, own_ref, gout_ref, beside_ref, across_ref, hid_ref, gpre_ref, send_ref):
    pre = own_ref[...] + beside_ref[0].astype(F32) + across_ref[...].astype(F32)
    finish_gate(pre, gout_ref, hid_ref, gpre_ref)
    send_ref[...] = gpre_ref[:, block_rows(dom_ref[0] % 2, 1, send_ref.shape[1])]


def back_body(
    split, rep_ref, high_ref, low_ref, deg_ref, self_ref, neigh_ref, *refs,
):
    grads, (total_ref, mirror_ref) = refs[:-2], refs[-2:]
    rows, cols = total_ref.shape
    reps = self_ref.shape[1] // cols
    direct = jnp.zeros((rows, cols), F32)
    gagg = jnp.zeros((rows, cols), F32)
    for c in range(reps):
        grad = grads[c][...] if split else grads[0][c]
        at = column_block(split, rep_ref[0], c, reps, cols)
        gagg += dot(grad, neigh_ref[:, at], COLS)
        direct += dot(grad, self_ref[:, at], COLS)
    gagg = (gagg / wide_degree(deg_ref, cols)).astype(BF16)
    table = dot(high_ref[...], gagg, ROWS) + dot(low_ref[...], gagg, ROWS)
    total_ref[...] = direct + table[:rows]
    mirror_ref[...] = table[rows:].astype(BF16)


def weight_body(feat_ref, agg_ref, gfull_ref, out_ref):
    cols = feat_ref.shape[1]
    parts = out_ref.shape[0]
    piece = out_ref.shape[1] // 2
    for k, ref in enumerate((feat_ref, agg_ref)):
        left = ref[...]
        for c in range(gfull_ref.shape[0]):
            value = dot(left, gfull_ref[c], ROWS)
            out_ref[:, k * piece:(k + 1) * piece, c * cols:(c + 1) * cols] = value.reshape(
                parts, piece, cols
            ).astype(BF16)


def sum_body(scale, recv_ref, self_ref, neigh_ref):
    piece = self_ref.shape[0]
    for k, ref in enumerate((self_ref, neigh_ref)):
        total = jnp.zeros(ref.shape, F32)
        for d in range(recv_ref.shape[0]):
            total += recv_ref[d, k * piece:(k + 1) * piece].astype(F32)
        ref[...] = (total * scale).astype(BF16)


def group_weight_body(dom_ref, rep_ref, *refs):
    rows, (mine_ref, far_ref, send_ref, hold_ref) = refs[:4], refs[-4:]
    grads = refs[4:-4]
    count = len(grads) // 2
    lanes = mine_ref.shape[2]
    layer, side = dom_ref[0] // 2, dom_ref[0] % 2
    for c in range(count):
        at = lax.bitwise_xor(rep_ref[0], c)
        hold_ref[0, at] = grads[c][:, block_rows(side, 0, lanes)]
        hold_ref[1, at] = grads[count + c][...]
    for k in range(2):
        own, other = rows[2 * k][...], rows[2 * k + 1][...]
        for offset in range(count):
            at = lax.bitwise_xor(layer, offset)
            value = dot(own, hold_ref[0, at], ROWS) + dot(other, hold_ref[1, at], ROWS)
            if offset == 0:
                mine_ref[k] = value
            elif offset == 2:
                far_ref[k] = value
            else:
                send_ref[offset // 2, k] = value.astype(BF16)


def join_body(scale, mine_ref, next_ref, far_ref, out_ref):
    total = mine_ref[...] + next_ref[0].astype(F32) + far_ref[...].astype(F32)
    out_ref[...] = (total * scale).astype(BF16)


def place_body(offsets, dom_ref, *refs):
    blocks, outs, sems = refs[:len(offsets)], refs[-3:-1], refs[-1]
    lanes = blocks[0].shape[2]
    copies = []
    for offset, block in zip(offsets, blocks):
        at = block_rows(dom_ref[0], offset, lanes)
        for k, out_ref in enumerate(outs):
            copies.append(
                pltpu.make_async_copy(block.at[k], out_ref.at[:, at], sems.at[len(copies)])
            )
            copies[-1].start()
    for copy in copies:
        copy.wait()


def scatter_body(onehot_ref, total_ref, ret_ref, out_ref):
    out_ref[...] = (total_ref[...] + dot(onehot_ref[...], ret_ref[...])).astype(BF16)


def swap(array, axis, offset):
    return lax.ppermute(array, axis, [(i, i ^ offset) for i in range(lax.axis_size(axis))])


def gather_columns(array):
    across = swap(array, "rep", 2)
    return [array, swap(array, "rep", 1), across, swap(across, "rep", 1)]


def gather_pieces(array, peers):
    out = {0: array, 4: swap(array, "dom", 4), 2: swap(array, "dom", 2)}
    out[1] = swap(array, "dom", 1)
    out[3] = swap(out[2], "dom", 1)
    out[4], out[1] = lax.optimization_barrier((out[4], out[1]))
    out[6] = swap(out[4], "dom", 2)
    late, out[3] = lax.optimization_barrier((out[4], out[3]))
    out[5] = swap(late, "dom", 1)
    out[7] = swap(out[6], "dom", 1)
    return [out[offset] for offset in range(peers)]


def local(
    features, w_self, w_neigh, grad_out, mirror_list, mirror_count, tile_dst, tile_src, tiles
):
    rows, cols = features.shape
    width = w_self.shape[1]
    peers, slots = mirror_list.shape
    mirrors = peers * slots
    table_rows = rows + mirrors
    reps = width // cols
    struct = jax.ShapeDtypeStruct
    block = struct((rows, cols), BF16)
    rep = lax.axis_index("rep").astype(jnp.int32).reshape(1)
    dom = lax.axis_index("dom").astype(jnp.int32).reshape(1)
    lanes = width // peers
    split = peers == 8 and reps == 4 and slots % 16 == 0 and lanes % 128 == 0
    mirror_out = struct((mirrors, cols), BF16)

    def exchange(array):
        return lax.all_to_all(
            array.reshape(peers, slots, cols), "dom", split_axis=0, concat_axis=0, tiled=True
        ).reshape(mirrors, cols)

    onehot, outgoing = call(
        pick_body, (struct((rows, mirrors), BF16), mirror_out),
        [("h", mirror_count), ("h", mirror_list), ("h", features)],
        scratch=[
            pltpu.SMEM(mirror_count.shape, jnp.int32), pltpu.VMEM(mirror_list.shape, jnp.int32),
            pltpu.VMEM((rows, cols), BF16), pltpu.SemaphoreType.DMA((3,)),
        ],
        vmem=58,
        flops=2 * mirrors * rows * cols, moved=600_000,
    )
    incoming = exchange(outgoing)
    tiles_late, feat_late, self_late, neigh_late, _ = lax.optimization_barrier(
        (tiles, features, w_self, w_neigh, outgoing)
    )
    high, low, degree, self_near, neigh_near = call(
        prep_body,
        (
            struct((rows, table_rows), BF16), struct((rows, table_rows), BF16),
            struct((rows, 128), F32), struct(w_self.shape, BF16), struct(w_neigh.shape, BF16),
        ),
        [
            ("s", tile_dst), ("s", tile_src), ("v", tiles_late), ("h", self_late),
            ("h", neigh_late),
        ],
        scratch=[pltpu.VMEM((rows, table_rows), F32), pltpu.SemaphoreType.DMA((2,))],
        flops=1_000_000, moved=3_000_000,
    )
    if split:
        feat_beside = swap(features, "dom", 1)
        incoming, feat_beside = lax.optimization_barrier((incoming, feat_beside))
    own, agg, *parts = call(
        functools.partial(aggregate_body, split),
        (struct((rows, cols), F32), block)
        + (
            (struct((rows, cols), F32), struct((2, rows, cols), BF16)) if split
            else (struct((reps, rows, cols), BF16),)
        ),
        [
            ("s", rep), ("v", feat_late), ("v", incoming), ("v", high), ("v", low),
            ("v", degree), ("v", self_near), ("v", neigh_near),
        ],
        scratch=[pltpu.VMEM((table_rows, cols), BF16)],
        flops=600_000_000, moved=3_000_000,
    )
    scale = float(rows * peers) ** (-0.5)
    if split:
        agg_beside = swap(agg, "dom", 1)
        grad_out, agg_beside = lax.optimization_barrier((grad_out, agg_beside))
        beside = swap(parts[1], "rep", 1)
        across = call(
            across_body, block, [("v", parts[0]), ("v", beside)], flops=100_000, moved=500_000
        )
        across = swap(across, "rep", 2)
        hidden, grad_pre, half = call(
            gate_blocks_body, (block, block, struct((rows, lanes), BF16)),
            [("s", dom), ("v", own), ("v", grad_out), ("v", beside), ("v", across)],
            flops=2_000_000, moved=1_300_000,
        )
        grad_full = gather_columns(grad_pre)
        halves = gather_columns(swap(half, "dom", 1))
    else:
        recv = lax.all_to_all(parts[0], "rep", split_axis=0, concat_axis=0, tiled=True)
        hidden, grad_pre = call(
            gate_body, (block, block),
            [("s", rep), ("v", recv), ("v", own), ("v", grad_out)],
            flops=2_000_000, moved=1_300_000,
        )
        grad_full = [lax.all_gather(grad_pre, "rep", axis=0, tiled=False)]
    total, mirror_grad = call(
        functools.partial(back_body, split), (struct((rows, cols), F32), mirror_out),
        [
            ("s", rep), ("v", high), ("v", low), ("v", degree), ("v", self_near),
            ("v", neigh_near),
        ] + [("v", got) for got in grad_full],
        flops=600_000_000, moved=3_000_000,
    )
    if split:
        piece = struct((2, rows, lanes), F32)
        mine, far, send = call(
            group_weight_body, (piece, piece, struct((2, 2, rows, lanes), BF16)),
            [
                ("s", dom), ("s", rep), ("v", features), ("v", feat_beside), ("v", agg),
                ("v", agg_beside),
            ] + [("v", got) for got in grad_full + halves],
            scratch=[pltpu.VMEM((2, reps, rows, lanes), BF16)],
            flops=600_000_000, moved=3_000_000,
        )
        piece = struct((2, rows, lanes), BF16)
        beside = swap(send, "dom", 2)
        far = call(across_body, piece, [("v", far), ("v", beside)], flops=100_000, moved=500_000)
        mine = call(
            functools.partial(join_body, scale), piece,
            [("v", mine), ("v", beside), ("v", swap(far, "dom", 4))],
            flops=200_000, moved=500_000,
        )
        pieces = gather_pieces(mine, peers)
    returned = exchange(mirror_grad)
    grad_features = call(
        scatter_body, block, [("v", onehot), ("v", total), ("v", returned)],
        flops=2 * mirrors * rows * cols, moved=700_000,
    )
    if split:
        outs = ()
        for offsets in ((0, 1, 2, 3, 4), (5, 6, 7)):
            outs = call(
                functools.partial(place_body, offsets), (struct((rows, width), BF16),) * 2,
                [("s", dom)] + [("v", pieces[k]) for k in offsets] + [("h", out) for out in outs],
                scratch=[pltpu.SemaphoreType.DMA((2 * len(offsets),))], moved=1_000_000, out="h",
                aliases={len(offsets) + 1 + k: k for k in range(len(outs))},
            )
        out_self, out_neigh = outs
    else:
        piece = cols // peers
        partial = call(
            weight_body, struct((peers, 2 * piece, width), BF16),
            [("v", features), ("v", agg), ("v", grad_full[0])],
            flops=600_000_000, moved=2_000_000,
        )
        gathered = lax.all_to_all(partial, "dom", split_axis=0, concat_axis=0, tiled=True)
        mine_self, mine_neigh = call(
            functools.partial(sum_body, scale),
            (struct((piece, width), BF16), struct((piece, width), BF16)),
            [("v", gathered)], flops=1_000_000, moved=1_200_000,
        )
        out_self = lax.all_gather(mine_self, "dom", axis=0, tiled=True)
        out_neigh = lax.all_gather(mine_neigh, "dom", axis=0, tiled=True)
    return hidden, grad_features, out_self, out_neigh


def solution(mesh):
    in_specs = (
        P("dom", "rep"),
        P("rep", None),
        P("rep", None),
        P("dom", "rep"),
        P("dom", None),
        P("dom"),
        P("dom"),
        P("dom"),
        P("dom", None, None),
    )
    out_specs = (P("dom", "rep"), P("dom", "rep"), P("rep", None), P("rep", None))
    return jax.shard_map(local, mesh=mesh, in_specs=in_specs, out_specs=out_specs, check_vma=False)
```

```python
import functools

import jax
import jax.numpy as jnp
from jax import lax
from jax.experimental import pallas as pl
from jax.experimental.pallas import tpu as pltpu
from jax.sharding import PartitionSpec as P

F32 = jnp.float32
BF16 = jnp.bfloat16
SPECS = {
    "v": pl.BlockSpec(memory_space=pltpu.VMEM),
    "s": pl.BlockSpec(memory_space=pltpu.SMEM),
    "h": pl.BlockSpec(memory_space=pltpu.HBM),
}
ROWS = (((0,), (0,)), ((), ()))
COLS = (((1,), (1,)), ((), ()))


def call(body, outs, ins, scratch=(), flops=0, moved=0, vmem=16, out="v", aliases=None):
    return pl.pallas_call(
        body,
        out_shape=outs,
        in_specs=[SPECS[spec] for spec, _ in ins],
        out_specs=jax.tree.map(lambda _: SPECS[out], outs),
        scratch_shapes=list(scratch),
        input_output_aliases=aliases or {},
        compiler_params=pltpu.CompilerParams(vmem_limit_bytes=vmem * 1024 * 1024),
        cost_estimate=pl.CostEstimate(flops=flops, bytes_accessed=moved, transcendentals=0),
    )(*[array for _, array in ins])


def dot(left, right, dims=(((1,), (0,)), ((), ()))):
    return lax.dot_general(left, right, dims, preferred_element_type=F32)


def block_rows(place, offset, size):
    return pl.ds(pl.multiple_of(lax.bitwise_xor(place, offset) * size, size), size)


def row_onehot(count_ref, lists, rows):
    peers, slots = lists.shape
    peer = lax.broadcasted_iota(jnp.int32, (peers, slots), 0)
    slot = lax.broadcasted_iota(jnp.int32, (peers, slots), 1)

    def fill(at, used):
        return jnp.where(peer == at, count_ref[at], used)

    used = jnp.zeros((peers, slots), jnp.int32)
    if peers <= 16:
        for at in range(peers):
            used = fill(at, used)
    else:
        used = lax.fori_loop(0, peers, fill, used)
    index = jnp.where(slot < used, lists, -1).astype(F32).astype(BF16)
    flat = peers * slots
    spread = (
        lax.broadcasted_iota(jnp.int32, (slots, flat), 0)
        == lax.broadcasted_iota(jnp.int32, (slots, flat), 1) % slots
    )
    wide = dot(index, spread.astype(F32).astype(BF16))
    mine = (
        lax.broadcasted_iota(jnp.int32, (peers, flat), 0)
        == lax.broadcasted_iota(jnp.int32, (peers, flat), 1) // slots
    )
    line = jnp.sum(jnp.where(mine, wide, 0.0), axis=0, keepdims=True).astype(jnp.int32)
    hit = lax.broadcasted_iota(jnp.int32, (rows, flat), 0) == line
    return hit.astype(F32).astype(BF16)


def pick_body(
    count_hbm, list_hbm, feat_hbm, onehot_ref, out_ref, count_ref, list_ref, feat_ref, sems
):
    copies = [
        pltpu.make_async_copy(src, dst, sems.at[k])
        for k, (src, dst) in enumerate(
            ((count_hbm, count_ref), (list_hbm, list_ref), (feat_hbm, feat_ref))
        )
    ]
    for copy in copies:
        copy.start()
    for copy in copies:
        copy.wait()
    onehot = row_onehot(count_ref, list_ref[...], feat_ref.shape[0])
    onehot_ref[...] = onehot
    out_ref[...] = dot(onehot, feat_ref[...], ROWS).astype(BF16)


def prep_body(
    dst_ref, src_ref, tiles_ref, self_hbm, neigh_hbm,
    high_ref, low_ref, deg_ref, self_ref, neigh_ref, adj_ref, sems,
):
    copies = [
        pltpu.make_async_copy(src, dst, sems.at[k])
        for k, (src, dst) in enumerate(((self_hbm, self_ref), (neigh_hbm, neigh_ref)))
    ]
    for copy in copies:
        copy.start()
    slots, side, _ = tiles_ref.shape
    adj_ref[...] = jnp.zeros(adj_ref.shape, F32)
    for t in range(slots):
        dst = pl.ds(pl.multiple_of(dst_ref[t] * side, side), side)
        src = pl.ds(pl.multiple_of(src_ref[t] * side, side), side)
        adj_ref[dst, src] += tiles_ref[t].astype(F32)
    adj = adj_ref[...]
    high = adj.astype(BF16)
    high_ref[...] = high
    low_ref[...] = (adj - high.astype(F32)).astype(BF16)
    degree = jnp.maximum(jnp.sum(adj, axis=1, keepdims=True), 1.0)
    deg_ref[...] = jnp.broadcast_to(degree, deg_ref.shape)
    for copy in copies:
        copy.wait()


def column_block(split, rep, c, reps, cols):
    other = lax.bitwise_xor(rep, c) if split else c
    return pl.ds(pl.multiple_of(other * cols, cols), cols)


def wide_degree(deg_ref, cols):
    return jnp.concatenate([deg_ref[...]] * (cols // deg_ref.shape[1]), axis=1)


def aggregate_body(
    split, rep_ref, feat_ref, inc_ref, high_ref, low_ref, deg_ref, self_ref, neigh_ref,
    own_ref, agg_ref, *refs,
):
    part_refs, table_ref = refs[:-1], refs[-1]
    rows, cols = feat_ref.shape
    feat = feat_ref[...]
    table_ref[:rows] = feat
    table_ref[rows:] = inc_ref[...]
    table = table_ref[...]
    summed = dot(high_ref[...], table) + dot(low_ref[...], table)
    agg = (summed / wide_degree(deg_ref, cols)).astype(BF16)
    agg_ref[...] = agg
    reps = self_ref.shape[1] // cols
    for c in reversed(range(reps)):
        at = column_block(split, rep_ref[0], c, reps, cols)
        value = dot(feat, self_ref[:, at]) + dot(agg, neigh_ref[:, at])
        if not split:
            part_refs[0][c] = value.astype(BF16)

            @pl.when(rep_ref[0] == c)
            def _():
                own_ref[...] = value
        elif c == 0:
            own_ref[...] = value
        elif c == 2:
            part_refs[0][...] = value
        else:
            part_refs[1][c // 2] = value.astype(BF16)


def finish_gate(pre, gout_ref, hid_ref, gpre_ref):
    gate = jax.nn.sigmoid(pre)
    hid_ref[...] = (pre * gate).astype(BF16)
    gpre_ref[...] = (gout_ref[...].astype(F32) * (gate + pre * gate * (1.0 - gate))).astype(BF16)


def gate_body(rep_ref, recv_ref, own_ref, gout_ref, hid_ref, gpre_ref):
    pre = own_ref[...]
    for c in range(recv_ref.shape[0]):
        pre = pre + jnp.where(rep_ref[0] == c, 0.0, recv_ref[c].astype(F32))
    finish_gate(pre, gout_ref, hid_ref, gpre_ref)


def across_body(mine_ref, beside_ref, out_ref):
    out_ref[...] = (mine_ref[...] + beside_ref[1].astype(F32)).astype(BF16)


def gate_blocks_body(dom_ref, own_ref, gout_ref, beside_ref, across_ref, hid_ref, gpre_ref, send_ref):
    pre = own_ref[...] + beside_ref[0].astype(F32) + across_ref[...].astype(F32)
    finish_gate(pre, gout_ref, hid_ref, gpre_ref)
    send_ref[...] = gpre_ref[:, block_rows(dom_ref[0] % 2, 1, send_ref.shape[1])]


def back_body(
    split, rep_ref, high_ref, low_ref, deg_ref, self_ref, neigh_ref, *refs,
):
    grads, (total_ref, mirror_ref) = refs[:-2], refs[-2:]
    rows, cols = total_ref.shape
    reps = self_ref.shape[1] // cols
    direct = jnp.zeros((rows, cols), F32)
    gagg = jnp.zeros((rows, cols), F32)
    for c in range(reps):
        grad = grads[c][...] if split else grads[0][c]
        at = column_block(split, rep_ref[0], c, reps, cols)
        gagg += dot(grad, neigh_ref[:, at], COLS)
        direct += dot(grad, self_ref[:, at], COLS)
    gagg = (gagg / wide_degree(deg_ref, cols)).astype(BF16)
    table = dot(high_ref[...], gagg, ROWS) + dot(low_ref[...], gagg, ROWS)
    total_ref[...] = direct + table[:rows]
    mirror_ref[...] = table[rows:].astype(BF16)


def weight_body(feat_ref, agg_ref, gfull_ref, out_ref):
    cols = feat_ref.shape[1]
    parts = out_ref.shape[0]
    piece = out_ref.shape[1] // 2
    for k, ref in enumerate((feat_ref, agg_ref)):
        left = ref[...]
        for c in range(gfull_ref.shape[0]):
            value = dot(left, gfull_ref[c], ROWS)
            out_ref[:, k * piece:(k + 1) * piece, c * cols:(c + 1) * cols] = value.reshape(
                parts, piece, cols
            ).astype(BF16)


def sum_body(scale, recv_ref, self_ref, neigh_ref):
    piece = self_ref.shape[0]
    for k, ref in enumerate((self_ref, neigh_ref)):
        total = jnp.zeros(ref.shape, F32)
        for d in range(recv_ref.shape[0]):
            total += recv_ref[d, k * piece:(k + 1) * piece].astype(F32)
        ref[...] = (total * scale).astype(BF16)


def group_weight_body(dom_ref, rep_ref, *refs):
    rows, (mine_ref, far_ref, send_ref, hold_ref) = refs[:4], refs[-4:]
    grads = refs[4:-4]
    count = len(grads) // 2
    lanes = mine_ref.shape[2]
    layer, side = dom_ref[0] // 2, dom_ref[0] % 2
    for c in range(count):
        at = lax.bitwise_xor(rep_ref[0], c)
        hold_ref[0, at] = grads[c][:, block_rows(side, 0, lanes)]
        hold_ref[1, at] = grads[count + c][...]
    for k in range(2):
        own, other = rows[2 * k][...], rows[2 * k + 1][...]
        for offset in range(count):
            at = lax.bitwise_xor(layer, offset)
            value = dot(own, hold_ref[0, at], ROWS) + dot(other, hold_ref[1, at], ROWS)
            if offset == 0:
                mine_ref[k] = value
            elif offset == 2:
                far_ref[k] = value
            else:
                send_ref[offset // 2, k] = value.astype(BF16)


def join_body(scale, mine_ref, next_ref, far_ref, out_ref):
    total = mine_ref[...] + next_ref[0].astype(F32) + far_ref[...].astype(F32)
    out_ref[...] = (total * scale).astype(BF16)


def place_body(offsets, dom_ref, *refs):
    blocks, outs, sems = refs[:len(offsets)], refs[-3:-1], refs[-1]
    lanes = blocks[0].shape[2]
    copies = []
    for offset, block in zip(offsets, blocks):
        at = block_rows(dom_ref[0], offset, lanes)
        for k, out_ref in enumerate(outs):
            copies.append(
                pltpu.make_async_copy(block.at[k], out_ref.at[:, at], sems.at[len(copies)])
            )
            copies[-1].start()
    for copy in copies:
        copy.wait()


def scatter_body(onehot_ref, total_ref, ret_ref, out_ref):
    out_ref[...] = (total_ref[...] + dot(onehot_ref[...], ret_ref[...])).astype(BF16)


def swap(array, axis, offset):
    return lax.ppermute(array, axis, [(i, i ^ offset) for i in range(lax.axis_size(axis))])


def gather_columns(array):
    across = swap(array, "rep", 2)
    return [array, swap(array, "rep", 1), across, swap(across, "rep", 1)]


def gather_pieces(array, peers):
    out = {0: array, 4: swap(array, "dom", 4), 2: swap(array, "dom", 2)}
    out[1] = swap(array, "dom", 1)
    out[3] = swap(out[2], "dom", 1)
    out[4], out[1] = lax.optimization_barrier((out[4], out[1]))
    out[6] = swap(out[4], "dom", 2)
    late, out[3] = lax.optimization_barrier((out[4], out[3]))
    out[5] = swap(late, "dom", 1)
    out[7] = swap(out[6], "dom", 1)
    return [out[offset] for offset in range(peers)]


def local(
    features, w_self, w_neigh, grad_out, mirror_list, mirror_count, tile_dst, tile_src, tiles
):
    rows, cols = features.shape
    width = w_self.shape[1]
    peers, slots = mirror_list.shape
    mirrors = peers * slots
    table_rows = rows + mirrors
    reps = width // cols
    struct = jax.ShapeDtypeStruct
    block = struct((rows, cols), BF16)
    rep = lax.axis_index("rep").astype(jnp.int32).reshape(1)
    dom = lax.axis_index("dom").astype(jnp.int32).reshape(1)
    lanes = width // peers
    split = peers == 8 and reps == 4 and slots % 16 == 0 and lanes % 128 == 0
    mirror_out = struct((mirrors, cols), BF16)

    def exchange(array):
        return lax.all_to_all(
            array.reshape(peers, slots, cols), "dom", split_axis=0, concat_axis=0, tiled=True
        ).reshape(mirrors, cols)

    onehot, outgoing = call(
        pick_body, (struct((rows, mirrors), BF16), mirror_out),
        [("h", mirror_count), ("h", mirror_list), ("h", features)],
        scratch=[
            pltpu.SMEM(mirror_count.shape, jnp.int32), pltpu.VMEM(mirror_list.shape, jnp.int32),
            pltpu.VMEM((rows, cols), BF16), pltpu.SemaphoreType.DMA((3,)),
        ],
        vmem=58,
        flops=2 * mirrors * rows * cols, moved=600_000,
    )
    incoming = exchange(outgoing)
    tiles_late, feat_late, self_late, neigh_late, _ = lax.optimization_barrier(
        (tiles, features, w_self, w_neigh, outgoing)
    )
    high, low, degree, self_near, neigh_near = call(
        prep_body,
        (
            struct((rows, table_rows), BF16), struct((rows, table_rows), BF16),
            struct((rows, 128), F32), struct(w_self.shape, BF16), struct(w_neigh.shape, BF16),
        ),
        [
            ("s", tile_dst), ("s", tile_src), ("v", tiles_late), ("h", self_late),
            ("h", neigh_late),
        ],
        scratch=[pltpu.VMEM((rows, table_rows), F32), pltpu.SemaphoreType.DMA((2,))],
        flops=1_000_000, moved=3_000_000,
    )
    if split:
        feat_beside = swap(features, "dom", 1)
        incoming, feat_beside = lax.optimization_barrier((incoming, feat_beside))
    own, agg, *parts = call(
        functools.partial(aggregate_body, split),
        (struct((rows, cols), F32), block)
        + (
            (struct((rows, cols), F32), struct((2, rows, cols), BF16)) if split
            else (struct((reps, rows, cols), BF16),)
        ),
        [
            ("s", rep), ("v", feat_late), ("v", incoming), ("v", high), ("v", low),
            ("v", degree), ("v", self_near), ("v", neigh_near),
        ],
        scratch=[pltpu.VMEM((table_rows, cols), BF16)],
        flops=600_000_000, moved=3_000_000,
    )
    scale = float(rows * peers) ** (-0.5)
    if split:
        agg_beside = swap(agg, "dom", 1)
        grad_out, agg_beside = lax.optimization_barrier((grad_out, agg_beside))
        beside = swap(parts[1], "rep", 1)
        across = call(
            across_body, block, [("v", parts[0]), ("v", beside)], flops=100_000, moved=500_000
        )
        across = swap(across, "rep", 2)
        hidden, grad_pre, half = call(
            gate_blocks_body, (block, block, struct((rows, lanes), BF16)),
            [("s", dom), ("v", own), ("v", grad_out), ("v", beside), ("v", across)],
            flops=2_000_000, moved=1_300_000,
        )
        grad_full = gather_columns(grad_pre)
        halves = gather_columns(swap(half, "dom", 1))
    else:
        recv = lax.all_to_all(parts[0], "rep", split_axis=0, concat_axis=0, tiled=True)
        hidden, grad_pre = call(
            gate_body, (block, block),
            [("s", rep), ("v", recv), ("v", own), ("v", grad_out)],
            flops=2_000_000, moved=1_300_000,
        )
        grad_full = [lax.all_gather(grad_pre, "rep", axis=0, tiled=False)]
    total, mirror_grad = call(
        functools.partial(back_body, split), (struct((rows, cols), F32), mirror_out),
        [
            ("s", rep), ("v", high), ("v", low), ("v", degree), ("v", self_near),
            ("v", neigh_near),
        ] + [("v", got) for got in grad_full],
        flops=600_000_000, moved=3_000_000,
    )
    if split:
        piece = struct((2, rows, lanes), F32)
        mine, far, send = call(
            group_weight_body, (piece, piece, struct((2, 2, rows, lanes), BF16)),
            [
                ("s", dom), ("s", rep), ("v", features), ("v", feat_beside), ("v", agg),
                ("v", agg_beside),
            ] + [("v", got) for got in grad_full + halves],
            scratch=[pltpu.VMEM((2, reps, rows, lanes), BF16)],
            flops=600_000_000, moved=3_000_000,
        )
        piece = struct((2, rows, lanes), BF16)
        beside = swap(send, "dom", 2)
        far = call(across_body, piece, [("v", far), ("v", beside)], flops=100_000, moved=500_000)
        mine = call(
            functools.partial(join_body, scale), piece,
            [("v", mine), ("v", beside), ("v", swap(far, "dom", 4))],
            flops=200_000, moved=500_000,
        )
        pieces = gather_pieces(mine, peers)
    returned = exchange(mirror_grad)
    grad_features = call(
        scatter_body, block, [("v", onehot), ("v", total), ("v", returned)],
        flops=2 * mirrors * rows * cols, moved=700_000,
    )
    if split:
        outs = ()
        for offsets in ((0, 1, 2, 3, 4, 5, 6), (7,)):
            outs = call(
                functools.partial(place_body, offsets), (struct((rows, width), BF16),) * 2,
                [("s", dom)] + [("v", pieces[k]) for k in offsets] + [("h", out) for out in outs],
                scratch=[pltpu.SemaphoreType.DMA((2 * len(offsets),))], moved=1_000_000, out="h",
                aliases={len(offsets) + 1 + k: k for k in range(len(outs))},
            )
        out_self, out_neigh = outs
    else:
        piece = cols // peers
        partial = call(
            weight_body, struct((peers, 2 * piece, width), BF16),
            [("v", features), ("v", agg), ("v", grad_full[0])],
            flops=600_000_000, moved=2_000_000,
        )
        gathered = lax.all_to_all(partial, "dom", split_axis=0, concat_axis=0, tiled=True)
        mine_self, mine_neigh = call(
            functools.partial(sum_body, scale),
            (struct((piece, width), BF16), struct((piece, width), BF16)),
            [("v", gathered)], flops=1_000_000, moved=1_200_000,
        )
        out_self = lax.all_gather(mine_self, "dom", axis=0, tiled=True)
        out_neigh = lax.all_gather(mine_neigh, "dom", axis=0, tiled=True)
    return hidden, grad_features, out_self, out_neigh


def solution(mesh):
    in_specs = (
        P("dom", "rep"),
        P("rep", None),
        P("rep", None),
        P("dom", "rep"),
        P("dom", None),
        P("dom"),
        P("dom"),
        P("dom"),
        P("dom", None, None),
    )
    out_specs = (P("dom", "rep"), P("dom", "rep"), P("rep", None), P("rep", None))
    return jax.shard_map(local, mesh=mesh, in_specs=in_specs, out_specs=out_specs, check_vma=False)
```
